128 devices in a mesh: dp: 8 (over z_lo, x), tile: 16 (over z_hi, y, core).
Axes of the slice: x: 4, y: 4, z: 4 (z_hi: 2, z_lo: 2; z = z_hi * 2 + z_lo), core: 2. Of those that a mesh axis runs over, the one named last changes fastest.
Arguments:
- fields: bfloat16 [8, 16, 64, 64, 192], P('dp', 'tile'), may hold values from -6 to 6
- cotangent: bfloat16 [8, 16, 64, 64, 192], P('dp', 'tile'), may hold values from -6 to 6
- kernel: float32 [7, 7, 192], replicated, may hold values from -0.875 to 0.875
- conv_bias: float32 [192], replicated, may hold values from -3 to 3
- norm_gain: float32 [192], replicated, may hold values from 0.5 to 1.5
- norm_bias: float32 [192], replicated, may hold values from -3 to 3
- w_expand: bfloat16 [192, 384], replicated, may hold values from -0.4375 to 0.4375
- bias_expand: float32 [384], replicated, may hold values from -3 to 3
- w_reduce: bfloat16 [384, 192], replicated, may hold values from -0.3125 to 0.3125
- bias_reduce: float32 [192], replicated, may hold values from -3 to 3
- layer_scale: float32 [192], replicated, may hold values from 0.5 to 1.5
- neighbors: int32 [16, 8], replicated, may hold values from -1 to 15, as said below
- rotations: int32 [16, 8], replicated, may hold values from 0 to 3, as said below
Outputs:
- mixed: bfloat16 [8, 16, 64, 64, 192], P('dp', 'tile')
- input_grad: bfloat16 [8, 16, 64, 64, 192], P('dp', 'tile')
- kernel_grad: float32 [7, 7, 192], replicated
- expand_grad: float32 [192, 384], replicated
- reduce_grad: float32 [384, 192], replicated
The draws below stay inside these ranges and needn't reach their ends.
Inputs may be any that keep to these rules, and one draw needn't show every extreme that they name: `neighbors`: Sub-tile numbers of the neighbours in the sub-tile's own frame, from the adjacency of a closed strip of faces of 2 x 2 sub-tiles in a numbering drawn from the seed; -1 marks a missing corner neighbour where faces meet at a vertex, edges are never missing. `rotations`: zero between sub-tiles of one face.
All inputs are finite; a program needn't handle non-finite values.
Results may differ from the reference program's by a relative error of at most 0.0065.
Values may be sent and summed in bfloat16 or wider, within the bound.
A program may use at most 128 MiB of HBM per device.

```python
import math
import jax
import jax.numpy as jnp
from jax import lax

CHANNELS = 192
EXPAND = 384
KSIZE = 7
SIDE = 64
TILES = 16
BATCH = 8


def face_layout(key):
    order_key, base_key, flip_key = jax.random.split(key, 3)
    order = jax.random.permutation(order_key, TILES).astype(jnp.int32)
    columns = TILES // 2
    faces = columns // 2
    base = jax.random.randint(base_key, (), 0, 4)
    flips = jax.random.randint(flip_key, (faces,), 0, 2)
    orient = ((base + jnp.arange(faces) + 2 * flips) % 4).astype(jnp.int32)
    position = jnp.arange(TILES)
    row_pos = position % 2
    col_pos = position // 2
    face_of = col_pos // 2
    own_turn = orient[face_of][:, None]
    slot = jnp.arange(8)[None, :]
    global_slot = jnp.where(slot < 4, (slot + own_turn) % 4, (slot - 4 + own_turn) % 4 + 4)
    row_step = jnp.array([-1, 0, 1, 0, -1, 1, 1, -1], jnp.int32)
    col_step = jnp.array([0, 1, 0, -1, 1, 1, -1, -1], jnp.int32)
    raw_row = row_pos[:, None] + row_step[global_slot]
    raw_col = col_pos[:, None] + col_step[global_slot]
    next_row = raw_row % 2
    next_col = raw_col % columns
    next_face = next_col // 2
    cross_col = (raw_col < 0) | (raw_col >= columns) | (next_face != face_of[:, None])
    cross_row = (raw_row < 0) | (raw_row >= 2)
    missing = (global_slot >= 4) & cross_col & cross_row
    numbers = jnp.where(missing, -1, order[next_col * 2 + next_row])
    turns = jnp.where(missing, 0, (orient[next_face] - own_turn) % 4)
    neighbour_table = jnp.zeros((TILES, 8), jnp.int32).at[order].set(numbers.astype(jnp.int32))
    turn_table = jnp.zeros((TILES, 8), jnp.int32).at[order].set(turns.astype(jnp.int32))
    return (neighbour_table, turn_table)


def draw_neighbors(key, part):
    return face_layout(key)[0].astype(jnp.int32)


def draw_rotations(key, part):
    return face_layout(key)[1].astype(jnp.int32)


def block_levels(key, shape, cuts, least, high):
    loudness, own = 1.0, jax.random.fold_in(key, 6)
    for dim, blocks in cuts:
        heights = jnp.exp(jax.random.uniform(jax.random.fold_in(own, dim), (blocks,), jnp.float32, least / len(cuts), high / len(cuts)))
        loudness = loudness * jnp.repeat(heights, shape[dim] // blocks).reshape([-1 if axis == dim else 1 for axis in range(len(shape))])
    return loudness


def gaussian(own_key, shape, scale, limit, cuts=(), held_as=jnp.bfloat16):
    factor_of = block_levels(own_key, shape, cuts, -0.22, 0.18) if cuts else 1.0
    values = jax.random.normal(own_key, shape, jnp.float32) * scale * factor_of
    return jnp.minimum(jnp.maximum(values, -limit), limit).astype(held_as)


def setup_inputs(seed: int = 0) -> dict:
    key_of = jax.random.split(jax.random.key(seed), 14)
    return {
        "fields": gaussian(key_of[0], (BATCH, TILES, SIDE, SIDE, CHANNELS), 1.0, 6.0, ((0, 8), (1, 16))),
        "cotangent": gaussian(key_of[1], (BATCH, TILES, SIDE, SIDE, CHANNELS), 1.0, 6.0, ((0, 8), (1, 16))),
        "kernel": gaussian(key_of[2], (KSIZE, KSIZE, CHANNELS), (KSIZE * KSIZE) ** -0.5, 0.875, (), jnp.float32),
        "conv_bias": gaussian(key_of[3], (CHANNELS,), 0.5, 3.0, (), jnp.float32),
        "norm_gain": jnp.clip(jax.random.uniform(key_of[4], (CHANNELS,), jnp.float32, 0.5, 1.5), 0.5, 1.5),
        "norm_bias": gaussian(key_of[5], (CHANNELS,), 0.5, 3.0, (), jnp.float32),
        "w_expand": gaussian(key_of[6], (CHANNELS, EXPAND), CHANNELS ** -0.5, 0.4375),
        "bias_expand": gaussian(key_of[7], (EXPAND,), 0.5, 3.0, (), jnp.float32),
        "w_reduce": gaussian(key_of[8], (EXPAND, CHANNELS), EXPAND ** -0.5, 0.3125),
        "bias_reduce": gaussian(key_of[9], (CHANNELS,), 0.5, 3.0, (), jnp.float32),
        "layer_scale": jnp.clip(jax.random.uniform(key_of[10], (CHANNELS,), jnp.float32, 0.5, 1.5), 0.5, 1.5),
        "neighbors": draw_neighbors(jax.random.fold_in(key_of[13], 71), 0),
        "rotations": draw_rotations(jax.random.fold_in(key_of[13], 71), 0),
    }


OFFSETS = (2, 3, 0, 1, 2, 0, 0, 2)

def tile_bands(field, width):
    side = field.shape[0]
    return jnp.stack([field[:width], jnp.rot90(field[:, side - width:], 1, (0, 1)), jnp.rot90(field[side - width:], 2, (0, 1)), jnp.rot90(field[:, :width], 3, (0, 1))])

def pad_tile(field, picked):
    width = picked.shape[1]
    side = field.shape[0]
    north = jnp.rot90(picked[0], 2, (0, 1))
    east = jnp.rot90(picked[1], 1, (0, 1))
    south = picked[2]
    west = jnp.rot90(picked[3], 3, (0, 1))
    north_east = jnp.rot90(picked[4], 2, (0, 1))[:, :width]
    south_east = picked[5][:, :width]
    south_west = picked[6][:, side - width:]
    north_west = jnp.rot90(picked[7], 2, (0, 1))[:, side - width:]
    upper = jnp.concatenate([north_west, north, north_east], axis=1)
    middle = jnp.concatenate([west, field, east], axis=1)
    lower = jnp.concatenate([south_west, south, south_east], axis=1)
    return jnp.concatenate([upper, middle, lower], axis=0)

def bands_back(band_grad):
    width = band_grad.shape[1]
    side = band_grad.shape[2]
    zero_field = jnp.zeros((side, side, band_grad.shape[3]), jnp.float32)
    return jax.vjp(lambda f: tile_bands(f, width), zero_field)[1](band_grad)[0]

def pad_back(padded_grad, width):
    side = padded_grad.shape[0] - 2 * width
    channels = padded_grad.shape[2]
    zero_field = jnp.zeros((side, side, channels), jnp.float32)
    zero_picked = jnp.zeros((8, width, side, channels), jnp.float32)
    return jax.vjp(pad_tile, zero_field, zero_picked)[1](padded_grad)

def block_batch(padded, fields, cotangent, kernel, conv_bias, norm_gain, norm_bias, w_expand, bias_expand, w_reduce, bias_reduce, layer_scale):
    count = fields.shape[0]
    side = fields.shape[1]
    channels = fields.shape[3]
    ksize = kernel.shape[0]
    conv_out = conv_bias
    for row_off in range(ksize):
        for col_off in range(ksize):
            conv_out = conv_out + padded[:, row_off:row_off + side, col_off:col_off + side].astype(jnp.float32) * kernel[row_off, col_off]
    row_mean = lax.optimization_barrier(jnp.mean(conv_out, axis=-1, keepdims=True))
    shifted = conv_out - row_mean
    inv_std = lax.rsqrt(lax.optimization_barrier(jnp.mean(shifted * shifted, axis=-1, keepdims=True)) + 1e-06)
    centred = shifted * inv_std
    normed = (centred * norm_gain + norm_bias).astype(jnp.bfloat16)
    normed_rows = normed.reshape(-1, channels)
    pre_act = jnp.dot(normed_rows, w_expand, preferred_element_type=jnp.float32) + bias_expand
    phi_value = 0.5 * (1.0 + jax.scipy.special.erf(pre_act * 0.7071067811865476))
    activated = (pre_act * phi_value).astype(jnp.bfloat16)
    branch = jnp.dot(activated, w_reduce, preferred_element_type=jnp.float32) + bias_reduce
    mixed = (fields.astype(jnp.float32) + layer_scale * branch.reshape(fields.shape)).astype(jnp.bfloat16)
    branch_grad = (layer_scale * cotangent.astype(jnp.float32)).reshape(-1, channels).astype(jnp.bfloat16)
    reduce_grad = jnp.dot(activated.T, branch_grad, preferred_element_type=jnp.float32)
    act_grad = jnp.dot(branch_grad, w_reduce.T, preferred_element_type=jnp.float32)
    density = jnp.exp(-0.5 * pre_act * pre_act) * 0.3989422804014327
    pre_grad = (act_grad * (phi_value + pre_act * density)).astype(jnp.bfloat16)
    expand_grad = jnp.dot(normed_rows.T, pre_grad, preferred_element_type=jnp.float32)
    normed_grad = jnp.dot(pre_grad, w_expand.T, preferred_element_type=jnp.float32).reshape(conv_out.shape) * norm_gain
    conv_grad = inv_std * (normed_grad - lax.optimization_barrier(jnp.mean(normed_grad, axis=-1, keepdims=True)) - centred * lax.optimization_barrier(jnp.mean(normed_grad * centred, axis=-1, keepdims=True)))
    grown = jnp.pad(conv_grad, ((0, 0), (ksize - 1, ksize - 1), (ksize - 1, ksize - 1), (0, 0)))
    extent = side + ksize - 1
    padded_grad = jnp.zeros((count, extent, extent, channels), jnp.float32)
    kernel_terms = []
    for row_off in range(ksize):
        for col_off in range(ksize):
            low_row = ksize - 1 - row_off
            low_col = ksize - 1 - col_off
            padded_grad = padded_grad + kernel[row_off, col_off] * grown[:, low_row:low_row + extent, low_col:low_col + extent]
            window = padded[:, row_off:row_off + side, col_off:col_off + side].astype(jnp.float32)
            kernel_terms.append(lax.optimization_barrier(jnp.sum(window * conv_grad, axis=(0, 1, 2))))
    kernel_grad = jnp.stack(kernel_terms).reshape(ksize, ksize, channels)
    return (mixed, padded_grad, (kernel_grad, expand_grad, reduce_grad))

def reference(fields, cotangent, kernel, conv_bias, norm_gain, norm_bias, w_expand, bias_expand, w_reduce, bias_reduce, layer_scale, neighbors, rotations):
    width = kernel.shape[0] // 2
    side = fields.shape[2]
    channels = fields.shape[4]
    valid = neighbors >= 0
    offsets = jnp.array(OFFSETS, jnp.int32)[None, :]
    targets = jnp.where(valid, neighbors * 4 + (rotations + offsets) % 4, 0).astype(jnp.int32)
    params = (kernel, conv_bias, norm_gain, norm_bias, w_expand, bias_expand, w_reduce, bias_reduce, layer_scale)

    def per_sample(totals, sample):
        sample_fields, sample_cot = sample
        band_set = jax.vmap(lambda f: tile_bands(f, width))(sample_fields).reshape(-1, width, side, channels)

        def per_tile(state, index):
            sums, returned = state
            keep = valid[index][:, None, None, None]
            picked = jnp.where(keep, band_set[targets[index]], jnp.zeros((), jnp.bfloat16))
            padded = pad_tile(sample_fields[index], picked)
            mixed, padded_grad, grads = block_batch(padded[None], sample_fields[index][None], sample_cot[index][None], *params)
            field_grad, picked_grad = pad_back(padded_grad[0], width)
            picked_grad = jnp.where(keep, picked_grad, jnp.zeros((), jnp.float32))
            returned = returned.at[targets[index]].add(picked_grad)
            sums = (sums[0] + grads[0], sums[1] + grads[1], sums[2] + grads[2])
            direct = sample_cot[index].astype(jnp.float32) + field_grad
            return ((sums, returned), (mixed[0], direct))
        start = jnp.zeros((TILES * 4, width, side, channels), jnp.float32)
        (sums, returned), (mixed, direct) = lax.scan(per_tile, (totals, start), jnp.arange(TILES, dtype=jnp.int32))
        back = jax.vmap(bands_back)(returned.reshape(TILES, 4, width, side, channels))
        return (sums, (mixed, (direct + back).astype(jnp.bfloat16)))
    init = (jnp.zeros(kernel.shape, jnp.float32), jnp.zeros(w_expand.shape, jnp.float32), jnp.zeros(w_reduce.shape, jnp.float32))
    sums, (mixed, input_grad) = lax.scan(per_sample, init, (fields, cotangent))
    scale = 1.0 / math.sqrt(BATCH * TILES * side * side)
    return (mixed, input_grad, sums[0] * scale, sums[1] * scale, sums[2] * scale)
```

```python
import functools
import math

import jax
import jax.numpy as jnp
import numpy as np
from jax import lax
from jax.experimental import pallas as pl
from jax.experimental.pallas import tpu as pltpu
from jax.sharding import PartitionSpec as P

OFFSETS = (2, 3, 0, 1, 2, 0, 0, 2)
SIDE = 64
W = 3
CH = 192
HID = 384
TILES = 16
CELLS = 16
NFREQ = 40
KROW = 80
EXT = SIDE + 2 * W
BF = jnp.bfloat16
F32 = jnp.float32
MESH = pl.DeviceIdType.MESH
WROWS = 1280
WBLOCK = WROWS // TILES


def stripe_table():
    where = np.zeros((W, SIDE, 2), np.int64)
    used = {i: set() for i in range(16)}
    rest = []
    for w in range(W):
        for l in range(SIDE):
            if l < W:
                spot = (w * W + l, 0)
            elif l >= SIDE - W:
                spot = (7 + w * W + l - (SIDE - W), 11)
            else:
                rest.append((w, l))
                continue
            where[w, l] = spot
            used[spot[0]].add(spot[1])
    free = [(i, a) for i in range(16) for a in range(12) if a not in used[i]]
    for (w, l), spot in zip(rest, free):
        where[w, l] = spot
    return where


def np_pad(field, picked):
    north = np.rot90(picked[0], 2)
    east = np.rot90(picked[1], 1)
    south = picked[2]
    west = np.rot90(picked[3], 3)
    ne = np.rot90(picked[4], 2)[:, :W]
    se = picked[5][:, :W]
    sw = picked[6][:, SIDE - W :]
    nw = np.rot90(picked[7], 2)[:, SIDE - W :]
    return np.concatenate(
        [
            np.concatenate([nw, north, ne], 1),
            np.concatenate([west, field, east], 1),
            np.concatenate([sw, south, se], 1),
        ],
        0,
    )


def column_of(m):
    if m < SIDE:
        return m + W
    if m < SIDE + W:
        return m - SIDE
    if m < SIDE + 2 * W:
        return m
    return -1


@functools.lru_cache(None)
def static_tables():
    where = stripe_table()
    codes = np.arange(8 * W * SIDE).reshape(8, W, SIDE)
    padded = np_pad(np.full((SIDE, SIDE), -1), codes)

    def spot(code):
        k, w, l = np.unravel_index(code, (8, W, SIDE))
        i, a = where[w, l]
        return (k, i * CELLS + a) if k < 4 else (k - 4, i * CELLS + 12)

    def rows(p_list, m_list, slots):
        mats = {k: np.zeros((len(p_list) * len(m_list), 256), np.float32) for k in slots}
        for ip, p in enumerate(p_list):
            for im, m in enumerate(m_list):
                q = column_of(m)
                if q < 0 or padded[p, q] < 0:
                    continue
                k, row = spot(padded[p, q])
                mats[k][ip * len(m_list) + im, row] = 1
        return [mats[k] for k in slots]

    top0, top3 = rows([0, 1, 2], range(KROW), (0, 3))
    bot2, bot1 = rows([67, 68, 69], range(KROW), (2, 1))
    side3, side1 = rows(range(W, W + SIDE), range(SIDE, KROW), (3, 1))

    cells = np.arange(SIDE * SIDE).reshape(SIDE, SIDE)
    bands = [
        cells[:W],
        np.rot90(cells[:, SIDE - W :], 1),
        np.rot90(cells[SIDE - W :], 2),
        np.rot90(cells[:, :W], 3),
    ]
    sels = []
    for s, band in enumerate(bands):
        sel = np.zeros((256, 192 if s in (0, 2) else 1024), np.float32)
        for w in range(W):
            for l in range(SIDE):
                i, j = divmod(int(band[w, l]), SIDE)
                if s == 0:
                    col = i * SIDE + j
                elif s == 2:
                    col = (i - (SIDE - W)) * SIDE + j
                elif s == 1:
                    col = i * 16 + j - 48
                else:
                    col = i * 16 + j
                st, a = where[w, l]
                sel[st * CELLS + a, col] = 1
        sels.append(sel)
    assemble = (top0, top3, bot2, bot1, side3, side1)
    return assemble, tuple(sels)


@functools.lru_cache(None)
def dft_tables():
    n = 2 * NFREQ
    theta = 2 * np.pi * (np.arange(NFREQ) + 0.5) / n

    def cs(pos):
        ang = theta[:, None] * np.asarray(pos, np.float64)[None, :]
        live = (np.asarray(pos) >= 0)[None, :]
        return np.cos(ang) * live, np.sin(ang) * live

    cols = [column_of(m) for m in range(KROW)]
    c, s = cs(cols)
    fwd_x = np.concatenate([c, -s, c - s], 0)
    inv_p = (2 / n) * np.concatenate([c + s, -c + s, -s], 0).T
    c, s = cs(np.arange(SIDE))
    inv_y = (2 / n) * np.concatenate([c + s, -c + s, -s], 0).T
    fwd_g = np.concatenate([c, -s, c - s, c + s], 0)
    taps = [0, 1, 2, 3, 4, 5, 6, -1]
    c, s = cs(taps)
    fwd_k = np.concatenate([c, s, c + s, c, -s, c - s], 0)
    inv_k = (2 / n) * np.concatenate([c + s, c - s, -s], 0).T
    hi = fwd_x.astype(jnp.bfloat16)
    lo = (fwd_x - hi.astype(np.float64)).astype(jnp.bfloat16)
    return (
        np.concatenate([hi, lo], 1),
        inv_y.astype(jnp.bfloat16),
        fwd_g.astype(jnp.bfloat16),
        inv_p.astype(jnp.bfloat16),
        fwd_k.astype(np.float32),
        inv_k.astype(np.float32),
    )


def dot(a, b):
    return jnp.dot(a, b, preferred_element_type=F32)


def dot_nt(a, b):
    return lax.dot_general(a, b, (((1,), (1,)), ((), ())), preferred_element_type=F32)


def dot_tn(a, b):
    return lax.dot_general(a, b, (((0,), (0,)), ((), ())), preferred_element_type=F32)


def dot_exact(a, b):
    return jnp.dot(a, b, preferred_element_type=F32, precision=lax.Precision.HIGHEST)


def peer(me, off, n):
    return lax.rem(me + off, n)


def greet(axes):
    barrier = pltpu.get_barrier_semaphore()
    total = 0
    for axis, n in axes:
        me = lax.axis_index(axis)
        for off in range(1, n):
            pl.semaphore_signal(
                barrier, inc=1, device_id={axis: peer(me, off, n)}, device_id_type=MESH
            )
            total += 1
    return barrier, total


def exchange(axis, n, src_of, dst, send, recv):
    me = lax.axis_index(axis)
    copies = []
    for off in range(1, n):
        to = peer(me, off, n)
        copy = pltpu.make_async_remote_copy(
            src_ref=src_of(to),
            dst_ref=dst(me),
            send_sem=send.at[off],
            recv_sem=recv.at[off],
            device_id={axis: to},
            device_id_type=MESH,
        )
        copy.start()
        copies.append(copy)
    return copies


def finish(copies):
    for copy in copies:
        copy.wait()


def halo_kernel(
    field, sel_n, sel_e, sel_s, sel_w, target, out, own, got, routed, back, s1, r1, s2, r2
):
    me = lax.axis_index("tile")
    barrier, total = greet((("tile", TILES),))
    shape = (TILES, CELLS, CH)
    own[0] = dot(sel_n[...], field[0:W].reshape(W * SIDE, CH)).astype(BF).reshape(shape)
    own[1] = dot(sel_e[...], field[:, 48:64].reshape(1024, CH)).astype(BF).reshape(shape)
    own[2] = dot(sel_s[...], field[SIDE - W :].reshape(W * SIDE, CH)).astype(BF).reshape(shape)
    own[3] = dot(sel_w[...], field[:, 0:16].reshape(1024, CH)).astype(BF).reshape(shape)
    pl.semaphore_wait(barrier, total)
    copies = exchange("tile", TILES, lambda to: own.at[:, to], lambda m: got.at[:, m], s1, r1)
    got[:, me] = own[:, me]
    columns = lax.broadcasted_iota(jnp.int32, (1024, 1024), 1)
    route = (columns == target[...]).astype(F32).astype(BF)
    finish(copies)
    moved = dot(route, got[...].reshape(1024, CH)).astype(BF)
    routed[...] = moved.reshape(4, TILES, CELLS, CH)
    copies = exchange("tile", TILES, lambda to: routed.at[:, to], lambda m: back.at[:, m], s2, r2)
    back[:, me] = routed[:, me]
    finish(copies)
    out[...] = back[...].reshape(4, 256, CH)


def halo(fields, target_col):
    _, sels = static_tables()
    sels = [jnp.asarray(s, BF) for s in sels]
    vm = pl.BlockSpec(memory_space=pltpu.VMEM)
    block = pltpu.VMEM((4, TILES, CELLS, CH), BF)
    sem = pltpu.SemaphoreType.DMA((TILES,))
    return pl.pallas_call(
        halo_kernel,
        out_shape=jax.ShapeDtypeStruct((4, 256, CH), BF),
        in_specs=[vm] * 6,
        out_specs=vm,
        scratch_shapes=[block, block, block, block, sem, sem, sem, sem],
        compiler_params=pltpu.CompilerParams(
            collective_id=0, has_side_effects=True, vmem_limit_bytes=40 * 2**20
        ),
        name="halo",
    )(fields, *sels, target_col)


def return_kernel(
    slots, target, wsrc, out, wout, got, routed, back, w1, w2, w2s, w3, s1, r1, s2, r2, ws1, wr1, ws2, wr2, ws3, wr3
):
    me = lax.axis_index("tile")
    md = lax.axis_index("dp")
    ndp = w2.shape[0]
    barrier, total = greet((("tile", TILES), ("dp", ndp)))
    pl.semaphore_wait(barrier, total)
    c1 = exchange("tile", TILES, lambda to: slots.at[:, to], lambda m: got.at[:, m], s1, r1)
    c2 = exchange("tile", TILES, lambda to: wsrc.at[to], lambda m: w1.at[m], ws1, wr1)
    got[:, me] = slots[:, me]
    w1[me] = wsrc[me]
    rows = lax.broadcasted_iota(jnp.int32, (1024, 1024), 0)
    route = (rows == target[...]).astype(F32).astype(BF)
    finish(c1)
    moved = dot(route, got[...].reshape(1024, CH)).astype(BF)
    routed[...] = moved.reshape(4, TILES, CELLS, CH)
    c1 = exchange("tile", TILES, lambda to: routed.at[:, to], lambda m: back.at[:, m], s2, r2)
    back[:, me] = routed[:, me]
    finish(c2)
    part = w1[0].astype(F32)
    for j in range(1, TILES):
        part = part + w1[j].astype(F32)
    w2s[...] = part
    c2 = exchange("dp", ndp, lambda to: w2s, lambda m: w2.at[m], ws2, wr2)
    w2[md] = part
    finish(c2)
    part = w2[0]
    for j in range(1, ndp):
        part = part + w2[j]
    w3[me] = part
    c2 = exchange("tile", TILES, lambda to: w3.at[me], lambda m: w3.at[m], ws3, wr3)
    finish(c1)
    out[...] = back[...].reshape(4, 256, CH)
    finish(c2)
    wout[...] = w3[...].reshape(WROWS, 128)


def send_back(slots, target_row, wsrc, ndp):
    vm = pl.BlockSpec(memory_space=pltpu.VMEM)
    block = pltpu.VMEM((4, TILES, CELLS, CH), BF)
    sem = pltpu.SemaphoreType.DMA((TILES,))
    sem_dp = pltpu.SemaphoreType.DMA((ndp,))
    return pl.pallas_call(
        return_kernel,
        out_shape=(
            jax.ShapeDtypeStruct((4, 256, CH), BF),
            jax.ShapeDtypeStruct((WROWS, 128), F32),
        ),
        in_specs=[vm] * 3,
        out_specs=(vm, vm),
        scratch_shapes=[
            block,
            block,
            block,
            pltpu.VMEM((TILES, WBLOCK, 128), BF),
            pltpu.VMEM((ndp, WBLOCK, 128), F32),
            pltpu.VMEM((WBLOCK, 128), F32),
            pltpu.VMEM((TILES, WBLOCK, 128), F32),
            sem,
            sem,
            sem,
            sem,
            sem,
            sem,
            sem_dp,
            sem_dp,
            sem,
            sem,
        ],
        compiler_params=pltpu.CompilerParams(
            collective_id=1, has_side_effects=True, vmem_limit_bytes=40 * 2**20
        ),
        name="send_back",
    )(slots, target_row, wsrc)


LANES = ((0, 128), (128, 64))


def block_kernel(
    fields,
    cot,
    hal,
    top0,
    top3,
    bot2,
    bot1,
    side3,
    side1,
    top0t,
    top3t,
    bot2t,
    bot1t,
    side3t,
    side1t,
    fwd_x,
    inv_y,
    fwd_g,
    inv_p,
    fwd_k,
    inv_k,
    kernel,
    conv_bias,
    gain,
    nbias,
    w_exp,
    b_exp,
    w_red,
    b_red,
    lscale,
    mixed,
    direct,
    slots,
    wout,
    xpad,
    x3,
    y3,
    g4,
    kpad,
    kf,
    m3,
    egrad,
    rgrad,
    psides,
    ptop,
    pbot,
):
    for u in range(7):
        kpad[0:7] = kernel[u]
        kpad[7:8] = jnp.zeros((1, CH), F32)
        kf[u] = dot_exact(fwd_k[...], kpad[...])
    xpad[W : W + SIDE, 0:SIDE] = fields[...]
    xpad[0:W] = (dot(top0[...], hal[0]) + dot(top3[...], hal[3])).astype(BF).reshape(W, KROW, CH)
    xpad[W + SIDE :] = (
        (dot(bot2[...], hal[2]) + dot(bot1[...], hal[1])).astype(BF).reshape(W, KROW, CH)
    )
    xpad[W : W + SIDE, SIDE:] = (
        (dot(side3[...], hal[3]) + dot(side1[...], hal[1])).astype(BF).reshape(SIDE, 16, CH)
    )

    def to_freq(r, _):
        x = xpad[r]
        x3[r] = dot(fwd_x[...], jnp.concatenate([x, x], axis=0))
        return 0

    lax.fori_loop(0, EXT, to_freq, 0, unroll=2)

    for l0, lw in LANES:
        for fb in range(5):
            rows = [slice(40 * t + 8 * fb, 40 * t + 8 * fb + 8) for t in range(3)]
            lanes = slice(l0, l0 + lw)
            kk = [[kf[u, rows[t], lanes] for t in range(3)] for u in range(7)]

            def conv(ib, _, rows=rows, lanes=lanes, kk=kk):
                i0 = ib * 4
                for t in range(3):
                    xs = [x3[i0 + r, rows[t], lanes] for r in range(10)]
                    for d in range(4):
                        acc = xs[d] * kk[0][t]
                        for u in range(1, 7):
                            acc = acc + xs[d + u] * kk[u][t]
                        y3[i0 + d, rows[t], lanes] = acc
                return 0

            lax.fori_loop(0, SIDE // 4, conv, 0)

    egrad[...] = jnp.zeros_like(egrad)
    rgrad[...] = jnp.zeros_like(rgrad)
    g4[0:6] = jnp.zeros((6, 4 * NFREQ, CH), F32)
    g4[6 + SIDE :] = jnp.zeros((6, 4 * NFREQ, CH), F32)
    step = 8
    n = step * SIDE

    def chunk(ic, _):
        i0 = pl.multiple_of(ic * step, step)
        conv_out = jnp.concatenate(
            [dot(inv_y[...], y3[i0 + d].astype(BF)) for d in range(step)], axis=0
        )
        conv_out = conv_out + conv_bias[...]
        shifted = conv_out - jnp.mean(conv_out, axis=-1, keepdims=True)
        inv_std = lax.rsqrt(jnp.mean(shifted * shifted, axis=-1, keepdims=True) + 1e-06)
        centred = shifted * inv_std
        normed = (centred * gain[...] + nbias[...]).astype(BF)
        pre = dot(normed, w_exp[...]) + b_exp[...]
        size = jnp.abs(pre)
        t = 1.0 / (1.0 + (0.3275911 * math.sqrt(0.5)) * size)
        dens = jnp.exp(-0.5 * pre * pre)
        poly = t * (
            0.127414796
            + t * (-0.142248368 + t * (0.7107068705 + t * (-0.7265760135 + t * 0.5307027145)))
        )
        tail = poly * dens
        phi = jnp.where(pre >= 0, 1.0 - tail, tail)
        act = (pre * phi).astype(BF)
        slope = phi + pre * (dens * 0.3989422804014327)
        cot_c = cot[pl.ds(i0, step)].reshape(n, CH).astype(F32)
        branch = dot(act, w_red[...]) + b_red[...]
        mix = fields[pl.ds(i0, step)].reshape(n, CH).astype(F32) + lscale[...] * branch
        mixed[pl.ds(i0, step)] = mix.astype(BF).reshape(step, SIDE, CH)
        bgrad = (lscale[...] * cot_c).astype(BF)
        pre_grad = (dot_nt(bgrad, w_red[...]) * slope).astype(BF)
        rgrad[...] += dot_tn(bgrad, act)
        egrad[...] += dot_tn(normed, pre_grad)
        ngrad = dot_nt(pre_grad, w_exp[...]) * gain[...]
        m1 = jnp.mean(ngrad, axis=-1, keepdims=True)
        m2 = jnp.mean(ngrad * centred, axis=-1, keepdims=True)
        cgrad = (inv_std * (ngrad - m1 - centred * m2)).astype(BF)
        for d in range(step):
            g4[6 + i0 + d] = dot(fwd_g[...], cgrad[d * SIDE : (d + 1) * SIDE])
        return 0

    lax.fori_loop(0, SIDE // step, chunk, 0)

    for l0, lw in LANES:
        for fb in range(5):
            rows = [slice(40 * t + 8 * fb, 40 * t + 8 * fb + 8) for t in range(4)]
            grow = (rows[0], rows[1], rows[3])
            lanes = slice(l0, l0 + lw)

            def kgrad(ib, accs, rows=rows, lanes=lanes, grow=grow):
                i0 = ib * 4
                accs = list(accs)
                for t in range(3):
                    xs = [x3[i0 + r, rows[t], lanes] for r in range(10)]
                    for d in range(4):
                        g = g4[6 + i0 + d, grow[t], lanes]
                        for u in range(7):
                            accs[7 * t + u] = accs[7 * t + u] + xs[d + u] * g
                return tuple(accs)

            zero = jnp.zeros((8, lw), F32)
            accs = lax.fori_loop(0, SIDE // 4, kgrad, (zero,) * 21)
            for t in range(3):
                for u in range(7):
                    m3[u, rows[t], lanes] = accs[7 * t + u]

            kk = [
                [kf[u, 120 + 40 * t + 8 * fb : 128 + 40 * t + 8 * fb, lanes] for t in range(3)]
                for u in range(7)
            ]

            def pconv(ib, _, rows=rows, lanes=lanes, kk=kk):
                p0 = ib * 5
                for t in range(3):
                    gs = [g4[p0 + r, rows[t], lanes] for r in range(11)]
                    for d in range(5):
                        acc = gs[d + 6] * kk[0][t]
                        for u in range(1, 7):
                            acc = acc + gs[d + 6 - u] * kk[u][t]
                        y3[p0 + d, rows[t], lanes] = acc
                return 0

            lax.fori_loop(0, EXT // 5, pconv, 0)

    for p in range(W):
        ptop[p] = dot(inv_p[...], y3[p].astype(BF)).astype(BF)
        pbot[p] = dot(inv_p[...], y3[W + SIDE + p].astype(BF)).astype(BF)

    def from_freq(i, _):
        back = dot(inv_p[...], y3[i + W].astype(BF))
        direct[i] = (cot[i].astype(F32) + back[0:SIDE]).astype(BF)
        psides[i] = back[SIDE:].astype(BF)
        return 0

    lax.fori_loop(0, SIDE, from_freq, 0, unroll=2)

    top = ptop[...].reshape(W * KROW, CH)
    bot = pbot[...].reshape(W * KROW, CH)
    sides = psides[...].reshape(SIDE * 16, CH)
    shape = (TILES, CELLS, CH)
    slots[0] = dot(top0t[...], top).astype(BF).reshape(shape)
    slots[1] = (dot(side1t[...], sides) + dot(bot1t[...], bot)).astype(BF).reshape(shape)
    slots[2] = dot(bot2t[...], bot).astype(BF).reshape(shape)
    slots[3] = (dot(side3t[...], sides) + dot(top3t[...], top)).astype(BF).reshape(shape)

    for g in range(3):
        lanes = slice(128 * g, 128 * g + 128)
        wout[192 * g : 192 * g + 192] = egrad[:, lanes].astype(BF)
        wout[576 + 192 * g : 768 + 192 * g] = rgrad[:, lanes].astype(BF)
    kg = jnp.concatenate([dot_exact(inv_k[...], m3[u]) for u in range(7)], axis=0)
    kg = jnp.concatenate([kg, jnp.zeros((8, CH), F32)], axis=0).astype(BF)
    wout[1152:1216] = kg[:, 0:128]
    wout[1216:1280] = jnp.concatenate([kg[:, 128:192], jnp.zeros((64, 64), BF)], axis=1)


def block(fields, cotangent, hal, params):
    assemble, _ = static_tables()
    mats = [jnp.asarray(a, BF) for a in assemble]
    mats_t = [jnp.asarray(a.T, BF) for a in assemble]
    tables = [jnp.asarray(t) for t in dft_tables()]
    vm = pl.BlockSpec(memory_space=pltpu.VMEM)
    args = [fields, cotangent, hal, *mats, *mats_t, *tables, *params]
    return pl.pallas_call(
        block_kernel,
        out_shape=(
            jax.ShapeDtypeStruct((SIDE, SIDE, CH), BF),
            jax.ShapeDtypeStruct((SIDE, SIDE, CH), BF),
            jax.ShapeDtypeStruct((4, TILES, CELLS, CH), BF),
            jax.ShapeDtypeStruct((WROWS, 128), BF),
        ),
        in_specs=[vm] * len(args),
        out_specs=(vm,) * 4,
        scratch_shapes=[
            pltpu.VMEM((EXT, KROW, CH), BF),
            pltpu.VMEM((EXT, 3 * NFREQ, CH), F32),
            pltpu.VMEM((EXT, 3 * NFREQ, CH), F32),
            pltpu.VMEM((SIDE + 12, 4 * NFREQ, CH), F32),
            pltpu.VMEM((8, CH), F32),
            pltpu.VMEM((7, 6 * NFREQ, CH), F32),
            pltpu.VMEM((7, 3 * NFREQ, CH), F32),
            pltpu.VMEM((CH, HID), F32),
            pltpu.VMEM((CH, HID), F32),
            pltpu.VMEM((SIDE, 16, CH), BF),
            pltpu.VMEM((W, KROW, CH), BF),
            pltpu.VMEM((W, KROW, CH), BF),
        ],
        compiler_params=pltpu.CompilerParams(vmem_limit_bytes=60 * 2**20),
        name="block",
    )(*args)


def last_kernel(scale, direct, bands, wsum, tn, te, ts, tw, out, kgrad, egrad, rgrad):
    north = dot(tn[...], bands[0]).reshape(W, SIDE, CH)
    south = dot(ts[...], bands[2]).reshape(W, SIDE, CH)
    east = dot(te[...], bands[1]).reshape(SIDE, 16, CH)
    west = dot(tw[...], bands[3]).reshape(SIDE, 16, CH)
    mid = slice(W, SIDE - W)
    out[mid, 16:48] = direct[mid, 16:48]
    out[mid, 0:16] = (direct[mid, 0:16].astype(F32) + west[mid]).astype(BF)
    out[mid, 48:64] = (direct[mid, 48:64].astype(F32) + east[mid]).astype(BF)
    zero = jnp.zeros((W, 32, CH), F32)
    for rows, add in ((slice(0, W), north), (slice(SIDE - W, SIDE), south)):
        more = jnp.concatenate([west[rows], zero, east[rows]], axis=1)
        out[rows] = (direct[rows].astype(F32) + add + more).astype(BF)
    for g in range(3):
        lanes = slice(128 * g, 128 * g + 128)
        egrad[:, lanes] = wsum[192 * g : 192 * g + 192] * scale
        rgrad[lanes, :] = wsum[576 + 192 * g : 768 + 192 * g].T * scale
    for u in range(7):
        kgrad[u, :, 0:128] = wsum[1152 + 8 * u : 1159 + 8 * u] * scale
        kgrad[u, :, 128:192] = wsum[1216 + 8 * u : 1223 + 8 * u, 0:64] * scale


def last(direct, bands, wsum, scale):
    _, sels = static_tables()
    sels_t = [jnp.asarray(s.T, BF) for s in sels]
    vm = pl.BlockSpec(memory_space=pltpu.VMEM)
    return pl.pallas_call(
        functools.partial(last_kernel, scale),
        out_shape=(
            jax.ShapeDtypeStruct((SIDE, SIDE, CH), BF),
            jax.ShapeDtypeStruct((7, 7, CH), F32),
            jax.ShapeDtypeStruct((CH, HID), F32),
            jax.ShapeDtypeStruct((HID, CH), F32),
        ),
        in_specs=[vm] * 7,
        out_specs=(vm,) * 4,
        compiler_params=pltpu.CompilerParams(vmem_limit_bytes=40 * 2**20),
        name="last",
    )(direct, bands, wsum, *sels_t)


def routing(neighbors, rotations):
    me = lax.axis_index("tile")
    offsets = jnp.array(OFFSETS, jnp.int32)[None, :]
    side = (rotations + offsets) % 4
    base = jnp.where(neighbors >= 0, side * 256 + neighbors * CELLS, -(1 << 20)).T
    right = jnp.where(me >= 7, 11, -(1 << 20))
    left = jnp.where(me <= 8, 0, -(1 << 20))
    corner_row = jnp.stack([right, left, right, left])[:, None]
    cell = jnp.arange(CELLS, dtype=jnp.int32)[None, None, :]
    edge = base[0:4][:, :, None] + cell
    corner = (base[4:8] + corner_row)[:, :, None]
    return jnp.where(cell < 12, edge, jnp.where(cell == 12, corner, -1)).astype(jnp.int32)


def on_device(
    fields,
    cotangent,
    kernel,
    conv_bias,
    norm_gain,
    norm_bias,
    w_expand,
    bias_expand,
    w_reduce,
    bias_reduce,
    layer_scale,
    neighbors,
    rotations,
):
    ndp = lax.axis_size("dp")
    field = fields.reshape(SIDE, SIDE, CH)
    cot = cotangent.reshape(SIDE, SIDE, CH)
    target = routing(neighbors, rotations)
    hal = halo(field, target.reshape(1024, 1))
    params = [
        kernel,
        conv_bias.reshape(1, CH),
        norm_gain.reshape(1, CH),
        norm_bias.reshape(1, CH),
        w_expand,
        bias_expand.reshape(1, HID),
        w_reduce,
        bias_reduce.reshape(1, CH),
        layer_scale.reshape(1, CH),
    ]
    mixed, direct, slots, wgrad = block(field, cot, hal, params)
    bands, wsum = send_back(
        slots, target.reshape(1, 1024), wgrad.reshape(TILES, WBLOCK, 128), ndp
    )
    scale = 1.0 / math.sqrt(ndp * TILES * SIDE * SIDE)
    input_grad, kgrad, egrad, rgrad = last(direct, bands, wsum, scale)
    return (
        mixed.reshape(fields.shape),
        input_grad.reshape(fields.shape),
        kgrad,
        egrad,
        rgrad,
    )


def solution(mesh):
    split = P("dp", "tile", None, None, None)
    return jax.shard_map(
        on_device,
        mesh=mesh,
        in_specs=(split, split) + (P(),) * 11,
        out_specs=(split, split, P(), P(), P()),
        check_vma=False,
    )
```

```python
import functools
import math

import jax
import jax.numpy as jnp
import numpy as np
from jax import lax
from jax.experimental import pallas as pl
from jax.experimental.pallas import tpu as pltpu
from jax.sharding import PartitionSpec as P

OFFSETS = (2, 3, 0, 1, 2, 0, 0, 2)
SIDE = 64
W = 3
CH = 192
HID = 384
TILES = 16
CELLS = 16
NFREQ = 40
KROW = 80
EXT = SIDE + 2 * W
BF = jnp.bfloat16
F32 = jnp.float32
MESH = pl.DeviceIdType.MESH
WROWS = 1280
WBLOCK = 16
INDEX = ("top0", "top3", "bot2", "bot1", "side3", "side1", "north", "east", "south", "west")


def stripe_table():
    where = np.zeros((W, SIDE, 2), np.int64)
    used = {i: set() for i in range(16)}
    rest = []
    for w in range(W):
        for l in range(SIDE):
            if l < W:
                spot = (w * W + l, 0)
            elif l >= SIDE - W:
                spot = (7 + w * W + l - (SIDE - W), 11)
            else:
                rest.append((w, l))
                continue
            where[w, l] = spot
            used[spot[0]].add(spot[1])
    free = [(i, a) for i in range(16) for a in range(12) if a not in used[i]]
    for (w, l), spot in zip(rest, free):
        where[w, l] = spot
    return where


def np_pad(field, picked):
    north = np.rot90(picked[0], 2)
    east = np.rot90(picked[1], 1)
    south = picked[2]
    west = np.rot90(picked[3], 3)
    ne = np.rot90(picked[4], 2)[:, :W]
    se = picked[5][:, :W]
    sw = picked[6][:, SIDE - W :]
    nw = np.rot90(picked[7], 2)[:, SIDE - W :]
    return np.concatenate(
        [
            np.concatenate([nw, north, ne], 1),
            np.concatenate([west, field, east], 1),
            np.concatenate([sw, south, se], 1),
        ],
        0,
    )


def column_of(m):
    if m < SIDE:
        return m + W
    if m < SIDE + W:
        return m - SIDE
    if m < SIDE + 2 * W:
        return m
    return -1


@functools.lru_cache(None)
def static_tables():
    where = stripe_table()
    codes = np.arange(8 * W * SIDE).reshape(8, W, SIDE)
    padded = np_pad(np.full((SIDE, SIDE), -1), codes)

    def spot(code):
        k, w, l = np.unravel_index(code, (8, W, SIDE))
        i, a = where[w, l]
        return (k, i * CELLS + a) if k < 4 else (k - 4, i * CELLS + 12)

    index = {name: np.full(256, -1, np.int64) for name in INDEX}

    def places(p_list, m_list, names):
        for ip, p in enumerate(p_list):
            for im, m in enumerate(m_list):
                q = column_of(m)
                if q < 0 or padded[p, q] < 0:
                    continue
                k, row = spot(padded[p, q])
                index[names[k]][row] = ip * len(m_list) + im

    places([0, 1, 2], range(KROW), {0: "top0", 3: "top3"})
    places([67, 68, 69], range(KROW), {2: "bot2", 1: "bot1"})
    places(range(W, W + SIDE), range(SIDE, KROW), {3: "side3", 1: "side1"})

    cells = np.arange(SIDE * SIDE).reshape(SIDE, SIDE)
    bands = {
        "north": (cells[:W], SIDE, 0, 0),
        "east": (np.rot90(cells[:, SIDE - W :], 1), 16, 0, 48),
        "south": (np.rot90(cells[SIDE - W :], 2), SIDE, SIDE - W, 0),
        "west": (np.rot90(cells[:, :W], 3), 16, 0, 0),
    }
    for name, (band, pitch, row0, col0) in bands.items():
        for w in range(W):
            for l in range(SIDE):
                i, j = divmod(int(band[w, l]), SIDE)
                st, a = where[w, l]
                index[name][st * CELLS + a] = (i - row0) * pitch + j - col0
    table = np.stack([index[name] for name in INDEX]).astype(np.int32)
    by_row = np.full((16, 256), -1, np.int32)
    by_row[: len(INDEX)] = table
    by_col = np.full((256, 128), -1, np.int32)
    by_col[:, : len(INDEX)] = table.T
    return by_row, by_col


def spread(by_row, name, n):
    k = INDEX.index(name)
    place = lax.broadcasted_iota(jnp.int32, (n, 256), 0)
    return (place == by_row[k : k + 1]).astype(F32).astype(BF)


def gather(by_col, name, n):
    k = INDEX.index(name)
    place = lax.broadcasted_iota(jnp.int32, (256, n), 1)
    return (place == by_col[:, k : k + 1]).astype(F32).astype(BF)


@functools.lru_cache(None)
def dft_tables():
    n = 2 * NFREQ
    theta = 2 * np.pi * (np.arange(NFREQ) + 0.5) / n

    def cs(pos):
        ang = theta[:, None] * np.asarray(pos, np.float64)[None, :]
        live = (np.asarray(pos) >= 0)[None, :]
        return np.cos(ang) * live, np.sin(ang) * live

    def inverse(c, s):
        both = np.stack([c.reshape(5, 8, -1), -s.reshape(5, 8, -1)], 1)
        return (2 / n) * both.reshape(2 * NFREQ, -1).T

    cols = [column_of(m) for m in range(KROW)]
    c, s = cs(cols)
    fwd_x = np.concatenate([c, -s, c - s], 0)
    inv_p = inverse(c, s)
    c, s = cs(np.arange(SIDE))
    inv_y = inverse(c, s)
    fwd_g = np.concatenate([c, -s, c - s, c + s], 0)
    taps = [0, 1, 2, 3, 4, 5, 6, -1]
    c, s = cs(taps)
    fwd_k = np.concatenate([c, s, c + s, c, -s, c - s], 0)
    inv_k = (2 / n) * np.concatenate([c + s, c - s, -s], 0).T
    return (
        fwd_x.astype(jnp.bfloat16),
        inv_y.astype(jnp.bfloat16),
        fwd_g.astype(jnp.bfloat16),
        inv_p.astype(jnp.bfloat16),
        fwd_k.astype(np.float32),
        inv_k.astype(np.float32),
    )


def dot(a, b):
    return jnp.dot(a, b, preferred_element_type=F32)


def dot_nt(a, b):
    return lax.dot_general(a, b, (((1,), (1,)), ((), ())), preferred_element_type=F32)


def dot_tn(a, b):
    return lax.dot_general(a, b, (((0,), (0,)), ((), ())), preferred_element_type=F32)


def dot_exact(a, b):
    return jnp.dot(a, b, preferred_element_type=F32, precision=lax.Precision.HIGHEST)


def peer(me, off, n):
    return lax.rem(me + off, n)


def greet(axes):
    barrier = pltpu.get_barrier_semaphore()
    total = 0
    for axis, n in axes:
        me = lax.axis_index(axis)
        for off in range(1, n):
            pl.semaphore_signal(
                barrier, inc=1, device_id={axis: peer(me, off, n)}, device_id_type=MESH
            )
            total += 1
    return barrier, total


def exchange(axis, n, src_of, dst, send, recv):
    me = lax.axis_index(axis)
    copies = []
    for off in range(1, n):
        to = peer(me, off, n)
        copy = pltpu.make_async_remote_copy(
            src_ref=src_of(to),
            dst_ref=dst(me),
            send_sem=send.at[off],
            recv_sem=recv.at[off],
            device_id={axis: to},
            device_id_type=MESH,
        )
        copy.start()
        copies.append(copy)
    return copies


def finish(copies):
    for copy in copies:
        copy.wait()


PACKED = (6, TILES, CELLS, 128)


def pack(ref, value):
    ref[0:4] = value[..., 0:128]
    ref[4:6] = jnp.concatenate([value[0:2, :, :, 128:CH], value[2:4, :, :, 128:CH]], axis=-1)


def unpack(ref):
    low = ref[0:4].reshape(1024, 128)
    pair = ref[4:6].reshape(512, 128)
    high = jnp.concatenate([pair[:, 0:64], pair[:, 64:128]], axis=0)
    return jnp.concatenate([low, high], axis=-1)


def halo_kernel(field, by_col, target, out, own, got, routed, back, s1, r1, s2, r2):
    me = lax.axis_index("tile")
    barrier, total = greet((("tile", TILES),))
    bands = jnp.concatenate(
        [
            dot(gather(by_col, "north", W * SIDE), field[0:W].reshape(W * SIDE, CH)),
            dot(gather(by_col, "east", 1024), field[:, 48:64].reshape(1024, CH)),
            dot(gather(by_col, "south", W * SIDE), field[SIDE - W :].reshape(W * SIDE, CH)),
            dot(gather(by_col, "west", 1024), field[:, 0:16].reshape(1024, CH)),
        ],
        axis=0,
    )
    pack(own, bands.astype(BF).reshape(4, TILES, CELLS, CH))
    pl.semaphore_wait(barrier, total)
    copies = exchange("tile", TILES, lambda to: own.at[:, to], lambda m: got.at[:, m], s1, r1)
    got[:, me] = own[:, me]
    columns = lax.broadcasted_iota(jnp.int32, (1024, 1024), 1)
    route = (columns == target[...]).astype(F32).astype(BF)
    finish(copies)
    pack(routed, dot(route, unpack(got)).astype(BF).reshape(4, TILES, CELLS, CH))
    copies = exchange("tile", TILES, lambda to: routed.at[:, to], lambda m: back.at[:, m], s2, r2)
    back[:, me] = routed[:, me]
    finish(copies)
    out[...] = unpack(back).reshape(4, 256, CH)


def halo(fields, target_col):
    _, by_col = static_tables()
    vm = pl.BlockSpec(memory_space=pltpu.VMEM)
    block = pltpu.VMEM(PACKED, BF)
    sem = pltpu.SemaphoreType.DMA((TILES,))
    return pl.pallas_call(
        halo_kernel,
        out_shape=jax.ShapeDtypeStruct((4, 256, CH), BF),
        in_specs=[vm] * 3,
        out_specs=vm,
        scratch_shapes=[block, block, block, block, sem, sem, sem, sem],
        compiler_params=pltpu.CompilerParams(
            collective_id=0, has_side_effects=True, vmem_limit_bytes=24 * 2**20
        ),
        name="halo",
    )(fields, jnp.asarray(by_col), target_col)


def return_kernel(
    slots, target, wsrc, out, wout, got, routed, back, wa, pa, wb, pc, wc, wd, *sems
):
    s1, r1, s2, r2, sa, ra, sb, rb, sc, rc, sd, rd = sems
    me = lax.axis_index("tile")
    md = lax.axis_index("dp")
    ndp = wa.shape[0]
    owners = pa.shape[0]
    barrier, total = greet((("tile", TILES), ("dp", ndp)))
    pl.semaphore_wait(barrier, total)
    ca = exchange("dp", ndp, lambda to: wsrc.at[to], lambda m: wa.at[m], sa, ra)
    c1 = exchange("tile", TILES, lambda to: slots.at[:, to], lambda m: got.at[:, m], s1, r1)
    got[:, me] = slots[:, me]
    wa[md] = wsrc[md]
    rows = lax.broadcasted_iota(jnp.int32, (1024, 1024), 0)
    route = (rows == target[...]).astype(F32).astype(BF)

    finish(ca)
    part = wa[0].astype(F32)
    for j in range(1, ndp):
        part = part + wa[j].astype(F32)
    pa[...] = part.reshape(owners, WBLOCK, 128)

    def share(off, src, dst, send, recv):
        to = peer(me, off, TILES)
        return pltpu.make_async_remote_copy(
            src_ref=src,
            dst_ref=dst,
            send_sem=send.at[off],
            recv_sem=recv.at[off],
            device_id={"tile": to},
            device_id_type=MESH,
        )

    def to_owner(off):
        to = peer(me, off, TILES)
        return to, share(off, pa.at[lax.rem(to, owners)], wb.at[me], sb, rb)

    for off in range(1, TILES):
        to, copy = to_owner(off)
        pl.when(to < owners)(copy.start)

    @pl.when(me < owners)
    def _():
        wb[me] = pa[lax.rem(me, owners)]

    finish(c1)
    pack(routed, dot(route, unpack(got)).astype(BF).reshape(4, TILES, CELLS, CH))
    c2 = exchange("tile", TILES, lambda to: routed.at[:, to], lambda m: back.at[:, m], s2, r2)
    back[:, me] = routed[:, me]

    for off in range(1, TILES):
        to, copy = to_owner(off)
        pl.when(to < owners)(copy.wait_send)
        pl.when(me < owners)(copy.wait_recv)

    mine = lax.rem(me, owners)

    @pl.when(me < owners)
    def _():
        total = wb[0]
        for j in range(1, TILES):
            total = total + wb[j]
        pc[...] = total.astype(BF)
        wc[mine] = total.astype(BF)
        for off in range(1, TILES):
            share(off, pc, wc.at[mine], sc, rc).start()

    for off in range(1, TILES):
        copy = share(off, pc, wc.at[mine], sc, rc)
        pl.when(me < owners)(copy.wait_send)
        pl.when(peer(me, TILES - off, TILES) < owners)(copy.wait_recv)

    block = wc[...].reshape(owners * WBLOCK, 128)
    pd = wa.at[0]
    pd[...] = block
    cd = exchange("dp", ndp, lambda to: pd, lambda m: wd.at[m], sd, rd)
    wd[md] = block
    finish(c2)
    out[...] = unpack(back).reshape(4, 256, CH)
    finish(cd)
    wout[...] = wd[...].reshape(WROWS, 128)


def send_back(slots, target_row, wsrc, ndp):
    vm = pl.BlockSpec(memory_space=pltpu.VMEM)
    block = pltpu.VMEM(PACKED, BF)
    sem = pltpu.SemaphoreType.DMA((TILES,))
    sem_dp = pltpu.SemaphoreType.DMA((ndp,))
    dp_rows = WROWS // ndp
    owners = dp_rows // WBLOCK
    return pl.pallas_call(
        return_kernel,
        out_shape=(
            jax.ShapeDtypeStruct((4, 256, CH), BF),
            jax.ShapeDtypeStruct((WROWS, 128), BF),
        ),
        in_specs=[vm] * 3,
        out_specs=(vm, vm),
        scratch_shapes=[
            block,
            block,
            block,
            pltpu.VMEM((ndp, dp_rows, 128), BF),
            pltpu.VMEM((owners, WBLOCK, 128), F32),
            pltpu.VMEM((TILES, WBLOCK, 128), F32),
            pltpu.VMEM((WBLOCK, 128), BF),
            pltpu.VMEM((owners, WBLOCK, 128), BF),
            pltpu.VMEM((ndp, dp_rows, 128), BF),
        ]
        + [sem] * 4
        + [sem_dp] * 2
        + [sem] * 4
        + [sem_dp] * 2,
        compiler_params=pltpu.CompilerParams(
            collective_id=1, has_side_effects=True, vmem_limit_bytes=24 * 2**20
        ),
        name="send_back",
    )(slots, target_row, wsrc)


LANES = ((0, 128), (128, 64))


def taps(xs, ks):
    acc = xs[0] * ks[0]
    for x, k in zip(xs[1:], ks[1:]):
        acc = acc + x * k
    return acc


def real_imag(a, b, c):
    return jnp.concatenate([a - b, c - a - b], axis=0).astype(BF)


def block_kernel(
    fields,
    cot,
    hal,
    by_row,
    by_col,
    fwd_x,
    inv_y,
    fwd_g,
    inv_p,
    fwd_k,
    inv_k,
    kernel,
    conv_bias,
    gain,
    nbias,
    w_exp,
    b_exp,
    w_red,
    b_red,
    lscale,
    mixed,
    direct,
    slots,
    wout,
    xpad,
    x3,
    y2,
    g4,
    kpad,
    kf,
    m3,
    egrad,
    rgrad,
    psides,
    ptop,
    pbot,
):
    conv_bias, gain, nbias, b_exp, b_red, lscale = (
        ref[...].reshape(1, -1) for ref in (conv_bias, gain, nbias, b_exp, b_red, lscale)
    )
    for u in range(7):
        kpad[0:7] = kernel[u]
        kpad[7:8] = jnp.zeros((1, CH), F32)
        kf[u] = dot_exact(fwd_k[...], kpad[...])
    xpad[W : W + SIDE, 0:SIDE] = fields[...]

    def put(n, *parts):
        return sum(dot(spread(by_row, name, n), hal[k]) for name, k in parts).astype(BF)

    xpad[0:W] = put(W * KROW, ("top0", 0), ("top3", 3)).reshape(W, KROW, CH)
    xpad[W + SIDE :] = put(W * KROW, ("bot2", 2), ("bot1", 1)).reshape(W, KROW, CH)
    xpad[W : W + SIDE, SIDE:] = put(SIDE * 16, ("side3", 3), ("side1", 1)).reshape(SIDE, 16, CH)

    def to_freq(r, _):
        x3[r] = dot(fwd_x[...], xpad[r])
        return 0

    lax.fori_loop(0, EXT, to_freq, 0, unroll=14)

    for l0, lw in LANES:
        for fb in range(5):
            rows = [slice(40 * t + 8 * fb, 40 * t + 8 * fb + 8) for t in range(3)]
            lanes = slice(l0, l0 + lw)
            kk = [[kf[u, rows[t], lanes] for t in range(3)] for u in range(7)]

            def conv(ib, _, fb=fb, rows=rows, lanes=lanes, kk=kk):
                i0 = ib * 4
                prods = []
                for t in range(3):
                    xs = [x3[i0 + r, rows[t], lanes] for r in range(10)]
                    prods.append([taps(xs[d : d + 7], [k[t] for k in kk]) for d in range(4)])
                for d in range(4):
                    y2[i0 + d, 16 * fb : 16 * fb + 16, lanes] = real_imag(*(p[d] for p in prods))
                return 0

            lax.fori_loop(0, SIDE // 4, conv, 0, unroll=2)

    egrad[...] = jnp.zeros_like(egrad)
    rgrad[...] = jnp.zeros_like(rgrad)
    g4[0:6] = jnp.zeros((6, 4 * NFREQ, CH), F32)
    g4[6 + SIDE :] = jnp.zeros((6, 4 * NFREQ, CH), F32)
    step = 16
    n = step * SIDE

    def chunk(ic, _):
        i0 = pl.multiple_of(ic * step, step)
        conv_out = jnp.concatenate(
            [dot(inv_y[...], y2[i0 + d]) for d in range(step)], axis=0
        )
        conv_out = conv_out + conv_bias
        shifted = conv_out - jnp.mean(conv_out, axis=-1, keepdims=True)
        inv_std = lax.rsqrt(jnp.mean(shifted * shifted, axis=-1, keepdims=True) + 1e-06)
        centred = shifted * inv_std
        normed = (centred * gain + nbias).astype(BF)
        pre = dot(normed, w_exp[...]) + b_exp
        size = jnp.abs(pre)
        t = 1.0 / (1.0 + (0.3275911 * math.sqrt(0.5)) * size)
        dens = jnp.exp(-0.5 * pre * pre)
        poly = t * (
            0.127414796
            + t * (-0.142248368 + t * (0.7107068705 + t * (-0.7265760135 + t * 0.5307027145)))
        )
        tail = poly * dens
        phi = jnp.where(pre >= 0, 1.0 - tail, tail)
        act = (pre * phi).astype(BF)
        slope = phi + pre * (dens * 0.3989422804014327)
        cot_c = cot[pl.ds(i0, step)].reshape(n, CH).astype(F32)
        branch = dot_nt(act, w_red[...]) + b_red
        mix = fields[pl.ds(i0, step)].reshape(n, CH).astype(F32) + lscale * branch
        mixed[pl.ds(i0, step)] = mix.astype(BF).reshape(step, SIDE, CH)
        bgrad = (lscale * cot_c).astype(BF)
        pre_grad = (dot(bgrad, w_red[...]) * slope).astype(BF)
        rgrad[...] += dot_tn(bgrad, act)
        egrad[...] += dot_tn(normed, pre_grad)
        ngrad = dot_nt(pre_grad, w_exp[...]) * gain
        m1 = jnp.mean(ngrad, axis=-1, keepdims=True)
        m2 = jnp.mean(ngrad * centred, axis=-1, keepdims=True)
        cgrad = (inv_std * (ngrad - m1 - centred * m2)).astype(BF)
        for d in range(step):
            g4[6 + i0 + d] = dot(fwd_g[...], cgrad[d * SIDE : (d + 1) * SIDE])
        return 0

    lax.fori_loop(0, SIDE // step, chunk, 0)

    for l0, lw in LANES:
        for fb in range(5):
            rows = [slice(40 * t + 8 * fb, 40 * t + 8 * fb + 8) for t in range(4)]
            grow = (rows[0], rows[1], rows[3])
            lanes = slice(l0, l0 + lw)

            def kgrad(ib, accs, rows=rows, lanes=lanes, grow=grow):
                i0 = ib * 4
                accs = list(accs)
                for t in range(3):
                    xs = [x3[i0 + r, rows[t], lanes] for r in range(10)]
                    for d in range(4):
                        g = g4[6 + i0 + d, grow[t], lanes]
                        for u in range(7):
                            accs[7 * t + u] = accs[7 * t + u] + xs[d + u] * g
                return tuple(accs)

            zero = jnp.zeros((8, lw), F32)
            accs = lax.fori_loop(0, SIDE // 4, kgrad, (zero,) * 21, unroll=2)
            for t in range(3):
                for u in range(7):
                    m3[u, rows[t], lanes] = accs[7 * t + u]

            kk = [
                [kf[u, 120 + 40 * t + 8 * fb : 128 + 40 * t + 8 * fb, lanes] for t in range(3)]
                for u in range(7)
            ]

            def pconv(ib, _, fb=fb, rows=rows, lanes=lanes, kk=kk):
                p0 = ib * 5
                prods = []
                for t in range(3):
                    gs = [g4[p0 + r, rows[t], lanes] for r in range(11)]
                    back = [k[t] for k in kk][::-1]
                    prods.append([taps(gs[d : d + 7], back) for d in range(5)])
                for d in range(5):
                    y2[p0 + d, 16 * fb : 16 * fb + 16, lanes] = real_imag(*(p[d] for p in prods))
                return 0

            lax.fori_loop(0, EXT // 5, pconv, 0, unroll=2)

    for p in range(W):
        ptop[p] = dot(inv_p[...], y2[p]).astype(BF)
        pbot[p] = dot(inv_p[...], y2[W + SIDE + p]).astype(BF)

    def from_freq(i, _):
        back = dot(inv_p[...], y2[i + W])
        direct[i] = (cot[i].astype(F32) + back[0:SIDE]).astype(BF)
        psides[i] = back[SIDE:].astype(BF)
        return 0

    lax.fori_loop(0, SIDE, from_freq, 0, unroll=8)

    top = ptop[...].reshape(W * KROW, CH)
    bot = pbot[...].reshape(W * KROW, CH)
    sides = psides[...].reshape(SIDE * 16, CH)


    def take(*parts):
        total = sum(dot(gather(by_col, name, part.shape[0]), part) for name, part in parts)
        return total.astype(BF).reshape(1, TILES, CELLS, CH)

    taken = [
        take(("top0", top)),
        take(("side1", sides), ("bot1", bot)),
        take(("bot2", bot)),
        take(("side3", sides), ("top3", top)),
    ]
    pack(slots, jnp.concatenate(taken, axis=0))

    for g in range(3):
        lanes = slice(128 * g, 128 * g + 128)
        wout[192 * g : 192 * g + 192] = egrad[:, lanes].astype(BF)
        wout[576 + 192 * g : 768 + 192 * g] = rgrad[:, lanes].astype(BF)
    kg = jnp.concatenate([dot_exact(inv_k[...], m3[u]) for u in range(7)], axis=0)
    kg = jnp.concatenate([kg, jnp.zeros((8, CH), F32)], axis=0).astype(BF)
    wout[1152:1216] = kg[:, 0:128]
    wout[1216:1280] = jnp.concatenate([kg[:, 128:192], jnp.zeros((64, 64), BF)], axis=1)


def block(fields, cotangent, hal, params):
    index = [jnp.asarray(t) for t in static_tables()]
    tables = [jnp.asarray(t) for t in dft_tables()]
    vm = pl.BlockSpec(memory_space=pltpu.VMEM)
    args = [fields, cotangent, hal, *index, *tables, *params]
    return pl.pallas_call(
        block_kernel,
        out_shape=(
            jax.ShapeDtypeStruct((SIDE, SIDE, CH), BF),
            jax.ShapeDtypeStruct((SIDE, SIDE, CH), BF),
            jax.ShapeDtypeStruct(PACKED, BF),
            jax.ShapeDtypeStruct((WROWS, 128), BF),
        ),
        in_specs=[vm] * len(args),
        out_specs=(vm,) * 4,
        scratch_shapes=[
            pltpu.VMEM((EXT, KROW, CH), BF),
            pltpu.VMEM((EXT, 3 * NFREQ, CH), F32),
            pltpu.VMEM((EXT, 2 * NFREQ, CH), BF),
            pltpu.VMEM((SIDE + 12, 4 * NFREQ, CH), F32),
            pltpu.VMEM((8, CH), F32),
            pltpu.VMEM((7, 6 * NFREQ, CH), F32),
            pltpu.VMEM((7, 3 * NFREQ, CH), F32),
            pltpu.VMEM((CH, HID), F32),
            pltpu.VMEM((CH, HID), F32),
            pltpu.VMEM((SIDE, 16, CH), BF),
            pltpu.VMEM((W, KROW, CH), BF),
            pltpu.VMEM((W, KROW, CH), BF),
        ],
        compiler_params=pltpu.CompilerParams(vmem_limit_bytes=60 * 2**20),
        name="block",
    )(*args)


def last_kernel(scale, direct, bands, wsum, by_row, out, kgrad, egrad, rgrad):
    north = dot(spread(by_row, "north", W * SIDE), bands[0]).reshape(W, SIDE, CH)
    south = dot(spread(by_row, "south", W * SIDE), bands[2]).reshape(W, SIDE, CH)
    east = dot(spread(by_row, "east", 1024), bands[1]).reshape(SIDE, 16, CH)
    west = dot(spread(by_row, "west", 1024), bands[3]).reshape(SIDE, 16, CH)
    mid = slice(W, SIDE - W)
    out[mid, 16:48] = direct[mid, 16:48]
    out[mid, 0:16] = (direct[mid, 0:16].astype(F32) + west[mid]).astype(BF)
    out[mid, 48:64] = (direct[mid, 48:64].astype(F32) + east[mid]).astype(BF)
    zero = jnp.zeros((W, 32, CH), F32)
    for rows, add in ((slice(0, W), north), (slice(SIDE - W, SIDE), south)):
        more = jnp.concatenate([west[rows], zero, east[rows]], axis=1)
        out[rows] = (direct[rows].astype(F32) + add + more).astype(BF)
    for g in range(3):
        lanes = slice(128 * g, 128 * g + 128)
        egrad[:, lanes] = wsum[192 * g : 192 * g + 192].astype(F32) * scale
        rgrad[:, lanes] = wsum[576 + 192 * g : 768 + 192 * g].astype(F32) * scale
    low = wsum[1152:1216].astype(F32) * scale
    high = wsum[1216:1280].astype(F32) * scale
    for u in range(7):
        kgrad[u, :, 0:128] = low[8 * u : 8 * u + 7]
        kgrad[u, :, 128:192] = high[8 * u : 8 * u + 7, 0:64]


def last(direct, bands, wsum, scale):
    by_row, _ = static_tables()
    vm = pl.BlockSpec(memory_space=pltpu.VMEM)
    return pl.pallas_call(
        functools.partial(last_kernel, scale),
        out_shape=(
            jax.ShapeDtypeStruct((SIDE, SIDE, CH), BF),
            jax.ShapeDtypeStruct((7, 7, CH), F32),
            jax.ShapeDtypeStruct((CH, HID), F32),
            jax.ShapeDtypeStruct((CH, HID), F32),
        ),
        in_specs=[vm] * 4,
        out_specs=(vm,) * 4,
        compiler_params=pltpu.CompilerParams(vmem_limit_bytes=24 * 2**20),
        name="last",
    )(direct, bands, wsum, jnp.asarray(by_row))


def routing(neighbors, rotations):
    me = lax.axis_index("tile")
    offsets = jnp.array(OFFSETS, jnp.int32)[None, :]
    side = (rotations + offsets) % 4
    base = jnp.where(neighbors >= 0, side * 256 + neighbors * CELLS, -(1 << 20)).T
    right = jnp.where(me >= 7, 11, -(1 << 20))
    left = jnp.where(me <= 8, 0, -(1 << 20))
    corner_row = jnp.stack([right, left, right, left])[:, None]
    cell = jnp.arange(CELLS, dtype=jnp.int32)[None, None, :]
    edge = base[0:4][:, :, None] + cell
    corner = (base[4:8] + corner_row)[:, :, None]
    return jnp.where(cell < 12, edge, jnp.where(cell == 12, corner, -1)).astype(jnp.int32)


def on_device(
    fields,
    cotangent,
    kernel,
    conv_bias,
    norm_gain,
    norm_bias,
    w_expand,
    bias_expand,
    w_reduce,
    bias_reduce,
    layer_scale,
    neighbors,
    rotations,
):
    ndp = lax.axis_size("dp")
    field = fields.reshape(SIDE, SIDE, CH)
    cot = cotangent.reshape(SIDE, SIDE, CH)
    target = routing(neighbors, rotations)
    hal = halo(field, target.reshape(1024, 1))
    params = [
        kernel,
        conv_bias,
        norm_gain,
        norm_bias,
        w_expand,
        bias_expand,
        w_reduce.T,
        bias_reduce,
        layer_scale,
    ]
    mixed, direct, slots, wgrad = block(field, cot, hal, params)
    bands, wsum = send_back(
        slots, target.reshape(1, 1024), wgrad.reshape(ndp, WROWS // ndp, 128), ndp
    )
    scale = 1.0 / math.sqrt(ndp * TILES * SIDE * SIDE)
    input_grad, kgrad, egrad, rgrad = last(direct, bands, wsum, scale)
    return (
        mixed.reshape(fields.shape),
        input_grad.reshape(fields.shape),
        kgrad,
        egrad,
        rgrad.T,
    )


def solution(mesh):
    split = P("dp", "tile", None, None, None)
    return jax.shard_map(
        on_device,
        mesh=mesh,
        in_specs=(split, split) + (P(),) * 11,
        out_specs=(split, split, P(), P(), P()),
        check_vma=False,
    )
```

```python
import functools
import math

import jax
import jax.numpy as jnp
import numpy as np
from jax import lax
from jax.experimental import pallas as pl
from jax.experimental.pallas import tpu as pltpu
from jax.sharding import PartitionSpec as P

OFFSETS = (2, 3, 0, 1, 2, 0, 0, 2)
SIDE = 64
W = 3
CH = 192
HID = 384
TILES = 16
CELLS = 16
NFREQ = 40
KROW = 80
EXT = SIDE + 2 * W
BF = jnp.bfloat16
F32 = jnp.float32
MESH = pl.DeviceIdType.MESH
WROWS = 1280
WBLOCK = 16
INDEX = ("top0", "top3", "bot2", "bot1", "side3", "side1", "north", "east", "south", "west")


def stripe_table():
    where = np.zeros((W, SIDE, 2), np.int64)
    used = {i: set() for i in range(16)}
    rest = []
    for w in range(W):
        for l in range(SIDE):
            if l < W:
                spot = (w * W + l, 0)
            elif l >= SIDE - W:
                spot = (7 + w * W + l - (SIDE - W), 11)
            else:
                rest.append((w, l))
                continue
            where[w, l] = spot
            used[spot[0]].add(spot[1])
    free = [(i, a) for i in range(16) for a in range(12) if a not in used[i]]
    for (w, l), spot in zip(rest, free):
        where[w, l] = spot
    return where


def np_pad(field, picked):
    north = np.rot90(picked[0], 2)
    east = np.rot90(picked[1], 1)
    south = picked[2]
    west = np.rot90(picked[3], 3)
    ne = np.rot90(picked[4], 2)[:, :W]
    se = picked[5][:, :W]
    sw = picked[6][:, SIDE - W :]
    nw = np.rot90(picked[7], 2)[:, SIDE - W :]
    return np.concatenate(
        [
            np.concatenate([nw, north, ne], 1),
            np.concatenate([west, field, east], 1),
            np.concatenate([sw, south, se], 1),
        ],
        0,
    )


def column_of(m):
    if m < SIDE:
        return m + W
    if m < SIDE + W:
        return m - SIDE
    if m < SIDE + 2 * W:
        return m
    return -1


@functools.lru_cache(None)
def static_tables():
    where = stripe_table()
    codes = np.arange(8 * W * SIDE).reshape(8, W, SIDE)
    padded = np_pad(np.full((SIDE, SIDE), -1), codes)

    def spot(code):
        k, w, l = np.unravel_index(code, (8, W, SIDE))
        i, a = where[w, l]
        return (k, i * CELLS + a) if k < 4 else (k - 4, i * CELLS + 12)

    index = {name: np.full(256, -1, np.int64) for name in INDEX}

    def places(p_list, m_list, names):
        for ip, p in enumerate(p_list):
            for im, m in enumerate(m_list):
                q = column_of(m)
                if q < 0 or padded[p, q] < 0:
                    continue
                k, row = spot(padded[p, q])
                index[names[k]][row] = ip * len(m_list) + im

    places([0, 1, 2], range(KROW), {0: "top0", 3: "top3"})
    places([67, 68, 69], range(KROW), {2: "bot2", 1: "bot1"})
    places(range(W, W + SIDE), range(SIDE, KROW), {3: "side3", 1: "side1"})

    cells = np.arange(SIDE * SIDE).reshape(SIDE, SIDE)
    bands = {
        "north": (cells[:W], SIDE, 0, 0),
        "east": (np.rot90(cells[:, SIDE - W :], 1), 16, 0, 48),
        "south": (np.rot90(cells[SIDE - W :], 2), SIDE, SIDE - W, 0),
        "west": (np.rot90(cells[:, :W], 3), 16, 0, 0),
    }
    for name, (band, pitch, row0, col0) in bands.items():
        for w in range(W):
            for l in range(SIDE):
                i, j = divmod(int(band[w, l]), SIDE)
                st, a = where[w, l]
                index[name][st * CELLS + a] = (i - row0) * pitch + j - col0
    table = np.stack([index[name] for name in INDEX]).astype(np.int32)
    by_row = np.full((16, 256), -1, np.int32)
    by_row[: len(INDEX)] = table
    by_col = np.full((256, 128), -1, np.int32)
    by_col[:, : len(INDEX)] = table.T
    return by_row, by_col


def spread(by_row, name, n):
    k = INDEX.index(name)
    place = lax.broadcasted_iota(jnp.int32, (n, 256), 0)
    return (place == by_row[k : k + 1]).astype(F32).astype(BF)


def gather(by_col, name, n):
    k = INDEX.index(name)
    place = lax.broadcasted_iota(jnp.int32, (256, n), 1)
    return (place == by_col[:, k : k + 1]).astype(F32).astype(BF)


@functools.lru_cache(None)
def dft_tables():
    n = 2 * NFREQ
    theta = 2 * np.pi * (np.arange(NFREQ) + 0.5) / n

    def cs(pos):
        ang = theta[:, None] * np.asarray(pos, np.float64)[None, :]
        live = (np.asarray(pos) >= 0)[None, :]
        return np.cos(ang) * live, np.sin(ang) * live

    def inverse(c, s):
        both = np.stack([c.reshape(5, 8, -1), -s.reshape(5, 8, -1)], 1)
        return (2 / n) * both.reshape(2 * NFREQ, -1).T

    cols = [column_of(m) for m in range(KROW)]
    c, s = cs(cols)
    fwd_x = np.concatenate([c, -s, c - s], 0)
    inv_p = inverse(c, s)
    c, s = cs(np.arange(SIDE))
    inv_y = inverse(c, s)
    fwd_g = np.concatenate([c, -s, c - s, c + s], 0)
    taps = [0, 1, 2, 3, 4, 5, 6, -1]
    c, s = cs(taps)
    fwd_k = np.concatenate([c, s, c + s, c, -s, c - s], 0)
    inv_k = (2 / n) * np.concatenate([c + s, c - s, -s], 0).T
    return (
        fwd_x.astype(jnp.bfloat16),
        inv_y.astype(jnp.bfloat16),
        fwd_g.astype(jnp.bfloat16),
        inv_p.astype(jnp.bfloat16),
        fwd_k.astype(np.float32),
        inv_k.astype(np.float32),
    )


def dot(a, b):
    return jnp.dot(a, b, preferred_element_type=F32)


def dot_nt(a, b):
    return lax.dot_general(a, b, (((1,), (1,)), ((), ())), preferred_element_type=F32)


def dot_tn(a, b):
    return lax.dot_general(a, b, (((0,), (0,)), ((), ())), preferred_element_type=F32)


def dot_exact(a, b):
    return jnp.dot(a, b, preferred_element_type=F32, precision=lax.Precision.HIGHEST)


def peer(me, off, n):
    return lax.rem(me + off, n)


def greet(axes):
    barrier = pltpu.get_barrier_semaphore()
    total = 0
    for axis, n in axes:
        me = lax.axis_index(axis)
        for off in range(1, n):
            pl.semaphore_signal(
                barrier, inc=1, device_id={axis: peer(me, off, n)}, device_id_type=MESH
            )
            total += 1
    return barrier, total


def exchange(axis, n, src_of, dst, send, recv):
    me = lax.axis_index(axis)
    copies = []
    for off in range(1, n):
        to = peer(me, off, n)
        copy = pltpu.make_async_remote_copy(
            src_ref=src_of(to),
            dst_ref=dst(me),
            send_sem=send.at[off],
            recv_sem=recv.at[off],
            device_id={axis: to},
            device_id_type=MESH,
        )
        copy.start()
        copies.append(copy)
    return copies


def finish(copies):
    for copy in copies:
        copy.wait()


PACKED = (6, TILES, CELLS, 128)


def pack(ref, value):
    ref[0:4] = value[..., 0:128]
    ref[4:6] = jnp.concatenate([value[0:2, :, :, 128:CH], value[2:4, :, :, 128:CH]], axis=-1)


def unpack(ref):
    low = ref[0:4].reshape(1024, 128)
    pair = ref[4:6].reshape(512, 128)
    high = jnp.concatenate([pair[:, 0:64], pair[:, 64:128]], axis=0)
    return jnp.concatenate([low, high], axis=-1)


LANES = ((0, 128), (128, 64))


def taps(xs, ks):
    acc = xs[0] * ks[0]
    for x, k in zip(xs[1:], ks[1:]):
        acc = acc + x * k
    return acc


def real_imag(a, b, c):
    return jnp.concatenate([a - b, c - a - b], axis=0).astype(BF)


def main_kernel(
    fields,
    cot_hbm,
    by_row,
    by_col,
    target_col,
    target_row,
    fwd_x,
    inv_y,
    fwd_g,
    inv_p,
    fwd_k,
    inv_k,
    kernel,
    conv_bias,
    gain,
    nbias,
    w_exp,
    b_exp,
    w_red,
    b_red,
    lscale,
    mixed,
    direct,
    bands,
    wout,
    xpad,
    x3,
    y2,
    g4,
    kpad,
    kf,
    m3,
    egrad,
    rgrad,
    psides,
    ptop,
    pbot,
    cot,
    mix_out,
    hal,
    own,
    got,
    routed,
    back,
    own2,
    got2,
    routed2,
    back2,
    wsrc,
    wa,
    pa,
    wb,
    pc,
    wc,
    wd,
    io_sem,
    *sems,
):
    s1, r1, s2, r2, s3, r3, s4, r4, sb, rb, sc, rc, sa, ra, sd, rd = sems
    me = lax.axis_index("tile")
    md = lax.axis_index("dp")
    ndp = wa.shape[0]
    dp_rows = wa.shape[1]
    owners = pa.shape[0]
    barrier, total = greet((("tile", TILES), ("dp", ndp)))
    load_cot = pltpu.make_async_copy(cot_hbm, cot, io_sem.at[0])
    load_cot.start()
    bands_own = jnp.concatenate(
        [
            dot(gather(by_col, "north", W * SIDE), fields[0:W].reshape(W * SIDE, CH)),
            dot(gather(by_col, "east", 1024), fields[:, 48:64].reshape(1024, CH)),
            dot(gather(by_col, "south", W * SIDE), fields[SIDE - W :].reshape(W * SIDE, CH)),
            dot(gather(by_col, "west", 1024), fields[:, 0:16].reshape(1024, CH)),
        ],
        axis=0,
    )
    pack(own, bands_own.astype(BF).reshape(4, TILES, CELLS, CH))
    pl.semaphore_wait(barrier, total)
    copies = exchange("tile", TILES, lambda to: own.at[:, to], lambda m: got.at[:, m], s1, r1)
    got[:, me] = own[:, me]
    conv_bias, gain, nbias, b_exp, b_red, lscale = (
        ref[...].reshape(1, -1) for ref in (conv_bias, gain, nbias, b_exp, b_red, lscale)
    )
    for u in range(7):
        kpad[0:7] = kernel[u]
        kpad[7:8] = jnp.zeros((1, CH), F32)
        kf[u] = dot_exact(fwd_k[...], kpad[...])
    g4[0:6] = jnp.zeros((6, 4 * NFREQ, CH), F32)
    g4[6 + SIDE :] = jnp.zeros((6, 4 * NFREQ, CH), F32)
    xpad[W : W + SIDE, 0:SIDE] = fields[...]
    columns = lax.broadcasted_iota(jnp.int32, (1024, 1024), 1)
    route = (columns == target_col[...]).astype(F32).astype(BF)
    finish(copies)
    pack(routed, dot(route, unpack(got)).astype(BF).reshape(4, TILES, CELLS, CH))
    copies = exchange("tile", TILES, lambda to: routed.at[:, to], lambda m: back.at[:, m], s2, r2)
    back[:, me] = routed[:, me]
    finish(copies)
    hal[...] = unpack(back).reshape(4, 256, CH)

    def put(n, *parts):
        return sum(dot(spread(by_row, name, n), hal[k]) for name, k in parts).astype(BF)

    xpad[0:W] = put(W * KROW, ("top0", 0), ("top3", 3)).reshape(W, KROW, CH)
    xpad[W + SIDE :] = put(W * KROW, ("bot2", 2), ("bot1", 1)).reshape(W, KROW, CH)
    xpad[W : W + SIDE, SIDE:] = put(SIDE * 16, ("side3", 3), ("side1", 1)).reshape(SIDE, 16, CH)

    def to_freq(r, _):
        x3[r] = dot(fwd_x[...], xpad[r])
        return 0

    lax.fori_loop(0, EXT, to_freq, 0, unroll=14)

    for l0, lw in LANES:
        for fb in range(5):
            rows = [slice(40 * t + 8 * fb, 40 * t + 8 * fb + 8) for t in range(3)]
            lanes = slice(l0, l0 + lw)
            kk = [[kf[u, rows[t], lanes] for t in range(3)] for u in range(7)]

            def conv(ib, _, fb=fb, rows=rows, lanes=lanes, kk=kk):
                i0 = ib * 4
                prods = []
                for t in range(3):
                    xs = [x3[i0 + r, rows[t], lanes] for r in range(10)]
                    prods.append([taps(xs[d : d + 7], [k[t] for k in kk]) for d in range(4)])
                for d in range(4):
                    y2[i0 + d, 16 * fb : 16 * fb + 16, lanes] = real_imag(*(p[d] for p in prods))
                return 0

            lax.fori_loop(0, SIDE // 4, conv, 0, unroll=2)

    load_cot.wait()
    egrad[...] = jnp.zeros_like(egrad)
    rgrad[...] = jnp.zeros_like(rgrad)
    step = 16
    n = step * SIDE

    def chunk(ic, _):
        i0 = pl.multiple_of(ic * step, step)
        conv_out = jnp.concatenate(
            [dot(inv_y[...], y2[i0 + d]) for d in range(step)], axis=0
        )
        conv_out = conv_out + conv_bias
        shifted = conv_out - jnp.mean(conv_out, axis=-1, keepdims=True)
        inv_std = lax.rsqrt(jnp.mean(shifted * shifted, axis=-1, keepdims=True) + 1e-06)
        centred = shifted * inv_std
        normed = (centred * gain + nbias).astype(BF)
        pre = dot(normed, w_exp[...]) + b_exp
        size = jnp.abs(pre)
        t = 1.0 / (1.0 + (0.3275911 * math.sqrt(0.5)) * size)
        dens = jnp.exp(-0.5 * pre * pre)
        poly = t * (
            0.127414796
            + t * (-0.142248368 + t * (0.7107068705 + t * (-0.7265760135 + t * 0.5307027145)))
        )
        tail = poly * dens
        phi = jnp.where(pre >= 0, 1.0 - tail, tail)
        act = (pre * phi).astype(BF)
        slope = phi + pre * (dens * 0.3989422804014327)
        cot_c = cot[pl.ds(i0, step)].reshape(n, CH).astype(F32)
        branch = dot_nt(act, w_red[...]) + b_red
        mix = fields[pl.ds(i0, step)].reshape(n, CH).astype(F32) + lscale * branch
        mix_out[pl.ds(i0, step)] = mix.astype(BF).reshape(step, SIDE, CH)
        bgrad = (lscale * cot_c).astype(BF)
        pre_grad = (dot(bgrad, w_red[...]) * slope).astype(BF)
        rgrad[...] += dot_tn(bgrad, act)
        egrad[...] += dot_tn(normed, pre_grad)
        ngrad = dot_nt(pre_grad, w_exp[...]) * gain
        m1 = jnp.mean(ngrad, axis=-1, keepdims=True)
        m2 = jnp.mean(ngrad * centred, axis=-1, keepdims=True)
        cgrad = (inv_std * (ngrad - m1 - centred * m2)).astype(BF)
        for d in range(step):
            g4[6 + i0 + d] = dot(fwd_g[...], cgrad[d * SIDE : (d + 1) * SIDE])
        return 0

    lax.fori_loop(0, SIDE // step, chunk, 0)

    store_mixed = pltpu.make_async_copy(mix_out, mixed, io_sem.at[1])
    store_mixed.start()

    for l0, lw in LANES:
        for fb in range(5):
            rows = [slice(40 * t + 8 * fb, 40 * t + 8 * fb + 8) for t in range(4)]
            grow = (rows[0], rows[1], rows[3])
            lanes = slice(l0, l0 + lw)

            def kgrad(ib, accs, rows=rows, lanes=lanes, grow=grow):
                i0 = ib * 4
                accs = list(accs)
                for t in range(3):
                    xs = [x3[i0 + r, rows[t], lanes] for r in range(10)]
                    for d in range(4):
                        g = g4[6 + i0 + d, grow[t], lanes]
                        for u in range(7):
                            accs[7 * t + u] = accs[7 * t + u] + xs[d + u] * g
                return tuple(accs)

            zero = jnp.zeros((8, lw), F32)
            accs = lax.fori_loop(0, SIDE // 4, kgrad, (zero,) * 21, unroll=2)
            for t in range(3):
                for u in range(7):
                    m3[u, rows[t], lanes] = accs[7 * t + u]


    for g in range(3):
        lanes = slice(128 * g, 128 * g + 128)
        wsrc[192 * g : 192 * g + 192] = egrad[:, lanes].astype(BF)
        wsrc[576 + 192 * g : 768 + 192 * g] = rgrad[:, lanes].astype(BF)
    kg = jnp.concatenate([dot_exact(inv_k[...], m3[u]) for u in range(7)], axis=0)
    kg = jnp.concatenate([kg, jnp.zeros((8, CH), F32)], axis=0).astype(BF)
    wsrc[1152:1216] = kg[:, 0:128]
    wsrc[1216:1280] = jnp.concatenate([kg[:, 128:192], jnp.zeros((64, 64), BF)], axis=1)

    def dp_block(to):
        return wsrc.at[pl.ds(pl.multiple_of(to * dp_rows, 16), dp_rows)]

    ca = exchange("dp", ndp, dp_block, lambda m: wa.at[m], sa, ra)
    wa[md] = wsrc[pl.ds(pl.multiple_of(md * dp_rows, 16), dp_rows)]

    for l0, lw in LANES:
        for fb in range(5):
            rows = [slice(40 * t + 8 * fb, 40 * t + 8 * fb + 8) for t in range(3)]
            lanes = slice(l0, l0 + lw)

            kk = [
                [kf[u, 120 + 40 * t + 8 * fb : 128 + 40 * t + 8 * fb, lanes] for t in range(3)]
                for u in range(7)
            ]

            def pconv(ib, _, fb=fb, rows=rows, lanes=lanes, kk=kk):
                p0 = ib * 5
                prods = []
                for t in range(3):
                    gs = [g4[p0 + r, rows[t], lanes] for r in range(11)]
                    back = [k[t] for k in kk][::-1]
                    prods.append([taps(gs[d : d + 7], back) for d in range(5)])
                for d in range(5):
                    y2[p0 + d, 16 * fb : 16 * fb + 16, lanes] = real_imag(*(p[d] for p in prods))
                return 0

            lax.fori_loop(0, EXT // 5, pconv, 0, unroll=2)


    finish(ca)
    part = wa[0].astype(F32)
    for j in range(1, ndp):
        part = part + wa[j].astype(F32)
    pa[...] = part.reshape(owners, WBLOCK, 128)

    def share(off, src, dst, send, recv):
        return pltpu.make_async_remote_copy(
            src_ref=src,
            dst_ref=dst,
            send_sem=send.at[off],
            recv_sem=recv.at[off],
            device_id={"tile": peer(me, off, TILES)},
            device_id_type=MESH,
        )

    def to_owner(off):
        to = peer(me, off, TILES)
        return to, share(off, pa.at[lax.rem(to, owners)], wb.at[me], sb, rb)

    for off in range(1, TILES):
        to, copy = to_owner(off)
        pl.when(to < owners)(copy.start)

    @pl.when(me < owners)
    def _():
        wb[me] = pa[lax.rem(me, owners)]

    for p in range(W):
        ptop[p] = dot(inv_p[...], y2[p]).astype(BF)
        pbot[p] = dot(inv_p[...], y2[W + SIDE + p]).astype(BF)

    def from_freq(i, _):
        back = dot(inv_p[...], y2[i + W])
        direct[i] = (cot[i].astype(F32) + back[0:SIDE]).astype(BF)
        psides[i] = back[SIDE:].astype(BF)
        return 0

    lax.fori_loop(0, SIDE, from_freq, 0, unroll=8)

    top = ptop[...].reshape(W * KROW, CH)
    bot = pbot[...].reshape(W * KROW, CH)
    sides = psides[...].reshape(SIDE * 16, CH)


    def take(*parts):
        total = sum(dot(gather(by_col, name, part.shape[0]), part) for name, part in parts)
        return total.astype(BF).reshape(1, TILES, CELLS, CH)

    taken = [
        take(("top0", top)),
        take(("side1", sides), ("bot1", bot)),
        take(("bot2", bot)),
        take(("side3", sides), ("top3", top)),
    ]
    pack(own2, jnp.concatenate(taken, axis=0))


    c3 = exchange("tile", TILES, lambda to: own2.at[:, to], lambda m: got2.at[:, m], s3, r3)
    got2[:, me] = own2[:, me]
    for off in range(1, TILES):
        to, copy = to_owner(off)
        pl.when(to < owners)(copy.wait_send)
        pl.when(me < owners)(copy.wait_recv)

    mine = lax.rem(me, owners)

    @pl.when(me < owners)
    def _():
        whole = wb[0]
        for j in range(1, TILES):
            whole = whole + wb[j]
        pc[...] = whole.astype(BF)
        wc[mine] = whole.astype(BF)
        for off in range(1, TILES):
            share(off, pc, wc.at[mine], sc, rc).start()

    rows = lax.broadcasted_iota(jnp.int32, (1024, 1024), 0)
    route_back = (rows == target_row[...]).astype(F32).astype(BF)
    for off in range(1, TILES):
        copy = share(off, pc, wc.at[mine], sc, rc)
        pl.when(me < owners)(copy.wait_send)
        pl.when(peer(me, TILES - off, TILES) < owners)(copy.wait_recv)

    block = wc[...].reshape(owners * WBLOCK, 128)
    pd = wa.at[0]
    pd[...] = block
    cd = exchange("dp", ndp, lambda to: pd, lambda m: wd.at[m], sd, rd)
    wd[md] = block
    finish(c3)
    pack(routed2, dot(route_back, unpack(got2)).astype(BF).reshape(4, TILES, CELLS, CH))
    c4 = exchange("tile", TILES, lambda to: routed2.at[:, to], lambda m: back2.at[:, m], s4, r4)
    back2[:, me] = routed2[:, me]
    finish(cd)
    wout[...] = wd[...].reshape(WROWS, 128)
    finish(c4)
    bands[...] = unpack(back2).reshape(4, 256, CH)
    store_mixed.wait()


def main(fields, cotangent, target, params, ndp):
    index = [jnp.asarray(t) for t in static_tables()]
    tables = [jnp.asarray(t) for t in dft_tables()]
    vm = pl.BlockSpec(memory_space=pltpu.VMEM)
    hbm = pl.BlockSpec(memory_space=pl.ANY)
    halo_buf = pltpu.VMEM(PACKED, BF)
    sem = pltpu.SemaphoreType.DMA((TILES,))
    sem_dp = pltpu.SemaphoreType.DMA((ndp,))
    dp_rows = WROWS // ndp
    owners = dp_rows // WBLOCK
    targets = [target.reshape(1024, 1), target.reshape(1, 1024)]
    args = [fields, cotangent, *index, *targets, *tables, *params]
    field = jax.ShapeDtypeStruct((SIDE, SIDE, CH), BF)
    return pl.pallas_call(
        main_kernel,
        out_shape=(
            field,
            field,
            jax.ShapeDtypeStruct((4, 256, CH), BF),
            jax.ShapeDtypeStruct((WROWS, 128), BF),
        ),
        in_specs=[vm, hbm] + [vm] * (len(args) - 2),
        out_specs=(hbm, vm, vm, vm),
        scratch_shapes=[
            pltpu.VMEM((EXT, KROW, CH), BF),
            pltpu.VMEM((EXT, 3 * NFREQ, CH), F32),
            pltpu.VMEM((EXT, 2 * NFREQ, CH), BF),
            pltpu.VMEM((SIDE + 12, 4 * NFREQ, CH), F32),
            pltpu.VMEM((8, CH), F32),
            pltpu.VMEM((7, 6 * NFREQ, CH), F32),
            pltpu.VMEM((7, 3 * NFREQ, CH), F32),
            pltpu.VMEM((CH, HID), F32),
            pltpu.VMEM((CH, HID), F32),
            pltpu.VMEM((SIDE, 16, CH), BF),
            pltpu.VMEM((W, KROW, CH), BF),
            pltpu.VMEM((W, KROW, CH), BF),
            pltpu.VMEM((SIDE, SIDE, CH), BF),
            pltpu.VMEM((SIDE, SIDE, CH), BF),
            pltpu.VMEM((4, 256, CH), BF),
        ]
        + [halo_buf] * 8
        + [
            pltpu.VMEM((WROWS, 128), BF),
            pltpu.VMEM((ndp, dp_rows, 128), BF),
            pltpu.VMEM((owners, WBLOCK, 128), F32),
            pltpu.VMEM((TILES, WBLOCK, 128), F32),
            pltpu.VMEM((WBLOCK, 128), BF),
            pltpu.VMEM((owners, WBLOCK, 128), BF),
            pltpu.VMEM((ndp, dp_rows, 128), BF),
            pltpu.SemaphoreType.DMA((2,)),
        ]
        + [sem] * 12
        + [sem_dp] * 4,
        compiler_params=pltpu.CompilerParams(
            collective_id=0, has_side_effects=True, vmem_limit_bytes=62 * 2**20
        ),
        name="main",
    )(*args)


def last_kernel(scale, direct, bands, wsum, by_row, out, kgrad, egrad, rgrad):
    north = dot(spread(by_row, "north", W * SIDE), bands[0]).reshape(W, SIDE, CH)
    south = dot(spread(by_row, "south", W * SIDE), bands[2]).reshape(W, SIDE, CH)
    east = dot(spread(by_row, "east", 1024), bands[1]).reshape(SIDE, 16, CH)
    west = dot(spread(by_row, "west", 1024), bands[3]).reshape(SIDE, 16, CH)
    mid = slice(W, SIDE - W)
    out[mid, 16:48] = direct[mid, 16:48]
    out[mid, 0:16] = (direct[mid, 0:16].astype(F32) + west[mid]).astype(BF)
    out[mid, 48:64] = (direct[mid, 48:64].astype(F32) + east[mid]).astype(BF)
    zero = jnp.zeros((W, 32, CH), F32)
    for rows, add in ((slice(0, W), north), (slice(SIDE - W, SIDE), south)):
        more = jnp.concatenate([west[rows], zero, east[rows]], axis=1)
        out[rows] = (direct[rows].astype(F32) + add + more).astype(BF)
    for g in range(3):
        lanes = slice(128 * g, 128 * g + 128)
        egrad[:, lanes] = wsum[192 * g : 192 * g + 192].astype(F32) * scale
        rgrad[:, lanes] = wsum[576 + 192 * g : 768 + 192 * g].astype(F32) * scale
    low = wsum[1152:1216].astype(F32) * scale
    high = wsum[1216:1280].astype(F32) * scale
    for u in range(7):
        kgrad[u, :, 0:128] = low[8 * u : 8 * u + 7]
        kgrad[u, :, 128:192] = high[8 * u : 8 * u + 7, 0:64]


def last(direct, bands, wsum, scale):
    by_row, _ = static_tables()
    vm = pl.BlockSpec(memory_space=pltpu.VMEM)
    return pl.pallas_call(
        functools.partial(last_kernel, scale),
        out_shape=(
            jax.ShapeDtypeStruct((SIDE, SIDE, CH), BF),
            jax.ShapeDtypeStruct((7, 7, CH), F32),
            jax.ShapeDtypeStruct((CH, HID), F32),
            jax.ShapeDtypeStruct((CH, HID), F32),
        ),
        in_specs=[vm] * 4,
        out_specs=(vm,) * 4,
        compiler_params=pltpu.CompilerParams(vmem_limit_bytes=24 * 2**20),
        name="last",
    )(direct, bands, wsum, jnp.asarray(by_row))


def routing(neighbors, rotations):
    me = lax.axis_index("tile")
    offsets = jnp.array(OFFSETS, jnp.int32)[None, :]
    side = (rotations + offsets) % 4
    base = jnp.where(neighbors >= 0, side * 256 + neighbors * CELLS, -(1 << 20)).T
    right = jnp.where(me >= 7, 11, -(1 << 20))
    left = jnp.where(me <= 8, 0, -(1 << 20))
    corner_row = jnp.stack([right, left, right, left])[:, None]
    cell = jnp.arange(CELLS, dtype=jnp.int32)[None, None, :]
    edge = base[0:4][:, :, None] + cell
    corner = (base[4:8] + corner_row)[:, :, None]
    return jnp.where(cell < 12, edge, jnp.where(cell == 12, corner, -1)).astype(jnp.int32)


def on_device(
    fields,
    cotangent,
    kernel,
    conv_bias,
    norm_gain,
    norm_bias,
    w_expand,
    bias_expand,
    w_reduce,
    bias_reduce,
    layer_scale,
    neighbors,
    rotations,
):
    ndp = lax.axis_size("dp")
    field = fields.reshape(SIDE, SIDE, CH)
    cot = cotangent.reshape(SIDE, SIDE, CH)
    target = routing(neighbors, rotations)
    params = [
        kernel,
        conv_bias,
        norm_gain,
        norm_bias,
        w_expand,
        bias_expand,
        w_reduce.T,
        bias_reduce,
        layer_scale,
    ]
    mixed, direct, bands, wsum = main(field, cot, target, params, ndp)
    scale = 1.0 / math.sqrt(ndp * TILES * SIDE * SIDE)
    input_grad, kgrad, egrad, rgrad = last(direct, bands, wsum, scale)
    return (
        mixed.reshape(fields.shape),
        input_grad.reshape(fields.shape),
        kgrad,
        egrad,
        rgrad.T,
    )


def solution(mesh):
    split = P("dp", "tile", None, None, None)
    return jax.shard_map(
        on_device,
        mesh=mesh,
        in_specs=(split, split) + (P(),) * 11,
        out_specs=(split, split, P(), P(), P()),
        check_vma=False,
    )
```

```python
import functools
import math

import jax
import jax.numpy as jnp
import numpy as np
from jax import lax
from jax.experimental import pallas as pl
from jax.experimental.pallas import tpu as pltpu
from jax.sharding import PartitionSpec as P

OFFSETS = (2, 3, 0, 1, 2, 0, 0, 2)
SIDE = 64
W = 3
CH = 192
HID = 384
TILES = 16
CELLS = 16
NFREQ = 40
KROW = 80
EXT = SIDE + 2 * W
BF = jnp.bfloat16
F32 = jnp.float32
MESH = pl.DeviceIdType.MESH
WROWS = 1152
KROWS = 128
WBLOCK = 16
INDEX = ("top0", "top3", "bot2", "bot1", "side3", "side1", "north", "east", "south", "west")


def stripe_table():
    where = np.zeros((W, SIDE, 2), np.int64)
    used = {i: set() for i in range(16)}
    rest = []
    for w in range(W):
        for l in range(SIDE):
            if l < W:
                spot = (w * W + l, 0)
            elif l >= SIDE - W:
                spot = (7 + w * W + l - (SIDE - W), 11)
            else:
                rest.append((w, l))
                continue
            where[w, l] = spot
            used[spot[0]].add(spot[1])
    free = [(i, a) for i in range(16) for a in range(12) if a not in used[i]]
    for (w, l), spot in zip(rest, free):
        where[w, l] = spot
    return where


def np_pad(field, picked):
    north = np.rot90(picked[0], 2)
    east = np.rot90(picked[1], 1)
    south = picked[2]
    west = np.rot90(picked[3], 3)
    ne = np.rot90(picked[4], 2)[:, :W]
    se = picked[5][:, :W]
    sw = picked[6][:, SIDE - W :]
    nw = np.rot90(picked[7], 2)[:, SIDE - W :]
    return np.concatenate(
        [
            np.concatenate([nw, north, ne], 1),
            np.concatenate([west, field, east], 1),
            np.concatenate([sw, south, se], 1),
        ],
        0,
    )


def column_of(m):
    if m < SIDE:
        return m + W
    if m < SIDE + W:
        return m - SIDE
    if m < SIDE + 2 * W:
        return m
    return -1


@functools.lru_cache(None)
def static_tables():
    where = stripe_table()
    codes = np.arange(8 * W * SIDE).reshape(8, W, SIDE)
    padded = np_pad(np.full((SIDE, SIDE), -1), codes)

    def spot(code):
        k, w, l = np.unravel_index(code, (8, W, SIDE))
        i, a = where[w, l]
        return (k, i * CELLS + a) if k < 4 else (k - 4, i * CELLS + 12)

    index = {name: np.full(256, -1, np.int64) for name in INDEX}

    def places(p_list, m_list, names):
        for ip, p in enumerate(p_list):
            for im, m in enumerate(m_list):
                q = column_of(m)
                if q < 0 or padded[p, q] < 0:
                    continue
                k, row = spot(padded[p, q])
                index[names[k]][row] = ip * len(m_list) + im

    places([0, 1, 2], range(KROW), {0: "top0", 3: "top3"})
    places([67, 68, 69], range(KROW), {2: "bot2", 1: "bot1"})
    places(range(W, W + SIDE), range(SIDE, KROW), {3: "side3", 1: "side1"})

    cells = np.arange(SIDE * SIDE).reshape(SIDE, SIDE)
    bands = {
        "north": (cells[:W], SIDE, 0, 0),
        "east": (np.rot90(cells[:, SIDE - W :], 1), 16, 0, 48),
        "south": (np.rot90(cells[SIDE - W :], 2), SIDE, SIDE - W, 0),
        "west": (np.rot90(cells[:, :W], 3), 16, 0, 0),
    }
    for name, (band, pitch, row0, col0) in bands.items():
        for w in range(W):
            for l in range(SIDE):
                i, j = divmod(int(band[w, l]), SIDE)
                st, a = where[w, l]
                index[name][st * CELLS + a] = (i - row0) * pitch + j - col0
    table = np.stack([index[name] for name in INDEX]).astype(np.int32)
    by_row = np.full((16, 256), -1, np.int32)
    by_row[: len(INDEX)] = table
    by_col = np.full((256, 128), -1, np.int32)
    by_col[:, : len(INDEX)] = table.T
    return by_row, by_col


def spread(by_row, name, n):
    k = INDEX.index(name)
    place = lax.broadcasted_iota(jnp.int32, (n, 256), 0)
    return (place == by_row[k : k + 1]).astype(F32).astype(BF)


def gather(by_col, name, n):
    k = INDEX.index(name)
    place = lax.broadcasted_iota(jnp.int32, (256, n), 1)
    return (place == by_col[:, k : k + 1]).astype(F32).astype(BF)


@functools.lru_cache(None)
def dft_tables():
    n = 2 * NFREQ
    theta = 2 * np.pi * (np.arange(NFREQ) + 0.5) / n

    def cs(pos):
        ang = theta[:, None] * np.asarray(pos, np.float64)[None, :]
        live = (np.asarray(pos) >= 0)[None, :]
        return np.cos(ang) * live, np.sin(ang) * live

    def inverse(c, s):
        both = np.stack([c.reshape(5, 8, -1), -s.reshape(5, 8, -1)], 1)
        return (2 / n) * both.reshape(2 * NFREQ, -1).T

    cols = [column_of(m) for m in range(KROW)]
    c, s = cs(cols)
    fwd_x = np.concatenate([c, -s, c - s], 0)
    inv_p = inverse(c, s)
    c, s = cs(np.arange(SIDE))
    inv_y = inverse(c, s)
    fwd_g = np.concatenate([c, -s, c - s, c + s], 0)
    taps = [0, 1, 2, 3, 4, 5, 6, -1]
    c, s = cs(taps)
    fwd_k = np.concatenate([c, s, c + s, c, -s, c - s], 0)
    inv_k = (2 / n) * np.concatenate([c + s, c - s, -s], 0).T
    return (
        fwd_x.astype(jnp.bfloat16),
        inv_y.astype(jnp.bfloat16),
        fwd_g.astype(jnp.bfloat16),
        inv_p.astype(jnp.bfloat16),
        fwd_k.astype(np.float32),
        inv_k.astype(np.float32),
    )


def dot(a, b):
    return jnp.dot(a, b, preferred_element_type=F32)


def dot_nt(a, b):
    return lax.dot_general(a, b, (((1,), (1,)), ((), ())), preferred_element_type=F32)


def dot_tn(a, b):
    return lax.dot_general(a, b, (((0,), (0,)), ((), ())), preferred_element_type=F32)


def dot_exact(a, b):
    return jnp.dot(a, b, preferred_element_type=F32, precision=lax.Precision.HIGHEST)


def peer(me, off, n):
    return lax.rem(me + off, n)


def greet(axes):
    barrier = pltpu.get_barrier_semaphore()
    total = 0
    for axis, n in axes:
        me = lax.axis_index(axis)
        for off in range(1, n):
            pl.semaphore_signal(
                barrier, inc=1, device_id={axis: peer(me, off, n)}, device_id_type=MESH
            )
            total += 1
    return barrier, total


def exchange(axis, n, src_of, dst, send, recv):
    me = lax.axis_index(axis)
    copies = []
    for off in range(1, n):
        to = peer(me, off, n)
        copy = pltpu.make_async_remote_copy(
            src_ref=src_of(to),
            dst_ref=dst(me),
            send_sem=send.at[off],
            recv_sem=recv.at[off],
            device_id={axis: to},
            device_id_type=MESH,
        )
        copy.start()
        copies.append(copy)
    return copies


def finish(copies):
    for copy in copies:
        copy.wait()


PACKED = (6, TILES, CELLS, 128)


def pack(ref, value):
    ref[0:4] = value[..., 0:128]
    ref[4:6] = jnp.concatenate([value[0:2, :, :, 128:CH], value[2:4, :, :, 128:CH]], axis=-1)


def unpack(ref):
    low = ref[0:4].reshape(1024, 128)
    pair = ref[4:6].reshape(512, 128)
    high = jnp.concatenate([pair[:, 0:64], pair[:, 64:128]], axis=0)
    return jnp.concatenate([low, high], axis=-1)


LANES = ((0, 128), (128, 64))


def taps(xs, ks):
    acc = xs[0] * ks[0]
    for x, k in zip(xs[1:], ks[1:]):
        acc = acc + x * k
    return acc


def real_imag(a, b, c):
    return jnp.concatenate([a - b, c - a - b], axis=0).astype(BF)


def route_targets(base, me, axis):
    shape = (1024, 16) if axis == 0 else (16, 1024)
    row = lax.broadcasted_iota(jnp.int32, shape, axis)
    tile = lax.broadcasted_iota(jnp.int32, shape, 1 - axis)
    pick = (((row >> 4) & 15) == tile).astype(F32).astype(BF)
    found = dot_nt(pick, base) if axis == 0 else dot(base, pick)
    slot = lax.broadcasted_iota(jnp.int32, found.shape, 1 - axis)
    row = lax.broadcasted_iota(jnp.int32, found.shape, axis)
    edge = jnp.sum(jnp.where(slot == row >> 8, found, 0.0), axis=1 - axis, keepdims=True)
    corner = jnp.sum(jnp.where(slot == (row >> 8) + 4, found, 0.0), axis=1 - axis, keepdims=True)
    row = lax.broadcasted_iota(jnp.int32, edge.shape, axis)
    cell = row & 15
    right = jnp.where(me >= 7, 11.0, -8192.0)
    left = jnp.where(me <= 8, 0.0, -8192.0)
    corner = corner + jnp.where((row >> 8) & 1 == 0, right, left)
    return jnp.where(cell < 12, edge + cell.astype(F32), jnp.where(cell == 12, corner, -1.0))


def route_matrix(base, me, axis):
    place = lax.broadcasted_iota(jnp.int32, (1024, 1024), 1 - axis).astype(F32)
    return (place == route_targets(base, me, axis)).astype(F32).astype(BF)


def main_kernel(
    fields,
    cot_hbm,
    by_row,
    by_col,
    neighbors,
    rotations,
    offsets,
    fwd_x,
    inv_y,
    fwd_g,
    inv_p,
    fwd_k,
    inv_k,
    kernel,
    conv_bias,
    gain,
    nbias,
    w_exp,
    b_exp,
    w_red,
    b_red,
    lscale,
    mixed,
    direct,
    bands,
    wout,
    xpad,
    x3,
    y2,
    g4,
    kpad,
    kf,
    m3,
    egrad,
    rgrad,
    psides,
    ptop,
    pbot,
    cot,
    mix_out,
    hal,
    own,
    got,
    routed,
    back,
    own2,
    got2,
    routed2,
    back2,
    wsrc,
    wa,
    pa,
    wb,
    pc,
    wc,
    wd,
    ksrc,
    kwa,
    kpart,
    kwb,
    kwhole,
    kwc,
    dir_out,
    io_sem,
    *sems,
):
    s1, r1, s2, r2, s3, r3, s4, r4, sb, rb, sc, rc, skb, rkb = sems[:14]
    sa, ra, sd, rd, ska, rka, skc, rkc = sems[14:]
    me = lax.axis_index("tile")
    md = lax.axis_index("dp")
    ndp = wa.shape[0]
    dp_rows = wa.shape[1]
    krows = kpart.shape[0]
    owners = pa.shape[0]
    base = jnp.where(
        neighbors[...] >= 0,
        ((rotations[...] + offsets[...]) & 3) * 256 + neighbors[...] * CELLS,
        -4096,
    )
    base = base.astype(F32).astype(BF)
    barrier, total = greet((("tile", TILES), ("dp", ndp)))
    load_cot = pltpu.make_async_copy(cot_hbm, cot, io_sem.at[0])
    load_cot.start()
    bands_own = jnp.concatenate(
        [
            dot(gather(by_col, "north", W * SIDE), fields[0:W].reshape(W * SIDE, CH)),
            dot(gather(by_col, "east", 1024), fields[:, 48:64].reshape(1024, CH)),
            dot(gather(by_col, "south", W * SIDE), fields[SIDE - W :].reshape(W * SIDE, CH)),
            dot(gather(by_col, "west", 1024), fields[:, 0:16].reshape(1024, CH)),
        ],
        axis=0,
    )
    pack(own, bands_own.astype(BF).reshape(4, TILES, CELLS, CH))
    pl.semaphore_wait(barrier, total)
    copies = exchange("tile", TILES, lambda to: own.at[:, to], lambda m: got.at[:, m], s1, r1)
    got[:, me] = own[:, me]
    conv_bias, gain, nbias, b_exp, b_red, lscale = (
        ref[...].reshape(1, -1) for ref in (conv_bias, gain, nbias, b_exp, b_red, lscale)
    )
    for u in range(7):
        kpad[0:7] = kernel[u]
        kpad[7:8] = jnp.zeros((1, CH), F32)
        kf[u] = dot_exact(fwd_k[...], kpad[...])
    g4[0:6] = jnp.zeros((6, 4 * NFREQ, CH), F32)
    g4[6 + SIDE :] = jnp.zeros((6, 4 * NFREQ, CH), F32)
    xpad[W : W + SIDE, 0:SIDE] = fields[...]
    route = route_matrix(base, me, 0)
    finish(copies)
    pack(routed, dot(route, unpack(got)).astype(BF).reshape(4, TILES, CELLS, CH))
    copies = exchange("tile", TILES, lambda to: routed.at[:, to], lambda m: back.at[:, m], s2, r2)
    back[:, me] = routed[:, me]
    finish(copies)
    hal[...] = unpack(back).reshape(4, 256, CH)

    def put(n, *parts):
        return sum(dot(spread(by_row, name, n), hal[k]) for name, k in parts).astype(BF)

    xpad[0:W] = put(W * KROW, ("top0", 0), ("top3", 3)).reshape(W, KROW, CH)
    xpad[W + SIDE :] = put(W * KROW, ("bot2", 2), ("bot1", 1)).reshape(W, KROW, CH)
    xpad[W : W + SIDE, SIDE:] = put(SIDE * 16, ("side3", 3), ("side1", 1)).reshape(SIDE, 16, CH)

    def to_freq(r, _):
        x3[r] = dot(fwd_x[...], xpad[r])
        return 0

    lax.fori_loop(0, EXT, to_freq, 0, unroll=14)

    for l0, lw in LANES:
        for fb in range(5):
            rows = [slice(40 * t + 8 * fb, 40 * t + 8 * fb + 8) for t in range(3)]
            lanes = slice(l0, l0 + lw)
            kk = [[kf[u, rows[t], lanes] for t in range(3)] for u in range(7)]

            def conv(ib, _, fb=fb, rows=rows, lanes=lanes, kk=kk):
                i0 = ib * 4
                prods = []
                for t in range(3):
                    xs = [x3[i0 + r, rows[t], lanes] for r in range(10)]
                    prods.append([taps(xs[d : d + 7], [k[t] for k in kk]) for d in range(4)])
                for d in range(4):
                    y2[i0 + d, 16 * fb : 16 * fb + 16, lanes] = real_imag(*(p[d] for p in prods))
                return 0

            lax.fori_loop(0, SIDE // 4, conv, 0, unroll=2)

    load_cot.wait()
    egrad[...] = jnp.zeros_like(egrad)
    rgrad[...] = jnp.zeros_like(rgrad)
    step = 4
    parts = 8
    n = step * SIDE

    def part(i0):
        conv_out = jnp.concatenate([dot(inv_y[...], y2[i0 + d]) for d in range(step)], axis=0)
        yield
        conv_out = conv_out + conv_bias
        shifted = conv_out - jnp.mean(conv_out, axis=-1, keepdims=True)
        inv_std = lax.rsqrt(jnp.mean(shifted * shifted, axis=-1, keepdims=True) + 1e-06)
        centred = shifted * inv_std
        normed = (centred * gain + nbias).astype(BF)
        yield
        pre = dot(normed, w_exp[...]) + b_exp
        bgrad = (lscale * cot[pl.ds(i0, step)].reshape(n, CH).astype(F32)).astype(BF)
        act_grad = dot(bgrad, w_red[...])
        yield
        size = jnp.abs(pre)
        t = 1.0 / (1.0 + (0.3275911 * math.sqrt(0.5)) * size)
        dens = jnp.exp(-0.5 * pre * pre)
        poly = t * (
            0.127414796
            + t * (-0.142248368 + t * (0.7107068705 + t * (-0.7265760135 + t * 0.5307027145)))
        )
        tail = poly * dens
        phi = jnp.where(pre >= 0, 1.0 - tail, tail)
        act = (pre * phi).astype(BF)
        pre_grad = (act_grad * (phi + pre * (dens * 0.3989422804014327))).astype(BF)
        yield
        ngrad = dot_nt(pre_grad, w_exp[...])
        branch = dot_nt(act, w_red[...])
        rgrad[...] += dot_tn(bgrad, act)
        egrad[...] += dot_tn(normed, pre_grad)
        yield
        mix = fields[pl.ds(i0, step)].reshape(n, CH).astype(F32) + lscale * (branch + b_red)
        mix_out[pl.ds(i0, step)] = mix.astype(BF).reshape(step, SIDE, CH)
        ngrad = ngrad * gain
        m1 = jnp.mean(ngrad, axis=-1, keepdims=True)
        m2 = jnp.mean(ngrad * centred, axis=-1, keepdims=True)
        cgrad = (inv_std * (ngrad - m1 - centred * m2)).astype(BF)
        yield
        for d in range(step):
            g4[6 + i0 + d] = dot(fwd_g[...], cgrad[d * SIDE : (d + 1) * SIDE])
        yield

    def chunk(ic, _):
        gens = [part(pl.multiple_of((ic * parts + k) * step, step)) for k in range(parts)]
        for tick in range(7 + 1 * (parts - 1)):
            for k in range(parts):
                if 0 <= tick - 1 * k < 7:
                    next(gens[k])
        return 0

    lax.fori_loop(0, SIDE // (step * parts), chunk, 0)

    store_mixed = pltpu.make_async_copy(mix_out, mixed, io_sem.at[1])
    store_mixed.start()

    for g in range(3):
        lanes = slice(128 * g, 128 * g + 128)
        wsrc[192 * g : 192 * g + 192] = egrad[:, lanes].astype(BF)
        wsrc[576 + 192 * g : 768 + 192 * g] = rgrad[:, lanes].astype(BF)

    def dp_block(to):
        return wsrc.at[pl.ds(pl.multiple_of(to * dp_rows, 16), dp_rows)]

    ca = exchange("dp", ndp, dp_block, lambda m: wa.at[m], sa, ra)
    wa[md] = wsrc[pl.ds(pl.multiple_of(md * dp_rows, 16), dp_rows)]

    for l0, lw in LANES:
        for fb in range(5):
            rows = [slice(40 * t + 8 * fb, 40 * t + 8 * fb + 8) for t in range(3)]
            lanes = slice(l0, l0 + lw)

            kk = [
                [kf[u, 120 + 40 * t + 8 * fb : 128 + 40 * t + 8 * fb, lanes] for t in range(3)]
                for u in range(7)
            ]

            def pconv(ib, _, fb=fb, rows=rows, lanes=lanes, kk=kk):
                p0 = ib * 5
                prods = []
                for t in range(3):
                    gs = [g4[p0 + r, rows[t], lanes] for r in range(11)]
                    back = [k[t] for k in kk][::-1]
                    prods.append([taps(gs[d : d + 7], back) for d in range(5)])
                for d in range(5):
                    y2[p0 + d, 16 * fb : 16 * fb + 16, lanes] = real_imag(*(p[d] for p in prods))
                return 0

            lax.fori_loop(0, EXT // 5, pconv, 0, unroll=2)


    finish(ca)
    part = wa[0].astype(F32)
    for j in range(1, ndp):
        part = part + wa[j].astype(F32)
    pa[...] = part.reshape(owners, WBLOCK, 128)

    def share(off, src, dst, send, recv):
        return pltpu.make_async_remote_copy(
            src_ref=src,
            dst_ref=dst,
            send_sem=send.at[off],
            recv_sem=recv.at[off],
            device_id={"tile": peer(me, off, TILES)},
            device_id_type=MESH,
        )

    def to_owner(off):
        to = peer(me, off, TILES)
        return to, share(off, pa.at[lax.rem(to, owners)], wb.at[me], sb, rb)

    for off in range(1, TILES):
        to, copy = to_owner(off)
        pl.when(to < owners)(copy.start)

    @pl.when(me < owners)
    def _():
        wb[me] = pa[lax.rem(me, owners)]

    for p in range(W):
        ptop[p] = dot(inv_p[...], y2[p]).astype(BF)
        pbot[p] = dot(inv_p[...], y2[W + SIDE + p]).astype(BF)

    def from_freq(i, _):
        back = dot(inv_p[...], y2[i + W])
        dir_out[i] = (cot[i].astype(F32) + back[0:SIDE]).astype(BF)
        psides[i] = back[SIDE:].astype(BF)
        return 0

    lax.fori_loop(0, SIDE, from_freq, 0, unroll=8)
    store_direct = pltpu.make_async_copy(dir_out, direct, io_sem.at[2])
    store_direct.start()

    top = ptop[...].reshape(W * KROW, CH)
    bot = pbot[...].reshape(W * KROW, CH)
    sides = psides[...].reshape(SIDE * 16, CH)


    def take(*parts):
        total = sum(dot(gather(by_col, name, part.shape[0]), part) for name, part in parts)
        return total.astype(BF).reshape(1, TILES, CELLS, CH)

    taken = [
        take(("top0", top)),
        take(("side1", sides), ("bot1", bot)),
        take(("bot2", bot)),
        take(("side3", sides), ("top3", top)),
    ]
    pack(own2, jnp.concatenate(taken, axis=0))


    c3 = exchange("tile", TILES, lambda to: own2.at[:, to], lambda m: got2.at[:, m], s3, r3)
    got2[:, me] = own2[:, me]
    for off in range(1, TILES):
        to, copy = to_owner(off)
        pl.when(to < owners)(copy.wait_send)
        pl.when(me < owners)(copy.wait_recv)

    mine = lax.rem(me, owners)

    @pl.when(me < owners)
    def _():
        whole = wb[0]
        for j in range(1, TILES):
            whole = whole + wb[j]
        pc[...] = whole.astype(BF)
        wc[mine] = whole.astype(BF)
        for off in range(1, TILES):
            share(off, pc, wc.at[mine], sc, rc).start()

    for l0, lw in LANES:
        for fb in range(5):
            rows = [slice(40 * t + 8 * fb, 40 * t + 8 * fb + 8) for t in range(4)]
            grow = (rows[0], rows[1], rows[3])
            lanes = slice(l0, l0 + lw)

            def kgrad(ib, accs, rows=rows, lanes=lanes, grow=grow):
                i0 = ib * 4
                accs = list(accs)
                for t in range(3):
                    xs = [x3[i0 + r, rows[t], lanes] for r in range(10)]
                    for d in range(4):
                        g = g4[6 + i0 + d, grow[t], lanes]
                        for u in range(7):
                            accs[7 * t + u] = accs[7 * t + u] + xs[d + u] * g
                return tuple(accs)

            zero = jnp.zeros((8, lw), F32)
            accs = lax.fori_loop(0, SIDE // 4, kgrad, (zero,) * 21, unroll=2)
            for t in range(3):
                for u in range(7):
                    m3[u, rows[t], lanes] = accs[7 * t + u]


    kg = jnp.concatenate([dot_exact(inv_k[...], m3[u]) for u in range(7)], axis=0)
    kg = jnp.concatenate([kg, jnp.zeros((8, CH), F32)], axis=0)
    ksrc[0:64] = kg[:, 0:128]
    ksrc[64:128] = jnp.concatenate([kg[:, 128:192], jnp.zeros((64, 64), F32)], axis=1)

    def kernel_block(to):
        return ksrc.at[pl.ds(pl.multiple_of(to * krows, 16), krows)]

    ka = exchange("dp", ndp, kernel_block, lambda m: kwa.at[m], ska, rka)
    kwa[md] = ksrc[pl.ds(pl.multiple_of(md * krows, 16), krows)]

    for off in range(1, TILES):
        copy = share(off, pc, wc.at[mine], sc, rc)
        pl.when(me < owners)(copy.wait_send)
        pl.when(peer(me, TILES - off, TILES) < owners)(copy.wait_recv)

    block = wc[...].reshape(owners * WBLOCK, 128)
    pd = wa.at[0]
    pd[...] = block
    cd = exchange("dp", ndp, lambda to: pd, lambda m: wd.at[m], sd, rd)
    wd[md] = block
    route_back = route_matrix(base, me, 1)
    finish(c3)
    pack(routed2, dot(route_back, unpack(got2)).astype(BF).reshape(4, TILES, CELLS, CH))
    c4 = exchange("tile", TILES, lambda to: routed2.at[:, to], lambda m: back2.at[:, m], s4, r4)
    back2[:, me] = routed2[:, me]

    finish(ka)
    part = kwa[0]
    for j in range(1, ndp):
        part = part + kwa[j]
    kpart[...] = part.astype(BF)
    kb = exchange("tile", TILES, lambda to: kpart, lambda m: kwb.at[m], skb, rkb)
    kwb[me] = kpart[...]
    finish(kb)
    part = kwb[0].astype(F32)
    for j in range(1, TILES):
        part = part + kwb[j].astype(F32)
    kwhole[...] = part.astype(BF)
    kc = exchange("dp", ndp, lambda to: kwhole, lambda m: kwc.at[m], skc, rkc)
    kwc[md] = kwhole[...]
    finish(cd)
    wout[0:WROWS] = wd[...].reshape(WROWS, 128)
    finish(c4)
    bands[...] = unpack(back2).reshape(4, 256, CH)
    finish(kc)
    wout[WROWS:] = kwc[...].reshape(KROWS, 128)
    store_direct.wait()
    store_mixed.wait()


def main(fields, cotangent, neighbors, rotations, params, ndp):
    index = [jnp.asarray(t) for t in static_tables()]
    tables = [jnp.asarray(t) for t in dft_tables()]
    vm = pl.BlockSpec(memory_space=pltpu.VMEM)
    hbm = pl.BlockSpec(memory_space=pl.ANY)
    halo_buf = pltpu.VMEM(PACKED, BF)
    sem = pltpu.SemaphoreType.DMA((TILES,))
    sem_dp = pltpu.SemaphoreType.DMA((ndp,))
    dp_rows = WROWS // ndp
    krows = KROWS // ndp
    owners = dp_rows // WBLOCK
    offsets = jnp.asarray(OFFSETS, jnp.int32).reshape(8, 1)
    args = [fields, cotangent, *index, neighbors.T, rotations.T, offsets, *tables, *params]
    field = jax.ShapeDtypeStruct((SIDE, SIDE, CH), BF)
    return pl.pallas_call(
        main_kernel,
        out_shape=(
            field,
            field,
            jax.ShapeDtypeStruct((4, 256, CH), BF),
            jax.ShapeDtypeStruct((WROWS + KROWS, 128), BF),
        ),
        in_specs=[vm, hbm] + [vm] * (len(args) - 2),
        out_specs=(hbm, hbm, vm, vm),
        scratch_shapes=[
            pltpu.VMEM((EXT, KROW, CH), BF),
            pltpu.VMEM((EXT, 3 * NFREQ, CH), F32),
            pltpu.VMEM((EXT, 2 * NFREQ, CH), BF),
            pltpu.VMEM((SIDE + 12, 4 * NFREQ, CH), F32),
            pltpu.VMEM((8, CH), F32),
            pltpu.VMEM((7, 6 * NFREQ, CH), F32),
            pltpu.VMEM((7, 3 * NFREQ, CH), F32),
            pltpu.VMEM((CH, HID), F32),
            pltpu.VMEM((CH, HID), F32),
            pltpu.VMEM((SIDE, 16, CH), BF),
            pltpu.VMEM((W, KROW, CH), BF),
            pltpu.VMEM((W, KROW, CH), BF),
            pltpu.VMEM((SIDE, SIDE, CH), BF),
            pltpu.VMEM((SIDE, SIDE, CH), BF),
            pltpu.VMEM((4, 256, CH), BF),
        ]
        + [halo_buf] * 8
        + [
            pltpu.VMEM((WROWS, 128), BF),
            pltpu.VMEM((ndp, dp_rows, 128), BF),
            pltpu.VMEM((owners, WBLOCK, 128), F32),
            pltpu.VMEM((TILES, WBLOCK, 128), F32),
            pltpu.VMEM((WBLOCK, 128), BF),
            pltpu.VMEM((owners, WBLOCK, 128), BF),
            pltpu.VMEM((ndp, dp_rows, 128), BF),
            pltpu.VMEM((KROWS, 128), F32),
            pltpu.VMEM((ndp, krows, 128), F32),
            pltpu.VMEM((krows, 128), BF),
            pltpu.VMEM((TILES, krows, 128), BF),
            pltpu.VMEM((krows, 128), BF),
            pltpu.VMEM((ndp, krows, 128), BF),
            pltpu.VMEM((SIDE, SIDE, CH), BF),
            pltpu.SemaphoreType.DMA((3,)),
        ]
        + [sem] * 14
        + [sem_dp] * 8,
        compiler_params=pltpu.CompilerParams(
            collective_id=0, has_side_effects=True, vmem_limit_bytes=62 * 2**20
        ),
        name="main",
    )(*args)


def last_kernel(
    scale, mixed, direct, bands, wsum, by_row, mixed_out, out, kgrad, egrad, rgrad, d, b, w, m, sem
):
    load_m = pltpu.make_async_copy(mixed, m, sem.at[0])
    store_m = pltpu.make_async_copy(m, mixed_out, sem.at[5])
    load_b = pltpu.make_async_copy(bands, b, sem.at[1])
    load_w = pltpu.make_async_copy(wsum, w, sem.at[2])
    load_d = pltpu.make_async_copy(direct, d, sem.at[3])
    store_d = pltpu.make_async_copy(d, out, sem.at[4])
    for copy in (load_b, load_m, load_d, load_w):
        copy.start()
    load_b.wait()
    north = dot(spread(by_row, "north", W * SIDE), b[0]).reshape(W, SIDE, CH)
    south = dot(spread(by_row, "south", W * SIDE), b[2]).reshape(W, SIDE, CH)
    east = dot(spread(by_row, "east", 1024), b[1]).reshape(SIDE, 16, CH)
    west = dot(spread(by_row, "west", 1024), b[3]).reshape(SIDE, 16, CH)
    mid = slice(W, SIDE - W)
    load_m.wait()
    store_m.start()
    load_d.wait()
    d[mid, 0:16] = (d[mid, 0:16].astype(F32) + west[mid]).astype(BF)
    d[mid, 48:64] = (d[mid, 48:64].astype(F32) + east[mid]).astype(BF)
    zero = jnp.zeros((W, 32, CH), F32)
    for rows, add in ((slice(0, W), north), (slice(SIDE - W, SIDE), south)):
        more = jnp.concatenate([west[rows], zero, east[rows]], axis=1)
        d[rows] = (d[rows].astype(F32) + add + more).astype(BF)
    store_d.start()
    load_w.wait()
    for g in range(3):
        lanes = slice(128 * g, 128 * g + 128)
        egrad[:, lanes] = w[192 * g : 192 * g + 192].astype(F32) * scale
        rgrad[:, lanes] = w[576 + 192 * g : 768 + 192 * g].astype(F32) * scale
    low = w[WROWS : WROWS + 64].astype(F32) * scale
    high = w[WROWS + 64 : WROWS + 128].astype(F32) * scale
    for u in range(7):
        kgrad[u, :, 0:128] = low[8 * u : 8 * u + 7]
        kgrad[u, :, 128:192] = high[8 * u : 8 * u + 7, 0:64]
    store_d.wait()
    store_m.wait()


def last(mixed, direct, bands, wsum, scale):
    by_row, _ = static_tables()
    vm = pl.BlockSpec(memory_space=pltpu.VMEM)
    hbm = pl.BlockSpec(memory_space=pl.ANY)
    field = jax.ShapeDtypeStruct((SIDE, SIDE, CH), BF)
    return pl.pallas_call(
        functools.partial(last_kernel, scale),
        out_shape=(
            field,
            field,
            jax.ShapeDtypeStruct((7, 7, CH), F32),
            jax.ShapeDtypeStruct((CH, HID), F32),
            jax.ShapeDtypeStruct((CH, HID), F32),
        ),
        in_specs=[hbm] * 4 + [vm],
        out_specs=(hbm, hbm, vm, vm, vm),
        scratch_shapes=[
            pltpu.VMEM((SIDE, SIDE, CH), BF),
            pltpu.VMEM((4, 256, CH), BF),
            pltpu.VMEM((WROWS + KROWS, 128), BF),
            pltpu.VMEM((SIDE, SIDE, CH), BF),
            pltpu.SemaphoreType.DMA((6,)),
        ],
        compiler_params=pltpu.CompilerParams(vmem_limit_bytes=62 * 2**20),
        name="last",
    )(mixed, direct, bands, wsum, jnp.asarray(by_row))


def on_device(
    fields,
    cotangent,
    kernel,
    conv_bias,
    norm_gain,
    norm_bias,
    w_expand,
    bias_expand,
    w_reduce,
    bias_reduce,
    layer_scale,
    neighbors,
    rotations,
):
    ndp = lax.axis_size("dp")
    field = fields.reshape(SIDE, SIDE, CH)
    cot = cotangent.reshape(SIDE, SIDE, CH)
    params = [
        kernel,
        conv_bias,
        norm_gain,
        norm_bias,
        w_expand,
        bias_expand,
        w_reduce.T,
        bias_reduce,
        layer_scale,
    ]
    mixed, direct, bands, wsum = main(field, cot, neighbors, rotations, params, ndp)
    scale = 1.0 / math.sqrt(ndp * TILES * SIDE * SIDE)
    mixed, input_grad, kgrad, egrad, rgrad = last(mixed, direct, bands, wsum, scale)
    return (
        mixed.reshape(fields.shape),
        input_grad.reshape(fields.shape),
        kgrad,
        egrad,
        rgrad.T,
    )


def solution(mesh):
    split = P("dp", "tile", None, None, None)
    return jax.shard_map(
        on_device,
        mesh=mesh,
        in_specs=(split, split) + (P(),) * 11,
        out_specs=(split, split, P(), P(), P()),
        check_vma=False,
    )
```

```python
import functools
import math

import jax
import jax.numpy as jnp
import numpy as np
from jax import lax
from jax.experimental import pallas as pl
from jax.experimental.pallas import tpu as pltpu
from jax.sharding import PartitionSpec as P

OFFSETS = (2, 3, 0, 1, 2, 0, 0, 2)
SIDE = 64
W = 3
CH = 192
HID = 384
TILES = 16
CELLS = 16
NFREQ = 40
KROW = 80
EXT = SIDE + 2 * W
BF = jnp.bfloat16
F32 = jnp.float32
MESH = pl.DeviceIdType.MESH
WROWS = 1152
KROWS = 128
WBLOCK = 16
INDEX = ("top0", "top3", "bot2", "bot1", "side3", "side1", "north", "east", "south", "west")


def stripe_table():
    where = np.zeros((W, SIDE, 2), np.int64)
    used = {i: set() for i in range(16)}
    rest = []
    for w in range(W):
        for l in range(SIDE):
            if l < W:
                spot = (w * W + l, 0)
            elif l >= SIDE - W:
                spot = (7 + w * W + l - (SIDE - W), 11)
            else:
                rest.append((w, l))
                continue
            where[w, l] = spot
            used[spot[0]].add(spot[1])
    free = [(i, a) for i in range(16) for a in range(12) if a not in used[i]]
    for (w, l), spot in zip(rest, free):
        where[w, l] = spot
    return where


def np_pad(field, picked):
    north = np.rot90(picked[0], 2)
    east = np.rot90(picked[1], 1)
    south = picked[2]
    west = np.rot90(picked[3], 3)
    ne = np.rot90(picked[4], 2)[:, :W]
    se = picked[5][:, :W]
    sw = picked[6][:, SIDE - W :]
    nw = np.rot90(picked[7], 2)[:, SIDE - W :]
    return np.concatenate(
        [
            np.concatenate([nw, north, ne], 1),
            np.concatenate([west, field, east], 1),
            np.concatenate([sw, south, se], 1),
        ],
        0,
    )


def column_of(m):
    if m < SIDE:
        return m + W
    if m < SIDE + W:
        return m - SIDE
    if m < SIDE + 2 * W:
        return m
    return -1


@functools.lru_cache(None)
def static_tables():
    where = stripe_table()
    codes = np.arange(8 * W * SIDE).reshape(8, W, SIDE)
    padded = np_pad(np.full((SIDE, SIDE), -1), codes)

    def spot(code):
        k, w, l = np.unravel_index(code, (8, W, SIDE))
        i, a = where[w, l]
        return (k, i * CELLS + a) if k < 4 else (k - 4, i * CELLS + 12)

    index = {name: np.full(256, -1, np.int64) for name in INDEX}

    def places(p_list, m_list, names):
        for ip, p in enumerate(p_list):
            for im, m in enumerate(m_list):
                q = column_of(m)
                if q < 0 or padded[p, q] < 0:
                    continue
                k, row = spot(padded[p, q])
                index[names[k]][row] = ip * len(m_list) + im

    places([0, 1, 2], range(KROW), {0: "top0", 3: "top3"})
    places([67, 68, 69], range(KROW), {2: "bot2", 1: "bot1"})
    places(range(W, W + SIDE), range(SIDE, KROW), {3: "side3", 1: "side1"})

    cells = np.arange(SIDE * SIDE).reshape(SIDE, SIDE)
    bands = {
        "north": (cells[:W], SIDE, 0, 0),
        "east": (np.rot90(cells[:, SIDE - W :], 1), 16, 0, 48),
        "south": (np.rot90(cells[SIDE - W :], 2), SIDE, SIDE - W, 0),
        "west": (np.rot90(cells[:, :W], 3), 16, 0, 0),
    }
    for name, (band, pitch, row0, col0) in bands.items():
        for w in range(W):
            for l in range(SIDE):
                i, j = divmod(int(band[w, l]), SIDE)
                st, a = where[w, l]
                index[name][st * CELLS + a] = (i - row0) * pitch + j - col0
    table = np.stack([index[name] for name in INDEX]).astype(np.int32)
    by_row = np.full((16, 256), -1, np.int32)
    by_row[: len(INDEX)] = table
    by_col = np.full((256, 128), -1, np.int32)
    by_col[:, : len(INDEX)] = table.T
    return by_row, by_col


def spread(by_row, name, n):
    k = INDEX.index(name)
    place = lax.broadcasted_iota(jnp.int32, (n, 256), 0)
    return (place == by_row[k : k + 1]).astype(F32).astype(BF)


def gather(by_col, name, n):
    k = INDEX.index(name)
    place = lax.broadcasted_iota(jnp.int32, (256, n), 1)
    return (place == by_col[:, k : k + 1]).astype(F32).astype(BF)


@functools.lru_cache(None)
def dft_tables():
    n = 2 * NFREQ
    theta = 2 * np.pi * (np.arange(NFREQ) + 0.5) / n

    def cs(pos):
        ang = theta[:, None] * np.asarray(pos, np.float64)[None, :]
        live = (np.asarray(pos) >= 0)[None, :]
        return np.cos(ang) * live, np.sin(ang) * live

    def inverse(c, s):
        both = np.stack([c.reshape(5, 8, -1), -s.reshape(5, 8, -1)], 1)
        return (2 / n) * both.reshape(2 * NFREQ, -1).T

    cols = [column_of(m) for m in range(KROW)]
    c, s = cs(cols)
    fwd_x = np.concatenate([c, -s, c - s], 0)
    inv_p = inverse(c, s)
    c, s = cs(np.arange(SIDE))
    inv_y = inverse(c, s)
    fwd_g = np.concatenate([c, -s, c - s, c + s], 0)
    taps = [0, 1, 2, 3, 4, 5, 6, -1]
    c, s = cs(taps)
    fwd_k = np.concatenate([c, s, c + s, c, -s, c - s], 0)
    inv_k = (2 / n) * np.concatenate([c + s, c - s, -s], 0).T
    return (
        fwd_x.astype(jnp.bfloat16),
        inv_y.astype(jnp.bfloat16),
        fwd_g.astype(jnp.bfloat16),
        inv_p.astype(jnp.bfloat16),
        fwd_k.astype(np.float32),
        inv_k.astype(np.float32),
    )


def dot(a, b):
    return jnp.dot(a, b, preferred_element_type=F32)


def dot_nt(a, b):
    return lax.dot_general(a, b, (((1,), (1,)), ((), ())), preferred_element_type=F32)


def dot_tn(a, b):
    return lax.dot_general(a, b, (((0,), (0,)), ((), ())), preferred_element_type=F32)


def dot_exact(a, b):
    return jnp.dot(a, b, preferred_element_type=F32, precision=lax.Precision.HIGHEST)


def peer(me, off, n):
    return lax.rem(me + off, n)


def greet(axes):
    barrier = pltpu.get_barrier_semaphore()
    total = 0
    for axis, n in axes:
        me = lax.axis_index(axis)
        for off in range(1, n):
            pl.semaphore_signal(
                barrier, inc=1, device_id={axis: peer(me, off, n)}, device_id_type=MESH
            )
            total += 1
    return barrier, total


def exchange(axis, n, src_of, dst, send, recv):
    me = lax.axis_index(axis)
    copies = []
    for off in range(1, n):
        to = peer(me, off, n)
        copy = pltpu.make_async_remote_copy(
            src_ref=src_of(to),
            dst_ref=dst(me),
            send_sem=send.at[off],
            recv_sem=recv.at[off],
            device_id={axis: to},
            device_id_type=MESH,
        )
        copy.start()
        copies.append(copy)
    return copies


def finish(copies):
    for copy in copies:
        copy.wait()


PACKED = (6, TILES, CELLS, 128)


def pack(ref, value):
    ref[0:4] = value[..., 0:128]
    ref[4:6] = jnp.concatenate([value[0:2, :, :, 128:CH], value[2:4, :, :, 128:CH]], axis=-1)


def unpack(ref):
    low = ref[0:4].reshape(1024, 128)
    pair = ref[4:6].reshape(512, 128)
    high = jnp.concatenate([pair[:, 0:64], pair[:, 64:128]], axis=0)
    return jnp.concatenate([low, high], axis=-1)


LANES = ((0, 128), (128, 64))


def taps(xs, ks):
    acc = xs[0] * ks[0]
    for x, k in zip(xs[1:], ks[1:]):
        acc = acc + x * k
    return acc


def real_imag(a, b, c):
    return jnp.concatenate([a - b, c - a - b], axis=0).astype(BF)


def route_targets(base, me, axis):
    shape = (1024, 16) if axis == 0 else (16, 1024)
    row = lax.broadcasted_iota(jnp.int32, shape, axis)
    tile = lax.broadcasted_iota(jnp.int32, shape, 1 - axis)
    pick = (((row >> 4) & 15) == tile).astype(F32).astype(BF)
    found = dot_nt(pick, base) if axis == 0 else dot(base, pick)
    slot = lax.broadcasted_iota(jnp.int32, found.shape, 1 - axis)
    row = lax.broadcasted_iota(jnp.int32, found.shape, axis)
    edge = jnp.sum(jnp.where(slot == row >> 8, found, 0.0), axis=1 - axis, keepdims=True)
    corner = jnp.sum(jnp.where(slot == (row >> 8) + 4, found, 0.0), axis=1 - axis, keepdims=True)
    row = lax.broadcasted_iota(jnp.int32, edge.shape, axis)
    cell = row & 15
    right = jnp.where(me >= 7, 11.0, -8192.0)
    left = jnp.where(me <= 8, 0.0, -8192.0)
    corner = corner + jnp.where((row >> 8) & 1 == 0, right, left)
    return jnp.where(cell < 12, edge + cell.astype(F32), jnp.where(cell == 12, corner, -1.0))


def route_matrix(base, me, axis):
    place = lax.broadcasted_iota(jnp.int32, (1024, 1024), 1 - axis).astype(F32)
    return (place == route_targets(base, me, axis)).astype(F32).astype(BF)


def main_kernel(
    fields,
    cot_hbm,
    by_row,
    by_col,
    neighbors,
    rotations,
    offsets,
    fwd_x,
    inv_y,
    fwd_g,
    inv_p,
    fwd_k,
    inv_k,
    kernel,
    conv_bias,
    gain,
    nbias,
    w_exp,
    b_exp,
    w_red,
    b_red,
    lscale,
    mixed,
    direct,
    bands,
    wout,
    xpad,
    x3,
    y2,
    g4,
    kpad,
    kf,
    m3,
    egrad,
    rgrad,
    psides,
    ptop,
    pbot,
    cot,
    mix_out,
    hal,
    own,
    got,
    routed,
    back,
    own2,
    got2,
    routed2,
    back2,
    wsrc,
    wa,
    pa,
    wb,
    pc,
    wc,
    wd,
    ksrc,
    kwa,
    kpart,
    kwb,
    kwhole,
    kwc,
    dir_out,
    io_sem,
    *sems,
):
    s1, r1, s2, r2, s3, r3, s4, r4, sb, rb, sc, rc, skb, rkb = sems[:14]
    sa, ra, sd, rd, ska, rka, skc, rkc = sems[14:]
    me = lax.axis_index("tile")
    md = lax.axis_index("dp")
    ndp = wa.shape[0]
    dp_rows = wa.shape[1]
    krows = kpart.shape[0]
    owners = pa.shape[0]
    base = jnp.where(
        neighbors[...] >= 0,
        ((rotations[...] + offsets[...]) & 3) * 256 + neighbors[...] * CELLS,
        -4096,
    )
    base = base.astype(F32).astype(BF)
    barrier, total = greet((("tile", TILES), ("dp", ndp)))
    load_cot = pltpu.make_async_copy(cot_hbm, cot, io_sem.at[0])
    load_cot.start()
    bands_own = jnp.concatenate(
        [
            dot(gather(by_col, "north", W * SIDE), fields[0:W].reshape(W * SIDE, CH)),
            dot(gather(by_col, "east", 1024), fields[:, 48:64].reshape(1024, CH)),
            dot(gather(by_col, "south", W * SIDE), fields[SIDE - W :].reshape(W * SIDE, CH)),
            dot(gather(by_col, "west", 1024), fields[:, 0:16].reshape(1024, CH)),
        ],
        axis=0,
    )
    pack(own, bands_own.astype(BF).reshape(4, TILES, CELLS, CH))
    pl.semaphore_wait(barrier, total)
    copies = exchange("tile", TILES, lambda to: own.at[:, to], lambda m: got.at[:, m], s1, r1)
    got[:, me] = own[:, me]
    conv_bias, gain, nbias, b_exp, b_red, lscale = (
        ref[...].reshape(1, -1) for ref in (conv_bias, gain, nbias, b_exp, b_red, lscale)
    )
    for u in range(7):
        kpad[0:7] = kernel[u]
        kpad[7:8] = jnp.zeros((1, CH), F32)
        kf[u] = dot_exact(fwd_k[...], kpad[...])
    g4[0:6] = jnp.zeros((6, 4 * NFREQ, CH), F32)
    g4[6 + SIDE :] = jnp.zeros((6, 4 * NFREQ, CH), F32)
    xpad[W : W + SIDE, 0:SIDE] = fields[...]
    route = route_matrix(base, me, 0)
    finish(copies)
    pack(routed, dot(route, unpack(got)).astype(BF).reshape(4, TILES, CELLS, CH))
    copies = exchange("tile", TILES, lambda to: routed.at[:, to], lambda m: back.at[:, m], s2, r2)
    back[:, me] = routed[:, me]
    finish(copies)
    hal[...] = unpack(back).reshape(4, 256, CH)

    def put(n, *parts):
        return sum(dot(spread(by_row, name, n), hal[k]) for name, k in parts).astype(BF)

    xpad[0:W] = put(W * KROW, ("top0", 0), ("top3", 3)).reshape(W, KROW, CH)
    xpad[W + SIDE :] = put(W * KROW, ("bot2", 2), ("bot1", 1)).reshape(W, KROW, CH)
    xpad[W : W + SIDE, SIDE:] = put(SIDE * 16, ("side3", 3), ("side1", 1)).reshape(SIDE, 16, CH)

    def to_freq(r, _):
        x3[r] = dot(fwd_x[...], xpad[r])
        return 0

    lax.fori_loop(0, EXT, to_freq, 0, unroll=14)

    for l0, lw in LANES:
        for fb in range(5):
            rows = [slice(40 * t + 8 * fb, 40 * t + 8 * fb + 8) for t in range(3)]
            lanes = slice(l0, l0 + lw)
            kk = [[kf[u, rows[t], lanes] for t in range(3)] for u in range(7)]

            def conv(ib, _, fb=fb, rows=rows, lanes=lanes, kk=kk):
                i0 = ib * 4
                prods = []
                for t in range(3):
                    xs = [x3[i0 + r, rows[t], lanes] for r in range(10)]
                    prods.append([taps(xs[d : d + 7], [k[t] for k in kk]) for d in range(4)])
                for d in range(4):
                    y2[i0 + d, 16 * fb : 16 * fb + 16, lanes] = real_imag(*(p[d] for p in prods))
                return 0

            lax.fori_loop(0, SIDE // 4, conv, 0, unroll=2)

    load_cot.wait()
    egrad[...] = jnp.zeros_like(egrad)
    rgrad[...] = jnp.zeros_like(rgrad)
    step = 4
    parts = 8
    n = step * SIDE

    def part(i0):
        conv_out = jnp.concatenate([dot(inv_y[...], y2[i0 + d]) for d in range(step)], axis=0)
        yield
        conv_out = conv_out + conv_bias
        shifted = conv_out - jnp.mean(conv_out, axis=-1, keepdims=True)
        inv_std = lax.rsqrt(jnp.mean(shifted * shifted, axis=-1, keepdims=True) + 1e-06)
        centred = shifted * inv_std
        normed = (centred * gain + nbias).astype(BF)
        yield
        pre = dot(normed, w_exp[...]) + b_exp
        bgrad = (lscale * cot[pl.ds(i0, step)].reshape(n, CH).astype(F32)).astype(BF)
        act_grad = dot(bgrad, w_red[...])
        yield
        size = jnp.abs(pre)
        t = 1.0 / (1.0 + (0.3275911 * math.sqrt(0.5)) * size)
        dens = jnp.exp(-0.5 * pre * pre)
        poly = t * (
            0.127414796
            + t * (-0.142248368 + t * (0.7107068705 + t * (-0.7265760135 + t * 0.5307027145)))
        )
        tail = poly * dens
        phi = jnp.where(pre >= 0, 1.0 - tail, tail)
        act = (pre * phi).astype(BF)
        pre_grad = (act_grad * (phi + pre * (dens * 0.3989422804014327))).astype(BF)
        yield
        ngrad = dot_nt(pre_grad, w_exp[...])
        branch = dot_nt(act, w_red[...])
        rgrad[...] += dot_tn(bgrad, act)
        egrad[...] += dot_tn(normed, pre_grad)
        yield
        mix = fields[pl.ds(i0, step)].reshape(n, CH).astype(F32) + lscale * (branch + b_red)
        mix_out[pl.ds(i0, step)] = mix.astype(BF).reshape(step, SIDE, CH)
        ngrad = ngrad * gain
        m1 = jnp.mean(ngrad, axis=-1, keepdims=True)
        m2 = jnp.mean(ngrad * centred, axis=-1, keepdims=True)
        cgrad = (inv_std * (ngrad - m1 - centred * m2)).astype(BF)
        yield
        for d in range(step):
            g4[6 + i0 + d] = dot(fwd_g[...], cgrad[d * SIDE : (d + 1) * SIDE])
        yield

    def chunk(ic, _):
        gens = [part(pl.multiple_of((ic * parts + k) * step, step)) for k in range(parts)]
        for tick in range(7 + 1 * (parts - 1)):
            for k in range(parts):
                if 0 <= tick - 1 * k < 7:
                    next(gens[k])
        return 0

    lax.fori_loop(0, SIDE // (step * parts), chunk, 0)

    store_mixed = pltpu.make_async_copy(mix_out, mixed, io_sem.at[1])
    store_mixed.start()

    for g in range(3):
        lanes = slice(128 * g, 128 * g + 128)
        wsrc[192 * g : 192 * g + 192] = egrad[:, lanes].astype(BF)
        wsrc[576 + 192 * g : 768 + 192 * g] = rgrad[:, lanes].astype(BF)

    def dp_block(to):
        return wsrc.at[pl.ds(pl.multiple_of(to * dp_rows, 16), dp_rows)]

    ca = exchange("dp", ndp, dp_block, lambda m: wa.at[m], sa, ra)
    wa[md] = wsrc[pl.ds(pl.multiple_of(md * dp_rows, 16), dp_rows)]

    for l0, lw in LANES:
        for fb in range(5):
            rows = [slice(40 * t + 8 * fb, 40 * t + 8 * fb + 8) for t in range(4)]
            grow = (rows[0], rows[1], rows[3])
            lanes = slice(l0, l0 + lw)

            def kgrad(ib, accs, rows=rows, lanes=lanes, grow=grow):
                i0 = ib * 4
                accs = list(accs)
                for t in range(3):
                    xs = [x3[i0 + r, rows[t], lanes] for r in range(10)]
                    for d in range(4):
                        g = g4[6 + i0 + d, grow[t], lanes]
                        for u in range(7):
                            accs[7 * t + u] = accs[7 * t + u] + xs[d + u] * g
                return tuple(accs)

            zero = jnp.zeros((8, lw), F32)
            accs = lax.fori_loop(0, SIDE // 4, kgrad, (zero,) * 21, unroll=2)
            for t in range(3):
                for u in range(7):
                    m3[u, rows[t], lanes] = accs[7 * t + u]


    kg = jnp.concatenate([dot_exact(inv_k[...], m3[u]) for u in range(7)], axis=0)
    kg = jnp.concatenate([kg, jnp.zeros((8, CH), F32)], axis=0)
    ksrc[0:64] = kg[:, 0:128]
    ksrc[64:128] = jnp.concatenate([kg[:, 128:192], jnp.zeros((64, 64), F32)], axis=1)

    def kernel_block(to):
        return ksrc.at[pl.ds(pl.multiple_of(to * krows, 16), krows)]

    ka = exchange("dp", ndp, kernel_block, lambda m: kwa.at[m], ska, rka)
    kwa[md] = ksrc[pl.ds(pl.multiple_of(md * krows, 16), krows)]

    for l0, lw in LANES:
        for fb in range(5):
            rows = [slice(40 * t + 8 * fb, 40 * t + 8 * fb + 8) for t in range(3)]
            lanes = slice(l0, l0 + lw)

            kk = [
                [kf[u, 120 + 40 * t + 8 * fb : 128 + 40 * t + 8 * fb, lanes] for t in range(3)]
                for u in range(7)
            ]

            def pconv(ib, _, fb=fb, rows=rows, lanes=lanes, kk=kk):
                p0 = ib * 5
                prods = []
                for t in range(3):
                    gs = [g4[p0 + r, rows[t], lanes] for r in range(11)]
                    back = [k[t] for k in kk][::-1]
                    prods.append([taps(gs[d : d + 7], back) for d in range(5)])
                for d in range(5):
                    y2[p0 + d, 16 * fb : 16 * fb + 16, lanes] = real_imag(*(p[d] for p in prods))
                return 0

            lax.fori_loop(0, EXT // 5, pconv, 0, unroll=2)


    finish(ca)
    part = wa[0].astype(F32)
    for j in range(1, ndp):
        part = part + wa[j].astype(F32)
    pa[...] = part.reshape(owners, WBLOCK, 128)

    def share(off, src, dst, send, recv):
        return pltpu.make_async_remote_copy(
            src_ref=src,
            dst_ref=dst,
            send_sem=send.at[off],
            recv_sem=recv.at[off],
            device_id={"tile": peer(me, off, TILES)},
            device_id_type=MESH,
        )

    def to_owner(off):
        to = peer(me, off, TILES)
        return to, share(off, pa.at[lax.rem(to, owners)], wb.at[me], sb, rb)

    for off in range(1, TILES):
        to, copy = to_owner(off)
        pl.when(to < owners)(copy.start)

    @pl.when(me < owners)
    def _():
        wb[me] = pa[lax.rem(me, owners)]

    finish(ka)
    part = kwa[0]
    for j in range(1, ndp):
        part = part + kwa[j]
    kpart[...] = part.astype(BF)
    kb = exchange("tile", TILES, lambda to: kpart, lambda m: kwb.at[m], skb, rkb)
    kwb[me] = kpart[...]
    for p in range(W):
        ptop[p] = dot(inv_p[...], y2[p]).astype(BF)
        pbot[p] = dot(inv_p[...], y2[W + SIDE + p]).astype(BF)

    def from_freq(i, _):
        back = dot(inv_p[...], y2[i + W])
        dir_out[i] = (cot[i].astype(F32) + back[0:SIDE]).astype(BF)
        psides[i] = back[SIDE:].astype(BF)
        return 0

    lax.fori_loop(0, SIDE, from_freq, 0, unroll=8)
    store_direct = pltpu.make_async_copy(dir_out, direct, io_sem.at[2])
    store_direct.start()

    top = ptop[...].reshape(W * KROW, CH)
    bot = pbot[...].reshape(W * KROW, CH)
    sides = psides[...].reshape(SIDE * 16, CH)


    def take(*parts):
        total = sum(dot(gather(by_col, name, part.shape[0]), part) for name, part in parts)
        return total.astype(BF).reshape(1, TILES, CELLS, CH)

    taken = [
        take(("top0", top)),
        take(("side1", sides), ("bot1", bot)),
        take(("bot2", bot)),
        take(("side3", sides), ("top3", top)),
    ]
    pack(own2, jnp.concatenate(taken, axis=0))


    c3 = exchange("tile", TILES, lambda to: own2.at[:, to], lambda m: got2.at[:, m], s3, r3)
    got2[:, me] = own2[:, me]
    for off in range(1, TILES):
        to, copy = to_owner(off)
        pl.when(to < owners)(copy.wait_send)
        pl.when(me < owners)(copy.wait_recv)

    mine = lax.rem(me, owners)

    @pl.when(me < owners)
    def _():
        whole = wb[0]
        for j in range(1, TILES):
            whole = whole + wb[j]
        pc[...] = whole.astype(BF)
        wc[mine] = whole.astype(BF)
        for off in range(1, TILES):
            share(off, pc, wc.at[mine], sc, rc).start()

    finish(kb)
    part = kwb[0].astype(F32)
    for j in range(1, TILES):
        part = part + kwb[j].astype(F32)
    kwhole[...] = part.astype(BF)
    kc = exchange("dp", ndp, lambda to: kwhole, lambda m: kwc.at[m], skc, rkc)
    kwc[md] = kwhole[...]
    route_back = route_matrix(base, me, 1)
    finish(c3)
    pack(routed2, dot(route_back, unpack(got2)).astype(BF).reshape(4, TILES, CELLS, CH))
    c4 = exchange("tile", TILES, lambda to: routed2.at[:, to], lambda m: back2.at[:, m], s4, r4)
    back2[:, me] = routed2[:, me]

    for off in range(1, TILES):
        copy = share(off, pc, wc.at[mine], sc, rc)
        pl.when(me < owners)(copy.wait_send)
        pl.when(peer(me, TILES - off, TILES) < owners)(copy.wait_recv)

    block = wc[...].reshape(owners * WBLOCK, 128)
    pd = wa.at[0]
    pd[...] = block
    cd = exchange("dp", ndp, lambda to: pd, lambda m: wd.at[m], sd, rd)
    wd[md] = block
    finish(cd)
    wout[0:WROWS] = wd[...].reshape(WROWS, 128)
    finish(c4)
    bands[...] = unpack(back2).reshape(4, 256, CH)
    finish(kc)
    wout[WROWS:] = kwc[...].reshape(KROWS, 128)
    store_direct.wait()
    store_mixed.wait()


def main(fields, cotangent, neighbors, rotations, params, ndp):
    index = [jnp.asarray(t) for t in static_tables()]
    tables = [jnp.asarray(t) for t in dft_tables()]
    vm = pl.BlockSpec(memory_space=pltpu.VMEM)
    hbm = pl.BlockSpec(memory_space=pl.ANY)
    halo_buf = pltpu.VMEM(PACKED, BF)
    sem = pltpu.SemaphoreType.DMA((TILES,))
    sem_dp = pltpu.SemaphoreType.DMA((ndp,))
    dp_rows = WROWS // ndp
    krows = KROWS // ndp
    owners = dp_rows // WBLOCK
    offsets = jnp.asarray(OFFSETS, jnp.int32).reshape(8, 1)
    args = [fields, cotangent, *index, neighbors.T, rotations.T, offsets, *tables, *params]
    field = jax.ShapeDtypeStruct((SIDE, SIDE, CH), BF)
    return pl.pallas_call(
        main_kernel,
        out_shape=(
            field,
            field,
            jax.ShapeDtypeStruct((4, 256, CH), BF),
            jax.ShapeDtypeStruct((WROWS + KROWS, 128), BF),
        ),
        in_specs=[vm, hbm] + [vm] * (len(args) - 2),
        out_specs=(hbm, hbm, vm, vm),
        scratch_shapes=[
            pltpu.VMEM((EXT, KROW, CH), BF),
            pltpu.VMEM((EXT, 3 * NFREQ, CH), F32),
            pltpu.VMEM((EXT, 2 * NFREQ, CH), BF),
            pltpu.VMEM((SIDE + 12, 4 * NFREQ, CH), F32),
            pltpu.VMEM((8, CH), F32),
            pltpu.VMEM((7, 6 * NFREQ, CH), F32),
            pltpu.VMEM((7, 3 * NFREQ, CH), F32),
            pltpu.VMEM((CH, HID), F32),
            pltpu.VMEM((CH, HID), F32),
            pltpu.VMEM((SIDE, 16, CH), BF),
            pltpu.VMEM((W, KROW, CH), BF),
            pltpu.VMEM((W, KROW, CH), BF),
            pltpu.VMEM((SIDE, SIDE, CH), BF),
            pltpu.VMEM((SIDE, SIDE, CH), BF),
            pltpu.VMEM((4, 256, CH), BF),
        ]
        + [halo_buf] * 8
        + [
            pltpu.VMEM((WROWS, 128), BF),
            pltpu.VMEM((ndp, dp_rows, 128), BF),
            pltpu.VMEM((owners, WBLOCK, 128), F32),
            pltpu.VMEM((TILES, WBLOCK, 128), F32),
            pltpu.VMEM((WBLOCK, 128), BF),
            pltpu.VMEM((owners, WBLOCK, 128), BF),
            pltpu.VMEM((ndp, dp_rows, 128), BF),
            pltpu.VMEM((KROWS, 128), F32),
            pltpu.VMEM((ndp, krows, 128), F32),
            pltpu.VMEM((krows, 128), BF),
            pltpu.VMEM((TILES, krows, 128), BF),
            pltpu.VMEM((krows, 128), BF),
            pltpu.VMEM((ndp, krows, 128), BF),
            pltpu.VMEM((SIDE, SIDE, CH), BF),
            pltpu.SemaphoreType.DMA((3,)),
        ]
        + [sem] * 14
        + [sem_dp] * 8,
        compiler_params=pltpu.CompilerParams(
            collective_id=0, has_side_effects=True, vmem_limit_bytes=62 * 2**20
        ),
        name="main",
    )(*args)


def last_kernel(
    scale, mixed, direct, bands, wsum, by_row, mixed_out, out, kgrad, egrad, rgrad, d, b, w, m, sem
):
    load_m = pltpu.make_async_copy(mixed, m, sem.at[0])
    store_m = pltpu.make_async_copy(m, mixed_out, sem.at[5])
    load_b = pltpu.make_async_copy(bands, b, sem.at[1])
    load_w = pltpu.make_async_copy(wsum, w, sem.at[2])
    load_d = pltpu.make_async_copy(direct, d, sem.at[3])
    store_d = pltpu.make_async_copy(d, out, sem.at[4])
    for copy in (load_b, load_d, load_w, load_m):
        copy.start()
    load_b.wait()
    north = dot(spread(by_row, "north", W * SIDE), b[0]).reshape(W, SIDE, CH)
    south = dot(spread(by_row, "south", W * SIDE), b[2]).reshape(W, SIDE, CH)
    east = dot(spread(by_row, "east", 1024), b[1]).reshape(SIDE, 16, CH)
    west = dot(spread(by_row, "west", 1024), b[3]).reshape(SIDE, 16, CH)
    mid = slice(W, SIDE - W)
    load_d.wait()
    d[mid, 0:16] = (d[mid, 0:16].astype(F32) + west[mid]).astype(BF)
    d[mid, 48:64] = (d[mid, 48:64].astype(F32) + east[mid]).astype(BF)
    zero = jnp.zeros((W, 32, CH), F32)
    for rows, add in ((slice(0, W), north), (slice(SIDE - W, SIDE), south)):
        more = jnp.concatenate([west[rows], zero, east[rows]], axis=1)
        d[rows] = (d[rows].astype(F32) + add + more).astype(BF)
    store_d.start()
    load_m.wait()
    store_m.start()
    load_w.wait()
    for g in range(3):
        lanes = slice(128 * g, 128 * g + 128)
        egrad[:, lanes] = w[192 * g : 192 * g + 192].astype(F32) * scale
        rgrad[:, lanes] = w[576 + 192 * g : 768 + 192 * g].astype(F32) * scale
    low = w[WROWS : WROWS + 64].astype(F32) * scale
    high = w[WROWS + 64 : WROWS + 128].astype(F32) * scale
    for u in range(7):
        kgrad[u, :, 0:128] = low[8 * u : 8 * u + 7]
        kgrad[u, :, 128:192] = high[8 * u : 8 * u + 7, 0:64]
    store_d.wait()
    store_m.wait()


def last(mixed, direct, bands, wsum, scale):
    by_row, _ = static_tables()
    vm = pl.BlockSpec(memory_space=pltpu.VMEM)
    hbm = pl.BlockSpec(memory_space=pl.ANY)
    field = jax.ShapeDtypeStruct((SIDE, SIDE, CH), BF)
    return pl.pallas_call(
        functools.partial(last_kernel, scale),
        out_shape=(
            field,
            field,
            jax.ShapeDtypeStruct((7, 7, CH), F32),
            jax.ShapeDtypeStruct((CH, HID), F32),
            jax.ShapeDtypeStruct((CH, HID), F32),
        ),
        in_specs=[hbm] * 4 + [vm],
        out_specs=(hbm, hbm, vm, vm, vm),
        scratch_shapes=[
            pltpu.VMEM((SIDE, SIDE, CH), BF),
            pltpu.VMEM((4, 256, CH), BF),
            pltpu.VMEM((WROWS + KROWS, 128), BF),
            pltpu.VMEM((SIDE, SIDE, CH), BF),
            pltpu.SemaphoreType.DMA((6,)),
        ],
        compiler_params=pltpu.CompilerParams(vmem_limit_bytes=62 * 2**20),
        name="last",
    )(mixed, direct, bands, wsum, jnp.asarray(by_row))


def on_device(
    fields,
    cotangent,
    kernel,
    conv_bias,
    norm_gain,
    norm_bias,
    w_expand,
    bias_expand,
    w_reduce,
    bias_reduce,
    layer_scale,
    neighbors,
    rotations,
):
    ndp = lax.axis_size("dp")
    field = fields.reshape(SIDE, SIDE, CH)
    cot = cotangent.reshape(SIDE, SIDE, CH)
    params = [
        kernel,
        conv_bias,
        norm_gain,
        norm_bias,
        w_expand,
        bias_expand,
        w_reduce.T,
        bias_reduce,
        layer_scale,
    ]
    mixed, direct, bands, wsum = main(field, cot, neighbors, rotations, params, ndp)
    scale = 1.0 / math.sqrt(ndp * TILES * SIDE * SIDE)
    mixed, input_grad, kgrad, egrad, rgrad = last(mixed, direct, bands, wsum, scale)
    return (
        mixed.reshape(fields.shape),
        input_grad.reshape(fields.shape),
        kgrad,
        egrad,
        rgrad.T,
    )


def solution(mesh):
    split = P("dp", "tile", None, None, None)
    return jax.shard_map(
        on_device,
        mesh=mesh,
        in_specs=(split, split) + (P(),) * 11,
        out_specs=(split, split, P(), P(), P()),
        check_vma=False,
    )
```

```python
import functools
import math

import jax
import jax.numpy as jnp
import numpy as np
from jax import lax
from jax.experimental import pallas as pl
from jax.experimental.pallas import tpu as pltpu
from jax.sharding import PartitionSpec as P

OFFSETS = (2, 3, 0, 1, 2, 0, 0, 2)
SIDE = 64
W = 3
CH = 192
HID = 384
TILES = 16
CELLS = 16
NFREQ = 40
KROW = 80
EXT = SIDE + 2 * W
BF = jnp.bfloat16
F32 = jnp.float32
MESH = pl.DeviceIdType.MESH
FAR_FIRST = (12, 4, 11, 13, 5, 3, 10, 14, 6, 2, 9, 7, 8, 15, 1)
WROWS = 1152
KROWS = 128
WBLOCK = 16
INDEX = ("top0", "top3", "bot2", "bot1", "side3", "side1", "north", "east", "south", "west")


def stripe_table():
    where = np.zeros((W, SIDE, 2), np.int64)
    used = {i: set() for i in range(16)}
    rest = []
    for w in range(W):
        for l in range(SIDE):
            if l < W:
                spot = (w * W + l, 0)
            elif l >= SIDE - W:
                spot = (7 + w * W + l - (SIDE - W), 11)
            else:
                rest.append((w, l))
                continue
            where[w, l] = spot
            used[spot[0]].add(spot[1])
    free = [(i, a) for i in range(16) for a in range(12) if a not in used[i]]
    for (w, l), spot in zip(rest, free):
        where[w, l] = spot
    return where


def np_pad(field, picked):
    north = np.rot90(picked[0], 2)
    east = np.rot90(picked[1], 1)
    south = picked[2]
    west = np.rot90(picked[3], 3)
    ne = np.rot90(picked[4], 2)[:, :W]
    se = picked[5][:, :W]
    sw = picked[6][:, SIDE - W :]
    nw = np.rot90(picked[7], 2)[:, SIDE - W :]
    return np.concatenate(
        [
            np.concatenate([nw, north, ne], 1),
            np.concatenate([west, field, east], 1),
            np.concatenate([sw, south, se], 1),
        ],
        0,
    )


def column_of(m):
    if m < SIDE:
        return m + W
    if m < SIDE + W:
        return m - SIDE
    if m < SIDE + 2 * W:
        return m
    return -1


@functools.lru_cache(None)
def static_tables():
    where = stripe_table()
    codes = np.arange(8 * W * SIDE).reshape(8, W, SIDE)
    padded = np_pad(np.full((SIDE, SIDE), -1), codes)

    def spot(code):
        k, w, l = np.unravel_index(code, (8, W, SIDE))
        i, a = where[w, l]
        return (k, i * CELLS + a) if k < 4 else (k - 4, i * CELLS + 12)

    index = {name: np.full(256, -1, np.int64) for name in INDEX}

    def places(p_list, m_list, names):
        for ip, p in enumerate(p_list):
            for im, m in enumerate(m_list):
                q = column_of(m)
                if q < 0 or padded[p, q] < 0:
                    continue
                k, row = spot(padded[p, q])
                index[names[k]][row] = ip * len(m_list) + im

    places([0, 1, 2], range(KROW), {0: "top0", 3: "top3"})
    places([67, 68, 69], range(KROW), {2: "bot2", 1: "bot1"})
    places(range(W, W + SIDE), range(SIDE, KROW), {3: "side3", 1: "side1"})

    cells = np.arange(SIDE * SIDE).reshape(SIDE, SIDE)
    bands = {
        "north": (cells[:W], SIDE, 0, 0),
        "east": (np.rot90(cells[:, SIDE - W :], 1), 16, 0, 48),
        "south": (np.rot90(cells[SIDE - W :], 2), SIDE, SIDE - W, 0),
        "west": (np.rot90(cells[:, :W], 3), 16, 0, 0),
    }
    for name, (band, pitch, row0, col0) in bands.items():
        for w in range(W):
            for l in range(SIDE):
                i, j = divmod(int(band[w, l]), SIDE)
                st, a = where[w, l]
                index[name][st * CELLS + a] = (i - row0) * pitch + j - col0
    table = np.stack([index[name] for name in INDEX]).astype(np.int32)
    by_row = np.full((16, 256), -1, np.int32)
    by_row[: len(INDEX)] = table
    by_col = np.full((256, 128), -1, np.int32)
    by_col[:, : len(INDEX)] = table.T
    return by_row, by_col


def spread(by_row, name, n):
    k = INDEX.index(name)
    place = lax.broadcasted_iota(jnp.int32, (n, 256), 0)
    return (place == by_row[k : k + 1]).astype(F32).astype(BF)


def gather(by_col, name, n):
    k = INDEX.index(name)
    place = lax.broadcasted_iota(jnp.int32, (256, n), 1)
    return (place == by_col[:, k : k + 1]).astype(F32).astype(BF)


@functools.lru_cache(None)
def dft_tables():
    n = 2 * NFREQ
    theta = 2 * np.pi * (np.arange(NFREQ) + 0.5) / n

    def cs(pos):
        ang = theta[:, None] * np.asarray(pos, np.float64)[None, :]
        live = (np.asarray(pos) >= 0)[None, :]
        return np.cos(ang) * live, np.sin(ang) * live

    def inverse(c, s):
        both = np.stack([c.reshape(5, 8, -1), -s.reshape(5, 8, -1)], 1)
        return (2 / n) * both.reshape(2 * NFREQ, -1).T

    cols = [column_of(m) for m in range(KROW)]
    c, s = cs(cols)
    fwd_x = np.concatenate([c, -s, c - s], 0)
    inv_p = inverse(c, s)
    c, s = cs(np.arange(SIDE))
    inv_y = inverse(c, s)
    fwd_g = np.concatenate([c, -s, c - s, c + s], 0)
    taps = [0, 1, 2, 3, 4, 5, 6, -1]
    c, s = cs(taps)
    fwd_k = np.concatenate([c, s, c + s, c, -s, c - s], 0)
    inv_k = (2 / n) * np.concatenate([c + s, c - s, -s], 0).T
    return (
        fwd_x.astype(jnp.bfloat16),
        inv_y.astype(jnp.bfloat16),
        fwd_g.astype(jnp.bfloat16),
        inv_p.astype(jnp.bfloat16),
        fwd_k.astype(np.float32),
        inv_k.astype(np.float32),
    )


def dot(a, b):
    return jnp.dot(a, b, preferred_element_type=F32)


def dot_nt(a, b):
    return lax.dot_general(a, b, (((1,), (1,)), ((), ())), preferred_element_type=F32)


def dot_tn(a, b):
    return lax.dot_general(a, b, (((0,), (0,)), ((), ())), preferred_element_type=F32)


def dot_exact(a, b):
    return jnp.dot(a, b, preferred_element_type=F32, precision=lax.Precision.HIGHEST)


def peer(me, off, n):
    return lax.rem(me + off, n)


def greet(axes):
    barrier = pltpu.get_barrier_semaphore()
    total = 0
    for axis, n in axes:
        me = lax.axis_index(axis)
        for off in range(1, n):
            pl.semaphore_signal(
                barrier, inc=1, device_id={axis: peer(me, off, n)}, device_id_type=MESH
            )
            total += 1
    return barrier, total


def exchange(axis, n, src_of, dst, send, recv):
    me = lax.axis_index(axis)
    copies = []
    for off in FAR_FIRST if n == TILES else range(1, n):
        to = peer(me, off, n)
        copy = pltpu.make_async_remote_copy(
            src_ref=src_of(to),
            dst_ref=dst(me),
            send_sem=send.at[off],
            recv_sem=recv.at[off],
            device_id={axis: to},
            device_id_type=MESH,
        )
        copy.start()
        copies.append(copy)
    return copies


def finish(copies):
    for copy in copies:
        copy.wait()


PACKED = (6, TILES, CELLS, 128)


def pack(ref, value):
    ref[0:4] = value[..., 0:128]
    ref[4:6] = jnp.concatenate([value[0:2, :, :, 128:CH], value[2:4, :, :, 128:CH]], axis=-1)


def unpack(ref):
    low = ref[0:4].reshape(1024, 128)
    pair = ref[4:6].reshape(512, 128)
    high = jnp.concatenate([pair[:, 0:64], pair[:, 64:128]], axis=0)
    return jnp.concatenate([low, high], axis=-1)


LANES = ((0, 128), (128, 64))


def taps(xs, ks):
    acc = xs[0] * ks[0]
    for x, k in zip(xs[1:], ks[1:]):
        acc = acc + x * k
    return acc


def real_imag(a, b, c):
    return jnp.concatenate([a - b, c - a - b], axis=0).astype(BF)


def route_targets(base, me, axis):
    shape = (1024, 16) if axis == 0 else (16, 1024)
    row = lax.broadcasted_iota(jnp.int32, shape, axis)
    tile = lax.broadcasted_iota(jnp.int32, shape, 1 - axis)
    pick = (((row >> 4) & 15) == tile).astype(F32).astype(BF)
    found = dot_nt(pick, base) if axis == 0 else dot(base, pick)
    slot = lax.broadcasted_iota(jnp.int32, found.shape, 1 - axis)
    row = lax.broadcasted_iota(jnp.int32, found.shape, axis)
    edge = jnp.sum(jnp.where(slot == row >> 8, found, 0.0), axis=1 - axis, keepdims=True)
    corner = jnp.sum(jnp.where(slot == (row >> 8) + 4, found, 0.0), axis=1 - axis, keepdims=True)
    row = lax.broadcasted_iota(jnp.int32, edge.shape, axis)
    cell = row & 15
    right = jnp.where(me >= 7, 11.0, -8192.0)
    left = jnp.where(me <= 8, 0.0, -8192.0)
    corner = corner + jnp.where((row >> 8) & 1 == 0, right, left)
    return jnp.where(cell < 12, edge + cell.astype(F32), jnp.where(cell == 12, corner, -1.0))


def route_matrix(base, me, axis):
    place = lax.broadcasted_iota(jnp.int32, (1024, 1024), 1 - axis).astype(F32)
    return (place == route_targets(base, me, axis)).astype(F32).astype(BF)


def main_kernel(
    fields,
    cot_hbm,
    by_row,
    by_col,
    neighbors,
    rotations,
    offsets,
    fwd_x,
    inv_y,
    fwd_g,
    inv_p,
    fwd_k,
    inv_k,
    kernel,
    conv_bias,
    gain,
    nbias,
    w_exp,
    b_exp,
    w_red,
    b_red,
    lscale,
    mixed,
    direct,
    bands,
    wout,
    xpad,
    x3,
    y2,
    g4,
    kpad,
    kf,
    m3,
    egrad,
    rgrad,
    psides,
    ptop,
    pbot,
    cot,
    mix_out,
    hal,
    own,
    got,
    routed,
    back,
    own2,
    got2,
    routed2,
    back2,
    wsrc,
    wa,
    pa,
    wb,
    pc,
    wc,
    wd,
    ksrc,
    kwa,
    kpart,
    kwb,
    kwhole,
    kwc,
    dir_out,
    io_sem,
    *sems,
):
    s1, r1, s2, r2, s3, r3, s4, r4, sb, rb, sc, rc, skb, rkb = sems[:14]
    sa, ra, sd, rd, ska, rka, skc, rkc = sems[14:]
    me = lax.axis_index("tile")
    md = lax.axis_index("dp")
    ndp = wa.shape[0]
    dp_rows = wa.shape[1]
    krows = kpart.shape[0]
    owners = pa.shape[0]
    base = jnp.where(
        neighbors[...] >= 0,
        ((rotations[...] + offsets[...]) & 3) * 256 + neighbors[...] * CELLS,
        -4096,
    )
    base = base.astype(F32).astype(BF)
    barrier, total = greet((("tile", TILES), ("dp", ndp)))
    load_cot = pltpu.make_async_copy(cot_hbm, cot, io_sem.at[0])
    load_cot.start()
    bands_own = jnp.concatenate(
        [
            dot(gather(by_col, "north", W * SIDE), fields[0:W].reshape(W * SIDE, CH)),
            dot(gather(by_col, "east", 1024), fields[:, 48:64].reshape(1024, CH)),
            dot(gather(by_col, "south", W * SIDE), fields[SIDE - W :].reshape(W * SIDE, CH)),
            dot(gather(by_col, "west", 1024), fields[:, 0:16].reshape(1024, CH)),
        ],
        axis=0,
    )
    pack(own, bands_own.astype(BF).reshape(4, TILES, CELLS, CH))
    pl.semaphore_wait(barrier, total)
    copies = exchange("tile", TILES, lambda to: own.at[:, to], lambda m: got.at[:, m], s1, r1)
    got[:, me] = own[:, me]
    conv_bias, gain, nbias, b_exp, b_red, lscale = (
        ref[...].reshape(1, -1) for ref in (conv_bias, gain, nbias, b_exp, b_red, lscale)
    )
    for u in range(7):
        kpad[0:7] = kernel[u]
        kpad[7:8] = jnp.zeros((1, CH), F32)
        kf[u] = dot_exact(fwd_k[...], kpad[...])
    g4[0:6] = jnp.zeros((6, 4 * NFREQ, CH), F32)
    g4[6 + SIDE :] = jnp.zeros((6, 4 * NFREQ, CH), F32)
    xpad[W : W + SIDE, 0:SIDE] = fields[...]
    route = route_matrix(base, me, 0)
    finish(copies)
    pack(routed, dot(route, unpack(got)).astype(BF).reshape(4, TILES, CELLS, CH))
    copies = exchange("tile", TILES, lambda to: routed.at[:, to], lambda m: back.at[:, m], s2, r2)
    back[:, me] = routed[:, me]
    finish(copies)
    hal[...] = unpack(back).reshape(4, 256, CH)

    def put(n, *parts):
        return sum(dot(spread(by_row, name, n), hal[k]) for name, k in parts).astype(BF)

    xpad[0:W] = put(W * KROW, ("top0", 0), ("top3", 3)).reshape(W, KROW, CH)
    xpad[W + SIDE :] = put(W * KROW, ("bot2", 2), ("bot1", 1)).reshape(W, KROW, CH)
    xpad[W : W + SIDE, SIDE:] = put(SIDE * 16, ("side3", 3), ("side1", 1)).reshape(SIDE, 16, CH)

    def to_freq(r, _):
        x3[r] = dot(fwd_x[...], xpad[r])
        return 0

    lax.fori_loop(0, EXT, to_freq, 0, unroll=14)

    for l0, lw in LANES:
        for fb in range(5):
            rows = [slice(40 * t + 8 * fb, 40 * t + 8 * fb + 8) for t in range(3)]
            lanes = slice(l0, l0 + lw)
            kk = [[kf[u, rows[t], lanes] for t in range(3)] for u in range(7)]

            def conv(ib, _, fb=fb, rows=rows, lanes=lanes, kk=kk):
                i0 = ib * 4
                prods = []
                for t in range(3):
                    xs = [x3[i0 + r, rows[t], lanes] for r in range(10)]
                    prods.append([taps(xs[d : d + 7], [k[t] for k in kk]) for d in range(4)])
                for d in range(4):
                    y2[i0 + d, 16 * fb : 16 * fb + 16, lanes] = real_imag(*(p[d] for p in prods))
                return 0

            lax.fori_loop(0, SIDE // 4, conv, 0, unroll=4)

    load_cot.wait()
    egrad[...] = jnp.zeros_like(egrad)
    rgrad[...] = jnp.zeros_like(rgrad)
    step = 4
    parts = 8
    n = step * SIDE

    def part(i0):
        conv_out = jnp.concatenate([dot(inv_y[...], y2[i0 + d]) for d in range(step)], axis=0)
        yield
        conv_out = conv_out + conv_bias
        shifted = conv_out - jnp.mean(conv_out, axis=-1, keepdims=True)
        inv_std = lax.rsqrt(jnp.mean(shifted * shifted, axis=-1, keepdims=True) + 1e-06)
        centred = shifted * inv_std
        normed = (centred * gain + nbias).astype(BF)
        yield
        pre = dot(normed, w_exp[...]) + b_exp
        bgrad = (lscale * cot[pl.ds(i0, step)].reshape(n, CH).astype(F32)).astype(BF)
        act_grad = dot(bgrad, w_red[...])
        yield
        size = jnp.abs(pre)
        t = 1.0 / (1.0 + (0.3275911 * math.sqrt(0.5)) * size)
        dens = jnp.exp(-0.5 * pre * pre)
        poly = t * (
            0.127414796
            + t * (-0.142248368 + t * (0.7107068705 + t * (-0.7265760135 + t * 0.5307027145)))
        )
        tail = poly * dens
        phi = jnp.where(pre >= 0, 1.0 - tail, tail)
        act = (pre * phi).astype(BF)
        pre_grad = (act_grad * (phi + pre * (dens * 0.3989422804014327))).astype(BF)
        yield
        ngrad = dot_nt(pre_grad, w_exp[...])
        branch = dot_nt(act, w_red[...])
        rgrad[...] += dot_tn(bgrad, act)
        egrad[...] += dot_tn(normed, pre_grad)
        yield
        mix = fields[pl.ds(i0, step)].reshape(n, CH).astype(F32) + lscale * (branch + b_red)
        mix_out[pl.ds(i0, step)] = mix.astype(BF).reshape(step, SIDE, CH)
        ngrad = ngrad * gain
        m1 = jnp.mean(ngrad, axis=-1, keepdims=True)
        m2 = jnp.mean(ngrad * centred, axis=-1, keepdims=True)
        cgrad = (inv_std * (ngrad - m1 - centred * m2)).astype(BF)
        yield
        for d in range(step):
            g4[6 + i0 + d] = dot(fwd_g[...], cgrad[d * SIDE : (d + 1) * SIDE])
        yield

    def chunk(ic, _):
        gens = [part(pl.multiple_of((ic * parts + k) * step, step)) for k in range(parts)]
        for tick in range(7 + 1 * (parts - 1)):
            for k in range(parts):
                if 0 <= tick - 1 * k < 7:
                    next(gens[k])
        return 0

    lax.fori_loop(0, SIDE // (step * parts), chunk, 0)

    store_mixed = pltpu.make_async_copy(mix_out, mixed, io_sem.at[1])
    store_mixed.start()

    for g in range(3):
        lanes = slice(128 * g, 128 * g + 128)
        wsrc[192 * g : 192 * g + 192] = egrad[:, lanes].astype(BF)
        wsrc[576 + 192 * g : 768 + 192 * g] = rgrad[:, lanes].astype(BF)

    def dp_block(to):
        return wsrc.at[pl.ds(pl.multiple_of(to * dp_rows, 16), dp_rows)]

    ca = exchange("dp", ndp, dp_block, lambda m: wa.at[m], sa, ra)
    wa[md] = wsrc[pl.ds(pl.multiple_of(md * dp_rows, 16), dp_rows)]

    for l0, lw in LANES:
        for fb in range(5):
            rows = [slice(40 * t + 8 * fb, 40 * t + 8 * fb + 8) for t in range(4)]
            grow = (rows[0], rows[1], rows[3])
            lanes = slice(l0, l0 + lw)

            def kgrad(ib, accs, rows=rows, lanes=lanes, grow=grow):
                i0 = ib * 4
                accs = list(accs)
                for t in range(3):
                    xs = [x3[i0 + r, rows[t], lanes] for r in range(10)]
                    for d in range(4):
                        g = g4[6 + i0 + d, grow[t], lanes]
                        for u in range(7):
                            accs[7 * t + u] = accs[7 * t + u] + xs[d + u] * g
                return tuple(accs)

            zero = jnp.zeros((8, lw), F32)
            accs = lax.fori_loop(0, SIDE // 4, kgrad, (zero,) * 21, unroll=2)
            for t in range(3):
                for u in range(7):
                    m3[u, rows[t], lanes] = accs[7 * t + u]


    kg = jnp.concatenate([dot_exact(inv_k[...], m3[u]) for u in range(7)], axis=0)
    kg = jnp.concatenate([kg, jnp.zeros((8, CH), F32)], axis=0)
    ksrc[0:64] = kg[:, 0:128]
    ksrc[64:128] = jnp.concatenate([kg[:, 128:192], jnp.zeros((64, 64), F32)], axis=1)

    def kernel_block(to):
        return ksrc.at[pl.ds(pl.multiple_of(to * krows, 16), krows)]

    ka = exchange("dp", ndp, kernel_block, lambda m: kwa.at[m], ska, rka)
    kwa[md] = ksrc[pl.ds(pl.multiple_of(md * krows, 16), krows)]

    for l0, lw in LANES:
        for fb in range(5):
            rows = [slice(40 * t + 8 * fb, 40 * t + 8 * fb + 8) for t in range(3)]
            lanes = slice(l0, l0 + lw)

            kk = [
                [kf[u, 120 + 40 * t + 8 * fb : 128 + 40 * t + 8 * fb, lanes] for t in range(3)]
                for u in range(7)
            ]

            def pconv(ib, _, fb=fb, rows=rows, lanes=lanes, kk=kk):
                p0 = ib * 5
                prods = []
                for t in range(3):
                    gs = [g4[p0 + r, rows[t], lanes] for r in range(11)]
                    back = [k[t] for k in kk][::-1]
                    prods.append([taps(gs[d : d + 7], back) for d in range(5)])
                for d in range(5):
                    y2[p0 + d, 16 * fb : 16 * fb + 16, lanes] = real_imag(*(p[d] for p in prods))
                return 0

            lax.fori_loop(0, EXT // 5, pconv, 0, unroll=2)


    finish(ca)
    part = wa[0].astype(F32)
    for j in range(1, ndp):
        part = part + wa[j].astype(F32)
    pa[...] = part.reshape(owners, WBLOCK, 128)

    def share(off, src, dst, send, recv):
        return pltpu.make_async_remote_copy(
            src_ref=src,
            dst_ref=dst,
            send_sem=send.at[off],
            recv_sem=recv.at[off],
            device_id={"tile": peer(me, off, TILES)},
            device_id_type=MESH,
        )

    def to_owner(off):
        to = peer(me, off, TILES)
        return to, share(off, pa.at[lax.rem(to, owners)], wb.at[me], sb, rb)

    for off in range(1, TILES):
        to, copy = to_owner(off)
        pl.when(to < owners)(copy.start)

    @pl.when(me < owners)
    def _():
        wb[me] = pa[lax.rem(me, owners)]

    finish(ka)
    part = kwa[0]
    for j in range(1, ndp):
        part = part + kwa[j]
    kpart[...] = part.astype(BF)
    kb = exchange("tile", TILES, lambda to: kpart, lambda m: kwb.at[m], skb, rkb)
    kwb[me] = kpart[...]
    for p in range(W):
        ptop[p] = dot(inv_p[...], y2[p]).astype(BF)
        pbot[p] = dot(inv_p[...], y2[W + SIDE + p]).astype(BF)

    def from_freq(i, _):
        back = dot(inv_p[...], y2[i + W])
        dir_out[i] = (cot[i].astype(F32) + back[0:SIDE]).astype(BF)
        psides[i] = back[SIDE:].astype(BF)
        return 0

    lax.fori_loop(0, SIDE, from_freq, 0, unroll=8)
    store_direct = pltpu.make_async_copy(dir_out, direct, io_sem.at[2])
    store_direct.start()

    top = ptop[...].reshape(W * KROW, CH)
    bot = pbot[...].reshape(W * KROW, CH)
    sides = psides[...].reshape(SIDE * 16, CH)


    def take(*parts):
        total = sum(dot(gather(by_col, name, part.shape[0]), part) for name, part in parts)
        return total.astype(BF).reshape(1, TILES, CELLS, CH)

    taken = [
        take(("top0", top)),
        take(("side1", sides), ("bot1", bot)),
        take(("bot2", bot)),
        take(("side3", sides), ("top3", top)),
    ]
    pack(own2, jnp.concatenate(taken, axis=0))


    c3 = exchange("tile", TILES, lambda to: own2.at[:, to], lambda m: got2.at[:, m], s3, r3)
    got2[:, me] = own2[:, me]
    for off in range(1, TILES):
        to, copy = to_owner(off)
        pl.when(to < owners)(copy.wait_send)
        pl.when(me < owners)(copy.wait_recv)

    mine = lax.rem(me, owners)

    @pl.when(me < owners)
    def _():
        whole = wb[0]
        for j in range(1, TILES):
            whole = whole + wb[j]
        pc[...] = whole.astype(BF)
        wc[mine] = whole.astype(BF)
        for off in range(1, TILES):
            share(off, pc, wc.at[mine], sc, rc).start()

    finish(kb)
    part = kwb[0].astype(F32)
    for j in range(1, TILES):
        part = part + kwb[j].astype(F32)
    kwhole[...] = part.astype(BF)
    kc = exchange("dp", ndp, lambda to: kwhole, lambda m: kwc.at[m], skc, rkc)
    kwc[md] = kwhole[...]
    route_back = route_matrix(base, me, 1)
    finish(c3)
    pack(routed2, dot(route_back, unpack(got2)).astype(BF).reshape(4, TILES, CELLS, CH))
    c4 = exchange("tile", TILES, lambda to: routed2.at[:, to], lambda m: back2.at[:, m], s4, r4)
    back2[:, me] = routed2[:, me]

    for off in range(1, TILES):
        copy = share(off, pc, wc.at[mine], sc, rc)
        pl.when(me < owners)(copy.wait_send)
        pl.when(peer(me, TILES - off, TILES) < owners)(copy.wait_recv)

    block = wc[...].reshape(owners * WBLOCK, 128)
    pd = wa.at[0]
    pd[...] = block
    cd = exchange("dp", ndp, lambda to: pd, lambda m: wd.at[m], sd, rd)
    wd[md] = block
    finish(cd)
    wout[0:WROWS] = wd[...].reshape(WROWS, 128)
    finish(c4)
    bands[...] = unpack(back2).reshape(4, 256, CH)
    finish(kc)
    wout[WROWS:] = kwc[...].reshape(KROWS, 128)
    store_direct.wait()
    store_mixed.wait()


def main(fields, cotangent, neighbors, rotations, params, ndp):
    index = [jnp.asarray(t) for t in static_tables()]
    tables = [jnp.asarray(t) for t in dft_tables()]
    vm = pl.BlockSpec(memory_space=pltpu.VMEM)
    hbm = pl.BlockSpec(memory_space=pl.ANY)
    halo_buf = pltpu.VMEM(PACKED, BF)
    sem = pltpu.SemaphoreType.DMA((TILES,))
    sem_dp = pltpu.SemaphoreType.DMA((ndp,))
    dp_rows = WROWS // ndp
    krows = KROWS // ndp
    owners = dp_rows // WBLOCK
    offsets = jnp.asarray(OFFSETS, jnp.int32).reshape(8, 1)
    args = [fields, cotangent, *index, neighbors.T, rotations.T, offsets, *tables, *params]
    field = jax.ShapeDtypeStruct((SIDE, SIDE, CH), BF)
    return pl.pallas_call(
        main_kernel,
        out_shape=(
            field,
            field,
            jax.ShapeDtypeStruct((4, 256, CH), BF),
            jax.ShapeDtypeStruct((WROWS + KROWS, 128), BF),
        ),
        in_specs=[vm, hbm] + [vm] * (len(args) - 2),
        out_specs=(hbm, hbm, vm, vm),
        scratch_shapes=[
            pltpu.VMEM((EXT, KROW, CH), BF),
            pltpu.VMEM((EXT, 3 * NFREQ, CH), F32),
            pltpu.VMEM((EXT, 2 * NFREQ, CH), BF),
            pltpu.VMEM((SIDE + 12, 4 * NFREQ, CH), F32),
            pltpu.VMEM((8, CH), F32),
            pltpu.VMEM((7, 6 * NFREQ, CH), F32),
            pltpu.VMEM((7, 3 * NFREQ, CH), F32),
            pltpu.VMEM((CH, HID), F32),
            pltpu.VMEM((CH, HID), F32),
            pltpu.VMEM((SIDE, 16, CH), BF),
            pltpu.VMEM((W, KROW, CH), BF),
            pltpu.VMEM((W, KROW, CH), BF),
            pltpu.VMEM((SIDE, SIDE, CH), BF),
            pltpu.VMEM((SIDE, SIDE, CH), BF),
            pltpu.VMEM((4, 256, CH), BF),
        ]
        + [halo_buf] * 8
        + [
            pltpu.VMEM((WROWS, 128), BF),
            pltpu.VMEM((ndp, dp_rows, 128), BF),
            pltpu.VMEM((owners, WBLOCK, 128), F32),
            pltpu.VMEM((TILES, WBLOCK, 128), F32),
            pltpu.VMEM((WBLOCK, 128), BF),
            pltpu.VMEM((owners, WBLOCK, 128), BF),
            pltpu.VMEM((ndp, dp_rows, 128), BF),
            pltpu.VMEM((KROWS, 128), F32),
            pltpu.VMEM((ndp, krows, 128), F32),
            pltpu.VMEM((krows, 128), BF),
            pltpu.VMEM((TILES, krows, 128), BF),
            pltpu.VMEM((krows, 128), BF),
            pltpu.VMEM((ndp, krows, 128), BF),
            pltpu.VMEM((SIDE, SIDE, CH), BF),
            pltpu.SemaphoreType.DMA((3,)),
        ]
        + [sem] * 14
        + [sem_dp] * 8,
        compiler_params=pltpu.CompilerParams(
            collective_id=0, has_side_effects=True, vmem_limit_bytes=62 * 2**20
        ),
        name="main",
    )(*args)


def last_kernel(
    scale, mixed, direct, bands, wsum, by_row, mixed_out, out, kgrad, egrad, rgrad, d, b, w, m, sem
):
    load_m = pltpu.make_async_copy(mixed, m, sem.at[0])
    store_m = pltpu.make_async_copy(m, mixed_out, sem.at[5])
    load_b = pltpu.make_async_copy(bands, b, sem.at[1])
    load_w = pltpu.make_async_copy(wsum, w, sem.at[2])
    load_d = pltpu.make_async_copy(direct, d, sem.at[3])
    store_d = pltpu.make_async_copy(d, out, sem.at[4])
    for copy in (load_b, load_d, load_w, load_m):
        copy.start()
    load_b.wait()
    north = dot(spread(by_row, "north", W * SIDE), b[0]).reshape(W, SIDE, CH)
    south = dot(spread(by_row, "south", W * SIDE), b[2]).reshape(W, SIDE, CH)
    east = dot(spread(by_row, "east", 1024), b[1]).reshape(SIDE, 16, CH)
    west = dot(spread(by_row, "west", 1024), b[3]).reshape(SIDE, 16, CH)
    mid = slice(W, SIDE - W)
    load_d.wait()
    d[mid, 0:16] = (d[mid, 0:16].astype(F32) + west[mid]).astype(BF)
    d[mid, 48:64] = (d[mid, 48:64].astype(F32) + east[mid]).astype(BF)
    zero = jnp.zeros((W, 32, CH), F32)
    for rows, add in ((slice(0, W), north), (slice(SIDE - W, SIDE), south)):
        more = jnp.concatenate([west[rows], zero, east[rows]], axis=1)
        d[rows] = (d[rows].astype(F32) + add + more).astype(BF)
    store_d.start()
    load_m.wait()
    store_m.start()
    load_w.wait()
    for g in range(3):
        lanes = slice(128 * g, 128 * g + 128)
        egrad[:, lanes] = w[192 * g : 192 * g + 192].astype(F32) * scale
        rgrad[:, lanes] = w[576 + 192 * g : 768 + 192 * g].astype(F32) * scale
    low = w[WROWS : WROWS + 64].astype(F32) * scale
    high = w[WROWS + 64 : WROWS + 128].astype(F32) * scale
    for u in range(7):
        kgrad[u, :, 0:128] = low[8 * u : 8 * u + 7]
        kgrad[u, :, 128:192] = high[8 * u : 8 * u + 7, 0:64]
    store_d.wait()
    store_m.wait()


def last(mixed, direct, bands, wsum, scale):
    by_row, _ = static_tables()
    vm = pl.BlockSpec(memory_space=pltpu.VMEM)
    hbm = pl.BlockSpec(memory_space=pl.ANY)
    field = jax.ShapeDtypeStruct((SIDE, SIDE, CH), BF)
    return pl.pallas_call(
        functools.partial(last_kernel, scale),
        out_shape=(
            field,
            field,
            jax.ShapeDtypeStruct((7, 7, CH), F32),
            jax.ShapeDtypeStruct((CH, HID), F32),
            jax.ShapeDtypeStruct((CH, HID), F32),
        ),
        in_specs=[hbm] * 4 + [vm],
        out_specs=(hbm, hbm, vm, vm, vm),
        scratch_shapes=[
            pltpu.VMEM((SIDE, SIDE, CH), BF),
            pltpu.VMEM((4, 256, CH), BF),
            pltpu.VMEM((WROWS + KROWS, 128), BF),
            pltpu.VMEM((SIDE, SIDE, CH), BF),
            pltpu.SemaphoreType.DMA((6,)),
        ],
        compiler_params=pltpu.CompilerParams(vmem_limit_bytes=62 * 2**20),
        name="last",
    )(mixed, direct, bands, wsum, jnp.asarray(by_row))


def on_device(
    fields,
    cotangent,
    kernel,
    conv_bias,
    norm_gain,
    norm_bias,
    w_expand,
    bias_expand,
    w_reduce,
    bias_reduce,
    layer_scale,
    neighbors,
    rotations,
):
    ndp = lax.axis_size("dp")
    field = fields.reshape(SIDE, SIDE, CH)
    cot = cotangent.reshape(SIDE, SIDE, CH)
    params = [
        kernel,
        conv_bias,
        norm_gain,
        norm_bias,
        w_expand,
        bias_expand,
        w_reduce.T,
        bias_reduce,
        layer_scale,
    ]
    mixed, direct, bands, wsum = main(field, cot, neighbors, rotations, params, ndp)
    scale = 1.0 / math.sqrt(ndp * TILES * SIDE * SIDE)
    mixed, input_grad, kgrad, egrad, rgrad = last(mixed, direct, bands, wsum, scale)
    return (
        mixed.reshape(fields.shape),
        input_grad.reshape(fields.shape),
        kgrad,
        egrad,
        rgrad.T,
    )


def solution(mesh):
    split = P("dp", "tile", None, None, None)
    return jax.shard_map(
        on_device,
        mesh=mesh,
        in_specs=(split, split) + (P(),) * 11,
        out_specs=(split, split, P(), P(), P()),
        check_vma=False,
    )
```
